32 devices in a mesh: img: 8 (over z, x), seq: 4 (over y, core).
Axes of the slice: x: 2, y: 2, z: 4, core: 2. Of those that a mesh axis runs over, the one named last changes fastest.
Arguments:
- tokens: bfloat16 [16, 1024, 1152], P('img', 'seq'), may hold values from -6 to 6
- time_embed: bfloat16 [16, 4, 1152], P('img'), may hold values from -6 to 6
- image_lengths: int32 [16, 4], P('img'), may hold values from 0 to 1024, as said below
- grid_turns: int32 [16, 4], P('img'), may hold values from 0 to 7
- ln1_gain: float32 [1152], replicated, may hold values from 0.5 to 1.5
- w_qkv: bfloat16 [1152, 3456], replicated, may hold values from -0.1875 to 0.1875
- w_time_q: bfloat16 [1152, 1152], replicated, may hold values from -0.1875 to 0.1875
- time_value_weight: bfloat16 [1152, 1152], replicated, may hold values from -0.0234375 to 0.0234375
- rel_rows: float32 [16, 63], replicated, may hold values from -3 to 3
- rel_cols: float32 [16, 63], replicated, may hold values from -3 to 3
- output_projection_weight: bfloat16 [1152, 1152], replicated, may hold values from -1.5 to 1.5
- ln2_gain: float32 [1152], replicated, may hold values from 0.5 to 1.5
- w_up: bfloat16 [1152, 4608], replicated, may hold values from -0.1875 to 0.1875
- w_down: bfloat16 [4608, 1152], replicated, may hold values from -0.09375 to 0.09375
- out_grad: bfloat16 [16, 1024, 1152], P('img', 'seq'), may hold values from -6 to 6
Outputs:
- output: bfloat16 [16, 1024, 1152], P('img', 'seq')
- input_grad: bfloat16 [16, 1024, 1152], P('img', 'seq')
- ln1_gain_grad: float32 [1152], P('img')
- w_qkv_grad: float32 [1152, 3456], P('img')
- w_time_q_grad: float32 [1152, 1152], P('img')
- w_time_v_grad: float32 [1152, 1152], P('img')
- rel_rows_grad: float32 [16, 63], replicated
- rel_cols_grad: float32 [16, 63], replicated
- w_proj_grad: float32 [1152, 1152], P('img')
- ln2_gain_grad: float32 [1152], P('img')
- w_up_grad: float32 [1152, 4608], P('img')
- w_down_grad: float32 [4608, 1152], P('img')
- rms_values: float32 [3], replicated
The draws below stay inside these ranges and needn't reach their ends.
Inputs may be any that keep to these rules, and one draw needn't show every extreme that they name: `image_lengths`: A slot holds one image of 1024 tokens, or one to four images of 256 tokens, or nothing; images come first, the rest of its 1024 tokens is padding. Every group of 2 slots along img has a slot with a 1024-token image, and one group has no empty slot. `grid_turns`: bit 0 flips the grid's rows, bit 1 its columns, bit 2 swaps rows and columns.
All inputs are finite; a program needn't handle non-finite values.
Results may differ from the reference program's by a relative error of at most 0.022.
Values may be sent and summed in bfloat16 or wider, within the bound.
No kernel may reach another device: no remote copies, remote signals or barrier semaphores. Data moves between devices by JAX's collectives and lax.ppermute only.
A program may use at most 384 MiB of HBM per device.

```python
import jax
import jax.numpy as jnp
from jax import lax

D = 1152
H = 16
FF = 4608
SIDE = 32
SLOTS = 2
LEN = 1024
SEQS = 16
N_IMG = 8


def draw_image_lengths(key, part):
    key = jax.random.fold_in(key, 11)
    key_live, key_full, key_long, key_kind, key_count = jax.random.split(key, 5)
    group_ids = jnp.arange(N_IMG, dtype=jnp.int32)
    live_count = jax.random.randint(key_live, (N_IMG,), (SLOTS + 1) // 2, SLOTS + 1, dtype=jnp.int32)
    full_group = jax.random.randint(key_full, (), 0, N_IMG, dtype=jnp.int32)
    live_count = jnp.where(group_ids == full_group, SLOTS, live_count)
    long_slot = jax.random.randint(key_long, (N_IMG,), 0, live_count, dtype=jnp.int32)
    slot_ids = jnp.arange(SLOTS, dtype=jnp.int32)[None, :]
    is_live = slot_ids < live_count[:, None]
    kind_draw = jax.random.randint(key_kind, (N_IMG, SLOTS), 0, 17, dtype=jnp.int32)
    is_long = (kind_draw < 10) | (slot_ids == long_slot[:, None])
    image_count = jax.random.randint(key_count, (N_IMG, SLOTS), 1, 5, dtype=jnp.int32)
    image_ids = jnp.arange(4, dtype=jnp.int32)
    long_row = jnp.where(image_ids == 0, LEN, 0)
    short_row = jnp.where(image_ids[None, None, :] < image_count[:, :, None], LEN // 4, 0)
    lengths = jnp.where(is_long[:, :, None], long_row[None, None, :], short_row)
    lengths = jnp.where(is_live[:, :, None], lengths, 0)
    return lengths.reshape(N_IMG * SLOTS, 4).astype(jnp.int32)


def touch_ends(entries, own_key, low, high):
    longest = entries.shape.index(max(entries.shape))
    spots = []
    for shift in (0, 1):
        where = [jax.random.randint(jax.random.fold_in(own_key, axis), (), 0, length) for axis, length in enumerate(entries.shape)]
        where[longest] = (where[longest] + shift) % entries.shape[longest]
        spots.append(tuple(where))
    return entries.at[spots[0]].set(low).at[spots[1]].set(high)


def level_of(own_key, dims, shards, least, top_value):
    gain = 1.0
    for axis_at, shards_of in shards:
        draws = jax.random.uniform(jax.random.fold_in(jax.random.fold_in(own_key, 6), axis_at), (shards_of,), jnp.float32, least / len(shards), top_value / len(shards))
        gain = gain * jnp.repeat(jnp.exp(draws), dims[axis_at] // shards_of).reshape((-1,) + (1,) * (len(dims) - 1 - axis_at))
    return gain


def centred(rng, extent, width, limit, shards=(), held_as=jnp.bfloat16):
    values = jax.random.normal(rng, extent, jnp.float32) * width
    if len(shards) > 0:
        values = level_of(rng, extent, shards, -0.22, 0.18) * values
    return jnp.clip(values, min=-limit, max=limit).astype(held_as)


def setup_inputs(seed: int = 0) -> dict:
    splits = jax.random.split(jax.random.key(seed), 16)
    tokens = centred(splits[0], (SEQS, LEN, D), 1.0, 6.0, ((0, 8), (1, 4)))
    time_embed = centred(splits[1], (SEQS, 4, D), 1.0, 6.0, ((0, 8),))
    image_lengths = draw_image_lengths(jax.random.fold_in(splits[15], 71), 0)
    grid_turns = touch_ends(jax.random.randint(splits[3], (SEQS, 4), 0, 8), jax.random.fold_in(splits[3], 1), 0, 7).astype(jnp.int32)
    ln1_gain = jnp.clip(1.0 + 0.1 * jax.random.normal(splits[4], (D,), jnp.float32), 0.5, 1.5)
    w_qkv = centred(splits[5], (D, 3 * D), D ** -0.5, 0.1875)
    w_time_q = centred(splits[6], (D, D), D ** -0.5, 0.1875)
    time_value_weight = centred(splits[7], (D, D), (64 * D) ** -0.5, 0.0234375)
    rel_rows = centred(splits[8], (H, 2 * SIDE - 1), 0.5, 3.0, (), jnp.float32)
    rel_cols = centred(splits[9], (H, 2 * SIDE - 1), 0.5, 3.0, (), jnp.float32)
    output_projection_weight = centred(splits[10], (D, D), (max(D // 64, 1)) ** -0.5, 1.5)
    ln2_gain = jnp.clip(1.0 + 0.1 * jax.random.normal(splits[11], (D,), jnp.float32), 0.5, 1.5)
    w_up = centred(splits[12], (D, FF), D ** -0.5, 0.1875)
    w_down = centred(splits[13], (FF, D), FF ** -0.5, 0.09375)
    out_grad = centred(splits[14], (SEQS, LEN, D), 1.0, 6.0, ((0, 8), (1, 4)))
    return dict(tokens=tokens, time_embed=time_embed, image_lengths=image_lengths, grid_turns=grid_turns, ln1_gain=ln1_gain, w_qkv=w_qkv, w_time_q=w_time_q, time_value_weight=time_value_weight, rel_rows=rel_rows, rel_cols=rel_cols, output_projection_weight=output_projection_weight, ln2_gain=ln2_gain, w_up=w_up, w_down=w_down, out_grad=out_grad)


@jax.custom_vjp
def low(v):
    return lax.optimization_barrier(v.astype(jnp.bfloat16)).astype(jnp.float32)

@jax.custom_vjp
def lower_backward(v):
    return v

def low_keep(v):
    return (low(v), None)

def low_pass(kept, grad):
    return (grad,)

def back_keep(v):
    return (v, None)

def back_low(kept, grad):
    return (low(grad),)
low.defvjp(low_keep, low_pass)
lower_backward.defvjp(back_keep, back_low)
eps_norm = 1e-06
seqs_per_block = 4
peak_value = lax.Precision.HIGHEST

def layout(lengths, turn_codes, positions, grid_side):
    image_end = jnp.cumsum(lengths, axis=1, dtype=jnp.int32)
    image_start = image_end - lengths
    token_at = positions[None, :]
    segment = lax.optimization_barrier(jnp.sum((token_at[:, :, None] >= image_end[:, None, :]).astype(jnp.int32), axis=2, dtype=jnp.int32))
    is_valid = token_at < image_end[:, 3:4]
    picked = jnp.minimum(segment, 3)
    onehot = (picked[:, :, None] == jnp.arange(4, dtype=jnp.int32)[None, None, :]).astype(jnp.int32)
    begin_at = lax.optimization_barrier(jnp.sum(onehot * image_start[:, None, :], axis=2, dtype=jnp.int32))
    image_len = lax.optimization_barrier(jnp.sum(onehot * lengths[:, None, :], axis=2, dtype=jnp.int32))
    turned = lax.optimization_barrier(jnp.sum(onehot * turn_codes[:, None, :], axis=2, dtype=jnp.int32))
    grid_width = jnp.where(image_len == grid_side * grid_side, grid_side, grid_side // 2).astype(jnp.int32)
    offset = token_at - begin_at
    row_raw = offset // grid_width
    col_raw = offset % grid_width
    row_flip = jnp.where(turned % 2 == 1, grid_width - 1 - row_raw, row_raw)
    col_flip = jnp.where(turned // 2 % 2 == 1, grid_width - 1 - col_raw, col_raw)
    row_pos = jnp.where(turned >= 4, col_flip, row_flip)
    col_pos = jnp.where(turned >= 4, row_flip, col_flip)
    row_pos = jnp.where(is_valid, row_pos, 0).astype(jnp.int32)
    col_pos = jnp.where(is_valid, col_pos, 0).astype(jnp.int32)
    return (segment, is_valid, row_pos, col_pos, onehot)

def layer_norm(inputs, gain_vec):
    centre = inputs - lax.optimization_barrier(jnp.mean(inputs, axis=-1, keepdims=True))
    spread = lax.optimization_barrier(jnp.mean(centre * centre, axis=-1, keepdims=True))
    return centre * lax.rsqrt(spread + eps_norm) * gain_vec

def block_forward(params, token_block, time_block, length_block, turn_block):
    ln1_gain, w_qkv, w_time_q, time_value_weight, rel_rows, rel_cols, output_projection_weight, ln2_gain, w_up, w_down = params
    block_seqs, seq_len, model_dim = token_block.shape
    head_count = rel_rows.shape[0]
    head_dim = model_dim // head_count
    q_scale = head_dim ** (-0.5)
    positions = jnp.arange(seq_len, dtype=jnp.int32)
    segment, is_valid, row_pos, col_pos, onehot = layout(length_block, turn_block, positions, SIDE)
    image_hot = onehot.astype(jnp.float32)
    attn_in = low(layer_norm(token_block, ln1_gain))
    qkv_full = jnp.einsum('snd,df->snf', attn_in, w_qkv, precision=peak_value)
    time_q = jnp.einsum('sjd,df->sjf', time_block, w_time_q, precision=peak_value)
    time_v = jnp.einsum('sjd,df->sjf', time_block, time_value_weight, precision=peak_value)
    token_tq = jnp.einsum('snj,sjf->snf', image_hot, time_q, precision=peak_value)
    token_tv = jnp.einsum('snj,sjf->snf', image_hot, time_v, precision=peak_value)
    queries = low(lower_backward(qkv_full[..., :model_dim] + token_tq) * q_scale)
    keys = low(lower_backward(qkv_full[..., model_dim:2 * model_dim]))
    values = low(lower_backward(qkv_full[..., 2 * model_dim:] + token_tv))
    row_table = low(rel_rows)
    col_table = low(rel_cols)

    def attend(item):
        seq_q, seq_k, seq_v, seq_seg, seq_row, seq_col = item
        query_heads = seq_q.reshape(seq_len, head_count, head_dim)
        key_heads = seq_k.reshape(seq_len, head_count, head_dim)
        value_heads = seq_v.reshape(seq_len, head_count, head_dim)
        score_matrix = jnp.einsum('qhe,khe->hqk', query_heads, key_heads, precision=peak_value)
        row_index = seq_row[:, None] - seq_row[None, :] + SIDE - 1
        col_index = seq_col[:, None] - seq_col[None, :] + SIDE - 1
        score_matrix = score_matrix + row_table[:, row_index] + col_table[:, col_index]
        score_matrix = lower_backward(score_matrix)
        same_image = seq_seg[:, None] == seq_seg[None, :]
        score_matrix = jnp.where(same_image[None, :, :], score_matrix, -1e+30)
        log_norm = jax.scipy.special.logsumexp(score_matrix, axis=2, keepdims=True)
        probs = low(jnp.exp(score_matrix - log_norm))
        mixed = jnp.einsum('hqk,khe->qhe', probs, value_heads, precision=peak_value)
        return mixed.reshape(seq_len, model_dim)
    attn_mix = lax.map(jax.checkpoint(attend), (queries, keys, values, segment, row_pos, col_pos))
    attention_result = low(lower_backward(attn_mix))
    first_branch = lower_backward(jnp.einsum('tlc,cg->tlg', attention_result, output_projection_weight, precision=peak_value))
    hidden_one = token_block + first_branch
    mlp_in = low(layer_norm(hidden_one, ln2_gain))
    up_proj = lower_backward(jnp.einsum('snd,df->snf', mlp_in, w_up, precision=peak_value))
    gelu_out = low(jax.nn.gelu(up_proj, approximate=False))
    branch_two = lower_backward(jnp.einsum('snf,fd->snd', gelu_out, w_down, precision=peak_value))
    hidden_two = hidden_one + branch_two
    valid_mask = is_valid.astype(jnp.float32)[:, :, None]
    stats = jnp.stack([jnp.sum(valid_mask * hidden_two * hidden_two), jnp.sum(valid_mask * first_branch * first_branch), jnp.sum(valid_mask * branch_two * branch_two), jnp.sum(valid_mask)])
    return (hidden_two * valid_mask, stats)

def reference(tokens, time_embed, image_lengths, grid_turns, ln1_gain, w_qkv, w_time_q, time_value_weight, rel_rows, rel_cols, output_projection_weight, ln2_gain, w_up, w_down, out_grad):
    params = (ln1_gain, w_qkv.astype(jnp.float32), w_time_q.astype(jnp.float32), time_value_weight.astype(jnp.float32), rel_rows, rel_cols, output_projection_weight.astype(jnp.float32), ln2_gain, w_up.astype(jnp.float32), w_down.astype(jnp.float32))
    block_total = tokens.shape[0] // seqs_per_block

    def regroup(array):
        return array.reshape((block_total, seqs_per_block) + array.shape[1:])
    time_grouped = regroup(time_embed.astype(jnp.float32))
    length_grouped = regroup(image_lengths)
    turn_grouped = regroup(grid_turns)

    def forward(token_float, weights):

        def advance(carry, item):
            token_block, time_block, length_block, turn_block = item
            result, stats = jax.checkpoint(block_forward)(weights, token_block, time_block, length_block, turn_block)
            return (carry + stats, result)
        totals, results = lax.scan(advance, jnp.zeros((4,), jnp.float32), (regroup(token_float), time_grouped, length_grouped, turn_grouped))
        return (results.reshape(token_float.shape), totals)
    output, pull, totals = jax.vjp(forward, tokens.astype(jnp.float32), params, has_aux=True)
    input_grad, grads = pull(out_grad.astype(jnp.float32))
    rms_values = jnp.sqrt(totals[:3] / (totals[3] * D))
    return (output.astype(jnp.bfloat16), input_grad.astype(jnp.bfloat16), grads[0], grads[1], grads[2], grads[3], grads[4], grads[5], grads[6], grads[7], grads[8], grads[9], rms_values)
```

```python
import functools
import math

import jax
import jax.numpy as jnp
from jax import lax
from jax.experimental import pallas as pl
from jax.experimental.pallas import tpu as pltpu
from jax.sharding import PartitionSpec as P

SIDE = 32
EPS = 1e-06
FAR = -1e30
BF = jnp.bfloat16
F32 = jnp.float32
HIGH = lax.Precision.HIGHEST
VMEM_LIMIT = 56 * 2**20
QUERY_BLOCK = 256

RC = 2 * SIDE
KEY_MASK = RC
QUERY_MASK = KEY_MASK + 16
IMAGE_HOT = QUERY_MASK + 16
FEATURES = IMAGE_HOT + 16


def dot(a, b, ca, cb):
    return lax.dot_general(a, b, (((ca,), (cb,)), ((), ())), preferred_element_type=F32)


def params(*semantics):
    return pltpu.CompilerParams(dimension_semantics=semantics, vmem_limit_bytes=VMEM_LIMIT)


def cost(flops, bytes_accessed, transcendentals=0):
    return pl.CostEstimate(
        flops=int(flops), bytes_accessed=int(bytes_accessed), transcendentals=int(transcendentals)
    )


def features_kernel(len_ref, turn_ref, base_ref, feat_ref, valid_ref, *, span):
    tokens = feat_ref.shape[1]

    def describe(shape, axis):
        index = lax.broadcasted_iota(jnp.int32, shape, axis)
        block = index // span
        pos = index - block * span
        for k in range(tokens // span):
            pos = pos + jnp.where(block == k, base_ref[k], 0)
        ends = []
        total = 0
        for j in range(4):
            total = total + len_ref[j]
            ends.append(total)
        segment = sum((pos >= ends[j]).astype(jnp.int32) for j in range(4))
        return pos, ends, segment

    pos, ends, segment = describe((1, tokens), 1)
    picked = jnp.minimum(segment, 3)
    begin = jnp.zeros_like(pos)
    length = jnp.zeros_like(pos)
    turn = jnp.zeros_like(pos)
    for j in range(4):
        here = picked == j
        begin = jnp.where(here, ends[j] - len_ref[j], begin)
        length = jnp.where(here, len_ref[j], length)
        turn = jnp.where(here, turn_ref[j], turn)
    full = length == SIDE * SIDE
    side = jnp.where(full, SIDE, SIDE // 2)
    u = pos - begin
    bits = SIDE.bit_length() - 1
    r0 = jnp.where(full, u >> bits, u >> (bits - 1))
    c0 = u & (side - 1)
    r1 = jnp.where((turn & 1) == 1, side - 1 - r0, r0)
    c1 = jnp.where(((turn >> 1) & 1) == 1, side - 1 - c0, c0)
    valid = pos < ends[3]
    row = jnp.where(valid, jnp.where(turn >= 4, c1, r1), 0)
    col = jnp.where(valid, jnp.where(turn >= 4, r1, c1), 0)
    which = lax.broadcasted_iota(jnp.int32, (SIDE, tokens), 0)
    few = lax.broadcasted_iota(jnp.int32, (16, tokens), 0)

    def put(start, value):
        feat_ref[start : start + value.shape[0], :] = value.astype(BF)

    put(0, jnp.where(which == row, 1.0, 0.0))
    put(SIDE, jnp.where(which == col, 1.0, 0.0))
    put(KEY_MASK, jnp.where(few == segment, 1.0, 0.0))
    put(QUERY_MASK, jnp.where((few < 5) & (few != segment), FAR, 0.0))
    put(IMAGE_HOT, jnp.where(few == picked, 1.0, 0.0))
    down_pos, down_ends, unused = describe(valid_ref.shape, 0)
    valid_ref[...] = jnp.where(down_pos < down_ends[3], 1.0, 0.0)


def token_features(lengths, turns, bases, span, mine):
    tokens = bases.shape[0] * span
    smem = pl.BlockSpec(memory_space=pltpu.SMEM)
    return pl.pallas_call(
        functools.partial(features_kernel, span=span),
        out_shape=(
            jax.ShapeDtypeStruct((FEATURES, tokens), BF),
            jax.ShapeDtypeStruct((mine, 128), F32),
        ),
        in_specs=[smem, smem, smem],
        name="token_features",
    )(lengths, turns, bases)


def stack_heads(ref):
    return jnp.concatenate([ref[p, 0].astype(F32) for p in range(ref.shape[0])], axis=0).astype(BF)


def forward_kernel(a_ref, w_ref, time_ref, table_ref, feat_ref, qkv_ref, o_ref, lse_ref, *, scale):
    width = w_ref.shape[2]
    tokens = a_ref.shape[1]
    qkv = jnp.dot(stack_heads(w_ref), a_ref[...], preferred_element_type=F32)
    hot = feat_ref[IMAGE_HOT:, :].astype(F32)

    def timed(k):
        return sum(time_ref[k, 0][:, j : j + 1] * hot[j : j + 1] for j in range(4))

    q = ((qkv[:width] + timed(0)) * scale).astype(BF)
    k = qkv[width : 2 * width].astype(BF)
    v = (qkv[2 * width :] + timed(1)).astype(BF)
    qkv_ref[0, 0] = q
    qkv_ref[1, 0] = k
    qkv_ref[2, 0] = v
    bias = jnp.dot(table_ref[0], feat_ref[:RC], preferred_element_type=F32).astype(BF)
    key = jnp.concatenate([feat_ref[:QUERY_MASK], k], axis=0).T
    for b in range(tokens // QUERY_BLOCK):
        at = slice(b * QUERY_BLOCK, (b + 1) * QUERY_BLOCK)
        query = jnp.concatenate(
            [bias[:, at], feat_ref[QUERY_MASK:IMAGE_HOT, at], q[:, at]], axis=0
        )
        s = jnp.dot(key, query, preferred_element_type=F32)
        top = jnp.max(s, axis=0, keepdims=True)
        e = jnp.exp(s - top)
        total = jnp.sum(e, axis=0, keepdims=True)
        o = jnp.dot(v, e.astype(BF), preferred_element_type=F32) / total
        o_ref[0, :, at] = o.astype(BF)
        lse_ref[0, :, at] = top + jnp.log(total)


def attend_forward(attn_t, w_heads, times, tables, feats, scale):
    parts, heads, width, dm = w_heads.shape
    tokens = attn_t.shape[1]
    whole = lambda h: (0, 0)
    return pl.pallas_call(
        functools.partial(forward_kernel, scale=scale),
        grid=(heads,),
        in_specs=[
            pl.BlockSpec(attn_t.shape, whole),
            pl.BlockSpec((parts, 1, width, dm), lambda h: (0, h, 0, 0)),
            pl.BlockSpec((2, 1, width, 4), lambda h: (0, h, 0, 0)),
            pl.BlockSpec((1, RC, RC), lambda h: (h, 0, 0)),
            pl.BlockSpec(feats.shape, whole),
        ],
        out_specs=[
            pl.BlockSpec((parts, 1, width, tokens), lambda h: (0, h, 0, 0)),
            pl.BlockSpec((1, width, tokens), lambda h: (h, 0, 0)),
            pl.BlockSpec((1, 1, tokens), lambda h: (h, 0, 0)),
        ],
        out_shape=[
            jax.ShapeDtypeStruct((parts, heads, width, tokens), BF),
            jax.ShapeDtypeStruct((heads, width, tokens), BF),
            jax.ShapeDtypeStruct((heads, 1, tokens), F32),
        ],
        compiler_params=params("arbitrary"),
        cost_estimate=cost(
            2 * heads * tokens * (3 * width * dm + tokens * 512), 12e6, heads * tokens * tokens
        ),
        name="attention_forward",
    )(attn_t, w_heads, times, tables, feats)


def backward_kernel(
    qkv_ref, o_ref, do_ref, lse_ref, table_ref, feat_ref, d_ref, toe_ref, image_ref, *, scale
):
    width = o_ref.shape[1]
    tokens = o_ref.shape[2]
    q, k, v = (qkv_ref[p, 0] for p in range(3))
    do = do_ref[0]
    delta = jnp.sum(do.astype(F32) * o_ref[0].astype(F32), axis=0, keepdims=True)
    rc = feat_ref[:RC]
    bias = jnp.dot(table_ref[0], rc, preferred_element_type=F32).astype(BF)
    key_t = jnp.concatenate([feat_ref[:QUERY_MASK], k], axis=0)
    key = key_t.T
    value = v.T
    dk = jnp.zeros((tokens, width), F32)
    dv = jnp.zeros((tokens, width), F32)
    toe = jnp.zeros((RC, RC), F32)
    dq_parts = []
    for b in range(tokens // QUERY_BLOCK):
        at = slice(b * QUERY_BLOCK, (b + 1) * QUERY_BLOCK)
        query = jnp.concatenate(
            [bias[:, at], feat_ref[QUERY_MASK:IMAGE_HOT, at], q[:, at]], axis=0
        )
        s = jnp.dot(key, query, preferred_element_type=F32)
        p = jnp.exp(s - lse_ref[0, :, at])
        dp = jnp.dot(value, do[:, at], preferred_element_type=F32)
        ds = (p * (dp - delta[:, at])).astype(BF)
        dq = jnp.dot(key_t, ds, preferred_element_type=F32)
        dq_parts.append((dq[QUERY_MASK:] * scale).astype(BF))
        high = dq[:RC].astype(BF)
        low = (dq[:RC] - high.astype(F32)).astype(BF)
        toe = toe + dot(rc[:, at], high, 1, 1) + dot(rc[:, at], low, 1, 1)
        dk = dk + dot(ds, q[:, at], 1, 1)
        dv = dv + dot(p.astype(BF), do[:, at], 1, 1)
    dq = jnp.concatenate(dq_parts, axis=1)
    dk = dk.T.astype(BF)
    dv = dv.T.astype(BF)
    d_ref[0, 0] = dq
    d_ref[1, 0] = dk
    d_ref[2, 0] = dv
    toe_ref[0] = toe
    hot = feat_ref[IMAGE_HOT:]
    image_ref[0, 0] = dot(dq, hot, 1, 1)
    image_ref[1, 0] = dot(dv, hot, 1, 1)


def attend_backward(qkv, o, do, lse, tables, feats, scale, first, count):
    parts, heads, width, tokens = qkv.shape
    head3 = lambda h: (first + h, 0, 0)
    head4 = lambda h: (0, first + h, 0, 0)
    return pl.pallas_call(
        functools.partial(backward_kernel, scale=scale),
        grid=(count,),
        in_specs=[
            pl.BlockSpec((parts, 1, width, tokens), head4),
            pl.BlockSpec((1, width, tokens), head3),
            pl.BlockSpec((1, width, tokens), head3),
            pl.BlockSpec((1, 1, tokens), head3),
            pl.BlockSpec((1, RC, RC), head3),
            pl.BlockSpec(feats.shape, lambda h: (0, 0)),
        ],
        out_specs=[
            pl.BlockSpec((parts, 1, width, tokens), lambda h: (0, h, 0, 0)),
            pl.BlockSpec((1, RC, RC), lambda h: (h, 0, 0)),
            pl.BlockSpec((2, 1, width, 16), lambda h: (0, h, 0, 0)),
        ],
        out_shape=[
            jax.ShapeDtypeStruct((parts, count, width, tokens), BF),
            jax.ShapeDtypeStruct((count, RC, RC), F32),
            jax.ShapeDtypeStruct((2, count, width, 16), F32),
        ],
        compiler_params=params("arbitrary"),
        cost_estimate=cost(
            2 * count * tokens * tokens * 5 * 256, 2e6 * count, count * tokens * tokens
        ),
        name="attention_backward",
    )(qkv, o, do, lse, tables, feats)


def mlp_kernel(
    tile_ref, m_ref, mt_ref, g_ref, up_ref, down_ref, two_ref, gm_ref,
    two_out, gm_out, send_ref, own_ref, wd_ref,
):
    step = pl.program_id(0)

    @pl.when(step == 0)
    def _():
        two_out[...] = two_ref[...]
        gm_out[...] = gm_ref[...]

    up = jnp.dot(m_ref[...], up_ref[...], preferred_element_type=F32)
    half = 0.5 + 0.5 * lax.erf(up * math.sqrt(0.5))
    slope = half + up * (jnp.exp(-0.5 * up * up) * (1.0 / math.sqrt(2.0 * math.pi)))
    act = (up * half).astype(BF)
    two_out[...] += jnp.dot(act, down_ref[...], preferred_element_type=F32)
    du = (dot(g_ref[...], down_ref[...], 1, 1) * slope).astype(BF)
    gm_out[...] += dot(du, up_ref[...], 1, 1)
    wd_ref[...] = dot(act, g_ref[...], 0, 0).astype(BF)
    wu = jnp.dot(mt_ref[...], du, preferred_element_type=F32).astype(BF)

    @pl.when(step == 0)
    def _():
        send_ref[...] = wu

    @pl.when(step == 1)
    def _():
        own_ref[...] = wu


def mlp(tiles, m, mt, g, w_up, w_down, two, gm, tile):
    rows, dm = m.shape
    whole = lambda i, t: (0, 0)
    return pl.pallas_call(
        mlp_kernel,
        grid_spec=pltpu.PrefetchScalarGridSpec(
            num_scalar_prefetch=1,
            grid=(2,),
            in_specs=[
                pl.BlockSpec((rows, dm), whole),
                pl.BlockSpec((dm, rows), whole),
                pl.BlockSpec((rows, dm), whole),
                pl.BlockSpec((dm, tile), lambda i, t: (0, t[i])),
                pl.BlockSpec((tile, dm), lambda i, t: (t[i], 0)),
                pl.BlockSpec((rows, dm), whole),
                pl.BlockSpec((rows, dm), whole),
            ],
            out_specs=[
                pl.BlockSpec((rows, dm), whole),
                pl.BlockSpec((rows, dm), whole),
                pl.BlockSpec((dm, tile), whole),
                pl.BlockSpec((dm, tile), whole),
                pl.BlockSpec((tile, dm), lambda i, t: (lax.rem(t[i], 2), 0)),
            ],
        ),
        out_shape=[
            jax.ShapeDtypeStruct((rows, dm), F32),
            jax.ShapeDtypeStruct((rows, dm), F32),
            jax.ShapeDtypeStruct((dm, tile), BF),
            jax.ShapeDtypeStruct((dm, tile), BF),
            jax.ShapeDtypeStruct((2 * tile, dm), BF),
        ],
        compiler_params=params("arbitrary"),
        cost_estimate=cost(24 * rows * dm * tile, 25e6, 2 * rows * tile),
        name="feed_forward",
    )(tiles, m, mt, g, w_up, w_down, two, gm)


def ring_order(count):
    return list(range(0, count, 2)) + list(range(1, count, 2))[::-1]


def ring_reduce(job, direction, count):
    order = ring_order(count)
    place = [order.index(i) for i in range(count)]
    route = [(order[p], order[(p + direction) % count]) for p in range(count)]
    me = jnp.asarray(place, jnp.int32)[lax.axis_index("img")]
    table = jnp.asarray(order, jnp.int32)
    moving = None
    for step in range(count):
        chunk = table[(me - direction * (1 + step)) % count]
        term = job(chunk)
        total = term if moving is None else moving.astype(F32) + term
        if step == count - 1:
            return total
        moving = lax.ppermute(total.astype(BF), "img", route)


def pick(array, index, axis=0):
    return lax.dynamic_index_in_dim(array, index, axis, keepdims=False)


def mean(x):
    return jnp.mean(x, axis=-1, keepdims=True)


def normalised(x):
    centre = x - mean(x)
    root = lax.rsqrt(mean(centre * centre) + EPS)
    return centre * root, root


def norm_backward(d, n, root):
    return root * (d - mean(d) - n * mean(d * n))


def toeplitz_tables(rel, count):
    d = jnp.arange(2 * count - 1, dtype=jnp.int32)
    t = jnp.arange(count, dtype=jnp.int32)
    hot = (d[:, None, None] == t[None, None, :] - t[None, :, None] + count - 1).astype(BF)
    return jnp.einsum("hd,dtr->htr", rel.astype(BF), hot, preferred_element_type=F32)


def per_device(
    tokens, time_embed, image_lengths, grid_turns, ln1_gain, w_qkv, w_time_q, time_value_weight,
    rel_rows, rel_cols, output_projection_weight, ln2_gain, w_up, w_down, out_grad,
):
    slots, span, dm = tokens.shape
    heads = rel_rows.shape[0]
    width = dm // heads
    ff = w_up.shape[1]
    scale = width ** (-0.5)
    n_seq = lax.axis_size("seq")
    n_img = lax.axis_size("img")
    cores = n_seq // slots
    own_heads = heads // cores
    cols = own_heads * width
    me_img = lax.axis_index("img")
    me_seq = lax.axis_index("seq")
    y = me_seq // cores
    c = me_seq % cores
    mine = slots * span
    over_y = [(s, (slots - 1 - s // cores) * cores + s % cores) for s in range(n_seq)]
    over_core = [(s, s // cores * cores + cores - 1 - s % cores) for s in range(n_seq)]

    def swap_y(a):
        return lax.ppermute(a, "seq", over_y)

    def swap_core(a):
        return lax.ppermute(a, "seq", over_core)

    tok_own = pick(tokens, y)
    tok_rx = swap_y(pick(tokens, 1 - y))
    grad_own = pick(out_grad, y)
    grad_rx = swap_y(pick(out_grad, 1 - y))
    block = lambda yy, cc: (yy * cores + cc) * span
    bases = jnp.stack([block(y, c), block(1 - y, c), block(y, 1 - c), block(1 - y, 1 - c)])
    feats, valid = token_features(
        pick(image_lengths, y), pick(grid_turns, y), bases.astype(jnp.int32), span, mine
    )
    valid = valid[:, :1]

    x = jnp.concatenate([tok_own, tok_rx], axis=0).astype(F32)
    n_one, root_one = normalised(x)
    attn_mine = (n_one * ln1_gain).astype(BF)
    attn_sib = swap_core(attn_mine)
    attn_in = jnp.concatenate([attn_mine, attn_sib], axis=0)

    w_heads = pick(w_qkv.reshape(dm, 3, cores, own_heads, width), c, 2)
    w_heads = jnp.transpose(w_heads, (1, 2, 3, 0))
    te = pick(time_embed, y)
    time_pair = jnp.stack(
        [
            dot(lax.dynamic_slice_in_dim(w, c * cols, cols, 1), te, 0, 1)
            for w in (w_time_q, time_value_weight)
        ]
    ).reshape(2, own_heads, width, 4)
    te_all = lax.all_gather(time_embed, "img")
    row_table = toeplitz_tables(lax.dynamic_slice_in_dim(rel_rows, c * own_heads, own_heads), SIDE)
    col_table = toeplitz_tables(lax.dynamic_slice_in_dim(rel_cols, c * own_heads, own_heads), SIDE)
    gap = jnp.zeros_like(row_table)
    tables = jnp.concatenate(
        [
            jnp.concatenate([row_table, gap], axis=2),
            jnp.concatenate([gap, col_table], axis=2),
        ],
        axis=1,
    ).astype(BF)

    qkv, o_own, lse = attend_forward(attn_in.T, w_heads, time_pair, tables, feats, scale)

    o_far = swap_core(o_own).reshape(cols, 2 * mine)
    o_flat = o_own.reshape(cols, 2 * mine)
    o_far = jnp.concatenate([o_far[:, mine:], o_far[:, :mine]], axis=1)
    attn_all = jnp.concatenate(
        [jnp.where(c == 0, o_flat, o_far), jnp.where(c == 0, o_far, o_flat)], axis=0
    )
    branch_one = dot(attn_all[:, :mine], output_projection_weight, 0, 0)
    hidden_one = x + branch_one
    n_two, root_two = normalised(hidden_one)
    mlp_in = (n_two * ln2_gain).astype(BF)
    grad_two = jnp.concatenate([grad_own, grad_rx], axis=0).astype(F32) * valid
    grad_branch = grad_two.astype(BF)

    tile = ff // 4
    zero = jnp.zeros((mine, dm), F32)
    mlp_in_t = mlp_in.T
    pair = jnp.stack([1 - c, c]).astype(jnp.int32)
    two, gm, send_a, own_a, down_a = mlp(
        pair, mlp_in, mlp_in_t, grad_branch, w_up, w_down, zero, zero, tile
    )
    two, gm, send_b, own_b, down_b = mlp(
        2 + pair, mlp_in, mlp_in_t, grad_branch, w_up, w_down, two, gm, tile
    )
    rx_a = swap_core(send_a)
    rx_b = swap_core(send_b)
    low = ff // n_img // cores
    down = jnp.concatenate([down_a, down_b], axis=0).reshape(n_img, cores, low, dm)
    down_rx = swap_core(pick(down, 1 - c, 1))
    rows = dm // n_img

    def up_job(own, rx):
        own = own.reshape(n_img, rows, tile)
        rx = rx.reshape(n_img, rows, tile)
        return lambda i: pick(own, i).astype(F32) + pick(rx, i).astype(F32)

    def down_job(start, size):
        def term(i):
            at = lax.dynamic_slice(down, (i, c, start, 0), (1, 1, size, dm)).reshape(size, dm)
            far = lax.dynamic_slice(down_rx, (i, start, 0), (1, size, dm)).reshape(size, dm)
            return at.astype(F32) + far.astype(F32)

        return term

    up_a = ring_reduce(up_job(own_a, rx_a), 1, n_img)
    up_b = ring_reduce(up_job(own_b, rx_b), 1, n_img)
    down_lo = ring_reduce(down_job(0, low // 2), -1, n_img)
    down_hi = ring_reduce(down_job(low // 2, low // 2), -1, n_img)

    hidden_two = hidden_one + two
    output = (hidden_two * valid).astype(BF)
    stats = jnp.stack(
        [
            jnp.sum(valid * hidden_two * hidden_two),
            jnp.sum(valid * branch_one * branch_one),
            jnp.sum(valid * two * two),
            jnp.sum(valid),
        ]
    )
    ln2_grad = jnp.sum(gm * n_two, axis=0)
    grad_one = grad_two + norm_backward(gm * ln2_gain, n_two, root_two)
    gb_mine = grad_one.astype(BF)
    gb_all = jnp.concatenate([gb_mine, swap_core(gb_mine)], axis=0)
    w_proj_rows = lax.dynamic_slice_in_dim(output_projection_weight, c * cols, cols, 0)
    do = dot(w_proj_rows, gb_all, 1, 1).astype(BF).reshape(own_heads, width, 2 * mine)
    gb_cols = lax.dynamic_slice_in_dim(gb_all, c * cols, cols, 1)
    proj_part = dot(attn_all, gb_cols, 1, 0).astype(BF).reshape(n_img, rows, cols)
    proj = ring_reduce(lambda i: pick(proj_part, i).astype(F32), 1, n_img)

    group = 2
    pieces = [
        attend_backward(qkv, o_own, do, lse, tables, feats, scale, h, group)
        for h in range(0, own_heads, group)
    ]
    d = jnp.concatenate([p[0] for p in pieces], axis=1).reshape(3, cols, 2 * mine)
    toe = jnp.concatenate([p[1] for p in pieces], axis=0)
    image_grads = jnp.concatenate([p[2] for p in pieces], axis=1)[..., :4]

    w_v_part = dot(attn_in, d[2], 0, 1).astype(BF).reshape(n_img, rows, cols)
    w_qk_part = dot(attn_in, d[:2].reshape(2 * cols, 2 * mine), 0, 1)
    w_qk_part = w_qk_part.astype(BF).reshape(n_img, rows, 2 * cols)
    w_v = ring_reduce(lambda i: pick(w_v_part, i).astype(F32), 1, n_img)
    w_qk = ring_reduce(lambda i: pick(w_qk_part, i).astype(F32), -1, n_img)

    back = dot(d.reshape(3 * cols, 2 * mine), w_heads.reshape(3 * cols, dm), 0, 0)
    back = back[:mine] + swap_core(back[mine:].astype(BF)).astype(F32)
    ln1_grad = jnp.sum(back * n_one, axis=0)
    input_grad = (grad_one + norm_backward(back * ln1_gain, n_one, root_one)).astype(BF)

    def returned(a):
        own, far = a[:span], swap_y(a[span:])
        return jnp.stack([jnp.where(y == 0, own, far), jnp.where(y == 0, far, own)])

    output = returned(output)
    input_grad = returned(input_grad)

    images = lax.all_gather(image_grads.reshape(2, cols, 4), ("img", "seq"))
    images = images.reshape(n_img, slots, cores, 2, cols, 4)
    images = jnp.transpose(images, (3, 0, 1, 5, 2, 4)).reshape(2, n_img * slots * 4, dm)
    te_rows = lax.dynamic_slice_in_dim(te_all.reshape(n_img * slots * 4, dm), me_img * rows, rows, 1)
    te_rows = te_rows.astype(F32)
    w_time_q_grad = lax.dot_general(te_rows, images[0], (((0,), (0,)), ((), ())), precision=HIGH)
    w_time_v_grad = lax.dot_general(te_rows, images[1], (((0,), (0,)), ((), ())), precision=HIGH)

    reach = jnp.arange(2 * SIDE - 1, dtype=jnp.int32)
    side = jnp.arange(SIDE, dtype=jnp.int32)
    diag = (reach == side[:, None, None] - side[None, :, None] + SIDE - 1).astype(F32)
    rel = jnp.stack([toe[:, :SIDE, :SIDE], toe[:, SIDE:, SIDE:]])
    rel = jnp.einsum("khrt,rtd->khd", rel, diag, precision=HIGH)
    rel_all = lax.dynamic_update_slice(
        jnp.zeros((2, heads, 2 * SIDE - 1), F32), rel, (0, c * own_heads, 0)
    )
    small = jnp.concatenate([ln1_grad, ln2_grad, rel_all.reshape(-1), stats])
    small = lax.psum(small, ("img", "seq"))
    ln1_gain_grad = lax.dynamic_slice_in_dim(small, me_img * rows, rows)
    ln2_gain_grad = lax.dynamic_slice_in_dim(small, dm + me_img * rows, rows)
    rel_all = small[2 * dm : -4].reshape(2, heads, 2 * SIDE - 1)
    rms_values = jnp.sqrt(small[-4:-1] / (small[-1] * dm))

    def finish(part):
        part = part.astype(BF)
        part = (part.astype(F32) + swap_y(part).astype(F32)).astype(BF)
        far = swap_core(part)
        first = jnp.where(c == 0, part, far).astype(F32)
        second = jnp.where(c == 0, far, part).astype(F32)
        return first, second

    ups = finish(up_a) + finish(up_b)
    w_up_grad = jnp.concatenate(ups, axis=1)
    d0, d1 = finish(jnp.concatenate([down_lo, down_hi], axis=0))
    w_down_grad = jnp.concatenate([d0, d1], axis=0)
    w_proj_grad = jnp.concatenate(finish(proj), axis=1)
    v0, v1 = finish(w_v)
    q0, q1 = finish(w_qk)
    w_qkv_grad = jnp.concatenate([q0[:, :cols], q1[:, :cols], q0[:, cols:], q1[:, cols:], v0, v1], axis=1)
    return (
        output,
        input_grad,
        ln1_gain_grad,
        w_qkv_grad,
        w_time_q_grad,
        w_time_v_grad,
        rel_all[0],
        rel_all[1],
        w_proj_grad,
        ln2_gain_grad,
        w_up_grad,
        w_down_grad,
        rms_values,
    )


def solution(mesh):
    return jax.shard_map(
        per_device,
        mesh=mesh,
        in_specs=(
            P("img", "seq", None),
            P("img", None, None),
            P("img", None),
            P("img", None),
        )
        + (P(),) * 10
        + (P("img", "seq", None),),
        out_specs=(
            P("img", "seq", None),
            P("img", "seq", None),
            P("img"),
            P("img", None),
            P("img", None),
            P("img", None),
            P(),
            P(),
            P("img", None),
            P("img"),
            P("img", None),
            P("img", None),
            P(),
        ),
        check_vma=False,
    )
```

```python
import functools
import math

import jax
import jax.numpy as jnp
from jax import lax
from jax.experimental import pallas as pl
from jax.experimental.pallas import tpu as pltpu
from jax.sharding import PartitionSpec as P

SIDE = 32
EPS = 1e-06
FAR = -1e30
LANES = 128
BF = jnp.bfloat16
F32 = jnp.float32
VMEM_LIMIT = 56 * 2**20
QUERY_BLOCK = 256
FF_STEP = 256

RC = 2 * SIDE
KEY_MASK = RC
QUERY_MASK = KEY_MASK + 16
IMAGE_HOT = QUERY_MASK + 16
FEATURES = IMAGE_HOT + 16
ANYWHERE = pl.BlockSpec(memory_space=pl.ANY)


def dot(a, b, ca, cb):
    return lax.dot_general(a, b, (((ca,), (cb,)), ((), ())), preferred_element_type=F32)


def params(*semantics):
    return pltpu.CompilerParams(dimension_semantics=semantics, vmem_limit_bytes=VMEM_LIMIT)


CHEAP = pl.CostEstimate(flops=10**6, bytes_accessed=10**5, transcendentals=0)


def features_kernel(len_ref, turn_ref, base_ref, feat_ref, valid_ref, *, span):
    tokens = feat_ref.shape[1]

    def describe(shape, axis):
        index = lax.broadcasted_iota(jnp.int32, shape, axis)
        block = index // span
        pos = index - block * span
        for k in range(tokens // span):
            pos = pos + jnp.where(block == k, base_ref[k], 0)
        ends = []
        total = 0
        for j in range(4):
            total = total + len_ref[j]
            ends.append(total)
        segment = sum((pos >= ends[j]).astype(jnp.int32) for j in range(4))
        return pos, ends, segment

    pos, ends, segment = describe((1, tokens), 1)
    picked = jnp.minimum(segment, 3)
    begin = jnp.zeros_like(pos)
    length = jnp.zeros_like(pos)
    turn = jnp.zeros_like(pos)
    for j in range(4):
        here = picked == j
        begin = jnp.where(here, ends[j] - len_ref[j], begin)
        length = jnp.where(here, len_ref[j], length)
        turn = jnp.where(here, turn_ref[j], turn)
    full = length == SIDE * SIDE
    side = jnp.where(full, SIDE, SIDE // 2)
    u = pos - begin
    bits = SIDE.bit_length() - 1
    r0 = jnp.where(full, u >> bits, u >> (bits - 1))
    c0 = u & (side - 1)
    r1 = jnp.where((turn & 1) == 1, side - 1 - r0, r0)
    c1 = jnp.where(((turn >> 1) & 1) == 1, side - 1 - c0, c0)
    valid = pos < ends[3]
    row = jnp.where(valid, jnp.where(turn >= 4, c1, r1), 0)
    col = jnp.where(valid, jnp.where(turn >= 4, r1, c1), 0)
    which = lax.broadcasted_iota(jnp.int32, (SIDE, tokens), 0)
    few = lax.broadcasted_iota(jnp.int32, (16, tokens), 0)

    def put(start, value):
        feat_ref[start : start + value.shape[0], :] = value.astype(BF)

    put(0, jnp.where(which == row, 1.0, 0.0))
    put(SIDE, jnp.where(which == col, 1.0, 0.0))
    put(KEY_MASK, jnp.where(few == segment, 1.0, 0.0))
    put(QUERY_MASK, jnp.where((few < 5) & (few != segment), FAR, 0.0))
    put(IMAGE_HOT, jnp.where(few == picked, 1.0, 0.0))
    down_pos, down_ends, unused = describe(valid_ref.shape, 0)
    valid_ref[...] = jnp.where(down_pos < down_ends[3], 1.0, 0.0)


def token_features(lengths, turns, bases, span, mine):
    tokens = bases.shape[0] * span
    smem = pl.BlockSpec(memory_space=pltpu.SMEM)
    return pl.pallas_call(
        functools.partial(features_kernel, span=span),
        out_shape=(
            jax.ShapeDtypeStruct((FEATURES, tokens), BF),
            jax.ShapeDtypeStruct((mine, LANES), F32),
        ),
        in_specs=[smem, smem, smem],
        cost_estimate=CHEAP,
        name="token_features",
    )(lengths, turns, bases)


def window(cols):
    return -(-(cols + LANES // 2) // LANES) * LANES


def fetch(part, core, w_ref, room, sems, cols, dm):
    start = part * dm + (core * cols) // LANES * LANES
    start = pl.multiple_of(start, LANES)
    return pltpu.make_async_copy(
        w_ref.at[:, pl.ds(start, room.shape[2])], room.at[part], sems.at[part]
    )


def project_kernel(
    core_ref, a_ref, b_ref, c_ref, d_ref, gain_ref, time_ref, feat_ref, w_ref,
    in_ref, qkv_ref, room, wide, sems, *, scale, cols,
):
    part = pl.program_id(0)
    core = core_ref[0]
    dm = in_ref.shape[1]
    width = qkv_ref.shape[2]

    @pl.when(part == 0)
    def _():
        for k in range(3):
            fetch(k, core, w_ref, room, sems, cols, dm).start()
        rows = a_ref.shape[0]
        for k, ref in enumerate((a_ref, b_ref, c_ref, d_ref)):
            x = ref[...].astype(F32)
            centre = x - jnp.mean(x, axis=-1, keepdims=True)
            spread = jnp.mean(centre * centre, axis=-1, keepdims=True)
            normed = centre * lax.rsqrt(spread + EPS) * gain_ref[...]
            in_ref[k * rows : (k + 1) * rows, :] = normed.astype(BF)

    fetch(part, core, w_ref, room, sems, cols, dm).wait()
    wide[...] = dot(room[part], in_ref[...], 0, 1)
    shift = core * cols - (core * cols) // LANES * LANES
    factor = jnp.where(part == 0, scale, 1.0)
    hot = feat_ref[IMAGE_HOT:, :].astype(F32)
    for h in range(cols // width):
        at = pl.multiple_of(shift + h * width, 8)
        x = wide[pl.ds(at, width), :]
        t = time_ref[0, h * width : (h + 1) * width, :]
        for j in range(4):
            x = x + t[:, j : j + 1] * hot[j : j + 1]
        qkv_ref[0, h] = (x * factor).astype(BF)


def project(core, blocks, gain, times, feats, w_qkv, scale, heads):
    rows, dm = blocks[0].shape
    tokens = 4 * rows
    cols = times.shape[1]
    width = cols // heads
    whole = lambda p, t: (0, 0)
    room = window(cols)
    return pl.pallas_call(
        functools.partial(project_kernel, scale=scale, cols=cols),
        grid_spec=pltpu.PrefetchScalarGridSpec(
            num_scalar_prefetch=1,
            grid=(3,),
            in_specs=[pl.BlockSpec((rows, dm), whole)] * 4
            + [
                pl.BlockSpec((1, dm), whole),
                pl.BlockSpec((1, cols, 4), lambda p, t: (p, 0, 0)),
                pl.BlockSpec(feats.shape, whole),
                ANYWHERE,
            ],
            out_specs=[
                pl.BlockSpec((tokens, dm), whole),
                pl.BlockSpec((1, heads, width, tokens), lambda p, t: (p, 0, 0, 0)),
            ],
            scratch_shapes=[
                pltpu.VMEM((3, dm, room), BF),
                pltpu.VMEM((room, tokens), F32),
                pltpu.SemaphoreType.DMA((3,)),
            ],
        ),
        out_shape=[
            jax.ShapeDtypeStruct((tokens, dm), BF),
            jax.ShapeDtypeStruct((3, heads, width, tokens), BF),
        ],
        compiler_params=params("arbitrary"),
        cost_estimate=CHEAP,
        name="project",
    )(core, *blocks, gain, times, feats, w_qkv)


def weights_kernel(clock_ref, in_ref, d_ref, out_ref):
    d = jnp.concatenate([d_ref[0, h].astype(F32) for h in range(d_ref.shape[1])], axis=0)
    out_ref[0] = dot(in_ref[...], d.astype(BF), 0, 1).astype(BF)


def project_weights(clock, attn_in, d):
    parts, heads, width, tokens = d.shape
    dm = attn_in.shape[1]
    return pl.pallas_call(
        weights_kernel,
        grid_spec=pltpu.PrefetchScalarGridSpec(
            num_scalar_prefetch=1,
            grid=(parts,),
            in_specs=[
                pl.BlockSpec((tokens, dm), lambda p, t: (0, 0)),
                pl.BlockSpec((1, heads, width, tokens), lambda p, t: (p, 0, 0, 0)),
            ],
            out_specs=pl.BlockSpec((1, dm, heads * width), lambda p, t: (p, 0, 0)),
        ),
        out_shape=jax.ShapeDtypeStruct((parts, dm, heads * width), BF),
        compiler_params=params("arbitrary"),
        cost_estimate=CHEAP,
        name="project_weights",
    )(clock, attn_in, d)


def project_back_kernel(
    clock_ref, core_ref, d_ref, w_ref, mine_ref, far_ref, room, wide, total, sems, *, cols
):
    part = pl.program_id(0)
    core = core_ref[0]
    dm = w_ref.shape[0]
    width = d_ref.shape[2]

    @pl.when(part == 0)
    def _():
        for k in range(3):
            fetch(k, core, w_ref, room, sems, cols, dm).start()
        wide[...] = jnp.zeros_like(wide)

    shift = core * cols - (core * cols) // LANES * LANES
    for h in range(cols // width):
        at = pl.multiple_of(shift + h * width, 8)
        wide[pl.ds(at, width), :] = d_ref[0, h].astype(F32)
    fetch(part, core, w_ref, room, sems, cols, dm).wait()
    term = dot(wide[...].astype(BF), room[part], 0, 1)

    @pl.when(part == 0)
    def _():
        total[...] = term

    @pl.when(part == 1)
    def _():
        total[...] += term

    @pl.when(part == 2)
    def _():
        rows = mine_ref.shape[0]
        mine_ref[...] = total[:rows, :] + term[:rows]
        far_ref[...] = (total[rows:, :] + term[rows:]).astype(BF)


def project_back(clock, core, d, w_qkv, mine):
    parts, heads, width, tokens = d.shape
    dm = w_qkv.shape[0]
    cols = heads * width
    room = window(cols)
    whole = lambda p, t, u: (0, 0)
    return pl.pallas_call(
        functools.partial(project_back_kernel, cols=cols),
        grid_spec=pltpu.PrefetchScalarGridSpec(
            num_scalar_prefetch=2,
            grid=(parts,),
            in_specs=[
                pl.BlockSpec((1, heads, width, tokens), lambda p, t, u: (p, 0, 0, 0)),
                ANYWHERE,
            ],
            out_specs=[pl.BlockSpec((mine, dm), whole), pl.BlockSpec((tokens - mine, dm), whole)],
            scratch_shapes=[
                pltpu.VMEM((3, dm, room), BF),
                pltpu.VMEM((room, tokens), F32),
                pltpu.VMEM((tokens, dm), F32),
                pltpu.SemaphoreType.DMA((3,)),
            ],
        ),
        out_shape=[
            jax.ShapeDtypeStruct((mine, dm), F32),
            jax.ShapeDtypeStruct((tokens - mine, dm), BF),
        ],
        compiler_params=params("arbitrary"),
        cost_estimate=CHEAP,
        name="project_back",
    )(clock, core, d, w_qkv)


def forward_kernel(clock_ref, p_ref, table_ref, feat_ref, o_ref, lse_ref):
    tokens = p_ref.shape[3]
    q, k, v = (p_ref[p, 0] for p in range(3))
    bias = jnp.dot(table_ref[0], feat_ref[:RC], preferred_element_type=F32).astype(BF)
    key = jnp.concatenate([feat_ref[:QUERY_MASK], k], axis=0).T
    for b in range(tokens // QUERY_BLOCK):
        at = slice(b * QUERY_BLOCK, (b + 1) * QUERY_BLOCK)
        query = jnp.concatenate(
            [bias[:, at], feat_ref[QUERY_MASK:IMAGE_HOT, at], q[:, at]], axis=0
        )
        s = jnp.dot(key, query, preferred_element_type=F32)
        top = jnp.max(s, axis=0, keepdims=True)
        e = jnp.exp(s - top)
        total = jnp.sum(e, axis=0, keepdims=True)
        o = jnp.dot(v, e.astype(BF), preferred_element_type=F32) / total
        o_ref[0, :, at] = o.astype(BF)
        lse_ref[0, :, at] = top + jnp.log(total)


def attend_forward(clock, qkv, tables, feats, first, count):
    parts, heads, width, tokens = qkv.shape
    return pl.pallas_call(
        forward_kernel,
        grid_spec=pltpu.PrefetchScalarGridSpec(
            num_scalar_prefetch=1,
            grid=(count,),
            in_specs=[
                pl.BlockSpec((parts, 1, width, tokens), lambda h, t: (0, first + h, 0, 0)),
                pl.BlockSpec((1, RC, RC), lambda h, t: (first + h, 0, 0)),
                pl.BlockSpec(feats.shape, lambda h, t: (0, 0)),
            ],
            out_specs=[
                pl.BlockSpec((1, width, tokens), lambda h, t: (h, 0, 0)),
                pl.BlockSpec((1, 1, tokens), lambda h, t: (h, 0, 0)),
            ],
        ),
        out_shape=[
            jax.ShapeDtypeStruct((count, width, tokens), BF),
            jax.ShapeDtypeStruct((count, 1, tokens), F32),
        ],
        compiler_params=params("arbitrary"),
        cost_estimate=CHEAP,
        name="attention_forward",
    )(clock, qkv, tables, feats)


def backward_kernel(clock_ref, qkv_ref, o_ref, do_ref, lse_ref, table_ref, feat_ref, *rest, scale):
    d_ref, toe_ref, image_ref = rest[-3:]
    width = o_ref.shape[1]
    tokens = o_ref.shape[2]
    q, k, v = (qkv_ref[p, 0] for p in range(3))
    do = do_ref[0]
    delta = jnp.sum(do.astype(F32) * o_ref[0].astype(F32), axis=0, keepdims=True)
    rc = feat_ref[:RC]
    bias = jnp.dot(table_ref[0], rc, preferred_element_type=F32).astype(BF)
    key_t = jnp.concatenate([feat_ref[:QUERY_MASK], k], axis=0)
    key = key_t.T
    value = v.T
    dk = jnp.zeros((tokens, width), F32)
    dv = jnp.zeros((tokens, width), F32)
    toe = jnp.zeros((RC, RC), F32)
    dq_parts = []
    for b in range(tokens // QUERY_BLOCK):
        at = slice(b * QUERY_BLOCK, (b + 1) * QUERY_BLOCK)
        query = jnp.concatenate(
            [bias[:, at], feat_ref[QUERY_MASK:IMAGE_HOT, at], q[:, at]], axis=0
        )
        s = jnp.dot(key, query, preferred_element_type=F32)
        p = jnp.exp(s - lse_ref[0, :, at])
        dp = jnp.dot(value, do[:, at], preferred_element_type=F32)
        ds = (p * (dp - delta[:, at])).astype(BF)
        dq = jnp.dot(key_t, ds, preferred_element_type=F32)
        dq_parts.append((dq[QUERY_MASK:] * scale).astype(BF))
        high = dq[:RC].astype(BF)
        low = (dq[:RC] - high.astype(F32)).astype(BF)
        toe = toe + dot(rc[:, at], high, 1, 1) + dot(rc[:, at], low, 1, 1)
        dk = dk + dot(ds, q[:, at], 1, 1)
        dv = dv + dot(p.astype(BF), do[:, at], 1, 1)
    dq = jnp.concatenate(dq_parts, axis=1)
    dk = dk.T.astype(BF)
    dv = dv.T.astype(BF)
    d_ref[0, 0] = dq
    d_ref[1, 0] = dk
    d_ref[2, 0] = dv
    toe_ref[0] = toe
    hot = feat_ref[IMAGE_HOT:]
    image_ref[0, 0] = dot(hot, dq, 1, 1)
    image_ref[1, 0] = dot(hot, dv, 1, 1)


def attend_backward(clock, qkv, o, do, lse, tables, feats, scale, first, count, before):
    parts, heads, width, tokens = qkv.shape
    head3 = lambda h, t: (first + h, 0, 0)
    head4 = lambda h, t: (0, first + h, 0, 0)
    return pl.pallas_call(
        functools.partial(backward_kernel, scale=scale),
        grid_spec=pltpu.PrefetchScalarGridSpec(
            num_scalar_prefetch=1,
            grid=(count,),
            in_specs=[
                pl.BlockSpec((parts, 1, width, tokens), head4),
                pl.BlockSpec((1, width, tokens), head3),
                pl.BlockSpec((1, width, tokens), head3),
                pl.BlockSpec((1, 1, tokens), head3),
                pl.BlockSpec((1, RC, RC), head3),
                pl.BlockSpec(feats.shape, lambda h, t: (0, 0)),
            ]
            + [ANYWHERE] * len(before),
            out_specs=[
                pl.BlockSpec((parts, 1, width, tokens), head4),
                pl.BlockSpec((1, RC, RC), head3),
                pl.BlockSpec((2, 1, 16, width), head4),
            ],
        ),
        out_shape=[
            jax.ShapeDtypeStruct((parts, heads, width, tokens), BF),
            jax.ShapeDtypeStruct((heads, RC, RC), F32),
            jax.ShapeDtypeStruct((2, heads, 16, width), F32),
        ],
        input_output_aliases={7 + k: k for k in range(len(before))},
        compiler_params=params("arbitrary"),
        cost_estimate=CHEAP,
        name="attention_backward",
    )(clock, qkv, o, do, lse, tables, feats, *before)


def rise_kernel(m_ref, g_ref, up_ref, down_ref, two_ref, slope_ref, wd_ref, mt_ref):
    @pl.when(pl.program_id(0) == 0)
    def _():
        two_ref[...] = jnp.zeros_like(two_ref)
        mt_ref[...] = m_ref[...].T

    acts = []
    for j in range(0, up_ref.shape[1], FF_STEP):
        at = slice(j, j + FF_STEP)
        up = jnp.dot(m_ref[...], up_ref[:, at], preferred_element_type=F32)
        half = 0.5 + 0.5 * lax.erf(up * math.sqrt(0.5))
        slope = half + up * (jnp.exp(-0.5 * up * up) * (1.0 / math.sqrt(2.0 * math.pi)))
        slope_ref[:, at] = slope.astype(BF)
        act = (up * half).astype(BF)
        acts.append(act)
        wd_ref[at, :] = dot(act, g_ref[...], 0, 0).astype(BF)
    two_ref[...] += jnp.dot(
        jnp.concatenate(acts, axis=1), down_ref[...], preferred_element_type=F32
    )


def mlp_rise(m, g, w_up, w_down, tile):
    rows, dm = m.shape
    ff = w_up.shape[1]
    whole = lambda i: (0, 0)
    return pl.pallas_call(
        rise_kernel,
        grid=(ff // tile,),
        in_specs=[
            pl.BlockSpec((rows, dm), whole),
            pl.BlockSpec((rows, dm), whole),
            pl.BlockSpec((dm, tile), lambda i: (0, i)),
            pl.BlockSpec((tile, dm), lambda i: (i, 0)),
        ],
        out_specs=[
            pl.BlockSpec((rows, dm), whole),
            pl.BlockSpec((rows, tile), lambda i: (0, i)),
            pl.BlockSpec((tile, dm), lambda i: (i, 0)),
            pl.BlockSpec((dm, rows), whole),
        ],
        out_shape=[
            jax.ShapeDtypeStruct((rows, dm), F32),
            jax.ShapeDtypeStruct((rows, ff), BF),
            jax.ShapeDtypeStruct((ff, dm), BF),
            jax.ShapeDtypeStruct((dm, rows), BF),
        ],
        compiler_params=params("arbitrary"),
        cost_estimate=CHEAP,
        name="feed_forward_rise",
    )(m, g, w_up, w_down)


def fall_kernel(clock_ref, tile_ref, mt_ref, g_ref, up_ref, down_ref, slope_ref, *rest):
    gm_out, send_ref, own_ref = rest[-3:]
    step = pl.program_id(0)

    @pl.when(step == 0)
    def _():
        gm_out[...] = rest[0][...] if len(rest) > 3 else jnp.zeros_like(gm_out)

    du = (dot(g_ref[...], down_ref[...], 1, 1) * slope_ref[...].astype(F32)).astype(BF)
    gm_out[...] += dot(du, up_ref[...], 1, 1)
    wu = jnp.dot(mt_ref[...], du, preferred_element_type=F32).astype(BF)

    @pl.when(step % 2 == 0)
    def _():
        send_ref[...] = wu

    @pl.when(step % 2 == 1)
    def _():
        own_ref[...] = wu


def mlp_fall(clock, tiles, mt, g, w_up, w_down, slope, tile, first, pairs, before):
    dm, rows = mt.shape
    ff = w_up.shape[1]
    whole = lambda i, u, t: (0, 0)
    column = lambda i, u, t: (0, first + i // 2)
    at = lambda i, t: 2 * (first + i // 2) + t[i % 2]
    return pl.pallas_call(
        fall_kernel,
        grid_spec=pltpu.PrefetchScalarGridSpec(
            num_scalar_prefetch=2,
            grid=(2 * pairs,),
            in_specs=[
                pl.BlockSpec((dm, rows), whole),
                pl.BlockSpec((rows, dm), whole),
                pl.BlockSpec((dm, tile), lambda i, u, t: (0, at(i, t))),
                pl.BlockSpec((tile, dm), lambda i, u, t: (at(i, t), 0)),
                pl.BlockSpec((rows, tile), lambda i, u, t: (0, at(i, t))),
            ]
            + ([pl.BlockSpec((rows, dm), whole), ANYWHERE, ANYWHERE] if before else []),
            out_specs=[
                pl.BlockSpec((rows, dm), whole),
                pl.BlockSpec((dm, tile), column),
                pl.BlockSpec((dm, tile), column),
            ],
        ),
        out_shape=[
            jax.ShapeDtypeStruct((rows, dm), F32),
            jax.ShapeDtypeStruct((dm, ff // 2), BF),
            jax.ShapeDtypeStruct((dm, ff // 2), BF),
        ],
        input_output_aliases={8: 1, 9: 2} if before else {},
        compiler_params=params("arbitrary"),
        cost_estimate=CHEAP,
        name="feed_forward_fall",
    )(clock, tiles, mt, g, w_up, w_down, slope, *before)


def moments(x):
    centre = x - jnp.mean(x, axis=-1, keepdims=True)
    root = lax.rsqrt(jnp.mean(centre * centre, axis=-1, keepdims=True) + EPS)
    return centre * root, root


def norm_backward(d, n, root):
    return root * (
        d - jnp.mean(d, axis=-1, keepdims=True) - n * jnp.mean(d * n, axis=-1, keepdims=True)
    )


def columns(x):
    return jnp.sum(x, axis=0, keepdims=True)


def middle_kernel(
    clock_ref, gm_ref, two_ref, one_ref, h_ref, g_ref, valid_ref, gain_ref,
    out_ref, grad_ref, low_ref, sums_ref,
):
    @pl.when(pl.program_id(0) == 0)
    def _():
        sums_ref[...] = jnp.zeros_like(sums_ref)

    valid = valid_ref[:, :1]
    two, one, h = two_ref[...], one_ref[...], h_ref[...]
    h2 = h + two
    out_ref[...] = (h2 * valid).astype(BF)
    n, root = moments(h)
    gm = gm_ref[...]
    grad = g_ref[...].astype(F32) * valid + norm_backward(gm * gain_ref[...], n, root)
    grad_ref[...] = grad
    low_ref[...] = grad.astype(BF)
    sums_ref[0:1, :] += columns(gm * n)
    sums_ref[1:2, :] += columns(valid * h2 * h2)
    sums_ref[2:3, :] += columns(valid * one * one)
    sums_ref[3:4, :] += columns(valid * two * two)


def middle(clock, gm, two, one, hidden, grads, valid, gain):
    rows, dm = gm.shape
    step = rows // 4
    block = pl.BlockSpec((step, dm), lambda i, t: (i, 0))
    return pl.pallas_call(
        middle_kernel,
        grid_spec=pltpu.PrefetchScalarGridSpec(
            num_scalar_prefetch=1,
            grid=(4,),
            in_specs=[block] * 5
            + [
                pl.BlockSpec((step, LANES), lambda i, t: (i, 0)),
                pl.BlockSpec((1, dm), lambda i, t: (0, 0)),
            ],
            out_specs=[block, block, block, pl.BlockSpec((8, dm), lambda i, t: (0, 0))],
        ),
        out_shape=[
            jax.ShapeDtypeStruct((rows, dm), BF),
            jax.ShapeDtypeStruct((rows, dm), F32),
            jax.ShapeDtypeStruct((rows, dm), BF),
            jax.ShapeDtypeStruct((8, dm), F32),
        ],
        compiler_params=params("arbitrary"),
        cost_estimate=CHEAP,
        name="middle",
    )(clock, gm, two, one, hidden, grads, valid, gain)


def last_kernel(back_ref, far_ref, x_ref, grad_ref, gain_ref, out_ref, sums_ref):
    @pl.when(pl.program_id(0) == 0)
    def _():
        sums_ref[...] = jnp.zeros_like(sums_ref)

    back = back_ref[...] + far_ref[...].astype(F32)
    n, root = moments(x_ref[...].astype(F32))
    out_ref[...] = (grad_ref[...] + norm_backward(back * gain_ref[...], n, root)).astype(BF)
    sums_ref[0:1, :] += columns(back * n)


def last(back, far, x, grad, gain):
    rows, dm = back.shape
    step = rows // 4
    block = pl.BlockSpec((step, dm), lambda i: (i, 0))
    return pl.pallas_call(
        last_kernel,
        grid=(4,),
        in_specs=[block] * 4 + [pl.BlockSpec((1, dm), lambda i: (0, 0))],
        out_specs=[block, pl.BlockSpec((8, dm), lambda i: (0, 0))],
        out_shape=[jax.ShapeDtypeStruct((rows, dm), BF), jax.ShapeDtypeStruct((8, dm), F32)],
        compiler_params=params("arbitrary"),
        cost_estimate=CHEAP,
        name="last",
    )(back, far, x, grad, gain)


class Halving:
    def __init__(self, names, dims, base, piece, prefix=(), suffix=(), column=0):
        self.names, self.dims, self.base, self.piece = names, dims, base, piece
        self.prefix, self.suffix, self.column = prefix, suffix, column
        self.stage, self.arrived, self.result = 0, [], None

    def left(self, stage):
        return [d for d in self.names if d in self.dims[stage + 1 :]]

    def specs(self, gridded):
        stage = self.stage
        open_dims = self.left(stage)

        def index(names, prefix, suffix, column):
            def at(*grid):
                t = grid[-1]
                out = list(prefix)
                for d in names:
                    if d in gridded:
                        out.append(grid[gridded.index(d)])
                    elif d in open_dims:
                        out.append(0)
                    elif stage < len(self.dims) and d == self.dims[stage]:
                        out.append(1 - t[d])
                    else:
                        out.append(t[d])
                return tuple(out) + tuple(suffix) + (0, column)

            return at

        def block(names, prefix, suffix):
            sizes = [2 if d in open_dims and d not in gridded else None for d in names]
            return (None,) * len(prefix) + tuple(sizes) + (None,) * len(suffix) + self.piece

        arrays, specs = [], []
        for array in self.base:
            arrays.append(array)
            specs.append(
                pl.BlockSpec(
                    block(self.names, self.prefix, self.suffix),
                    index(self.names, self.prefix, self.suffix, self.column),
                )
            )
        for s, (array, place) in enumerate(self.arrived):
            arrays.append(array)
            names = self.left(s)
            specs.append(pl.BlockSpec(block(names, (place,), ()), index(names, (place,), (), 0)))
        rest = index(open_dims, (), (), 0)
        inner = tuple(2 if d not in gridded else None for d in open_dims) + self.piece
        return arrays, specs, inner, rest, (2,) * len(open_dims) + self.piece


def sum_kernel(coord_ref, *refs, counts, places):
    outs = refs[sum(counts) :]
    at = 0
    for (out, place), count in zip(places, counts):
        total = refs[at][...].astype(F32)
        for k in range(1, count):
            total = total + refs[at + k][...].astype(F32)
        outs[out][place] = total.astype(BF)
        at += count


def advance(clock, swaps, jobs):
    arrays, in_specs, counts, groups, places = [], [], [], [], []
    stage = jobs[0].stage
    steps = min(2, max(0, len(jobs[0].left(stage)) - 1))
    for job in jobs:
        some, their, inner, rest, shape = job.specs(job.left(stage)[:steps])
        arrays, in_specs = arrays + some, in_specs + their
        counts.append(len(some))
        sent = job.dims[stage] if stage < len(job.dims) else None
        key = (sent, shape)
        found = [k for k, g in enumerate(groups) if g[0] == key]
        if not found:
            groups.append((key, inner, rest, []))
        group = found[0] if found else len(groups) - 1
        places.append((group, len(groups[group][3])))
        groups[group][3].append(job)
    out_specs = [
        pl.BlockSpec((len(g[3]),) + g[1], lambda *grid, f=g[2]: (0,) + f(*grid)) for g in groups
    ]
    sums = pl.pallas_call(
        functools.partial(sum_kernel, counts=counts, places=places),
        grid_spec=pltpu.PrefetchScalarGridSpec(
            num_scalar_prefetch=1,
            grid=(2,) * steps if steps else (1,),
            in_specs=in_specs,
            out_specs=out_specs,
        ),
        out_shape=[jax.ShapeDtypeStruct((len(g[3]),) + g[0][1], BF) for g in groups],
        compiler_params=params(*("arbitrary",) * max(steps, 1)),
        cost_estimate=CHEAP,
        name="sum_pieces",
    )(clock.now, *arrays)
    for (key, inner, rest, members), total in zip(groups, sums):
        if key[0] is not None:
            total = swaps[key[0]](total)
        for k, job in enumerate(members):
            if key[0] is None:
                job.result = total[k]
            else:
                job.arrived.append((total, k))
                job.stage += 1
    clock.passed(*sums)


class Clock:
    def __init__(self, now):
        self.now = now

    def passed(self, *results):
        self.now = lax.optimization_barrier((self.now, *results))[0]

    def tie(self, x):
        return lax.optimization_barrier((x, self.now))[0]


def gather_img(a):
    count = lax.axis_size("img")
    me = lax.axis_index("img")
    a = a[None]
    reach = 1
    while reach < count:
        far = lax.ppermute(a, "img", [(i, i ^ reach) for i in range(count)])
        upper = (me // reach) % 2 == 1
        a = jnp.concatenate([jnp.where(upper, far, a), jnp.where(upper, a, far)], axis=0)
        reach *= 2
    return a


def sum_all(a, swaps):
    for swap in swaps:
        a = a + swap(a)
    count = lax.axis_size("img")
    reach = 1
    while reach < count:
        a = a + lax.ppermute(a, "img", [(i, i ^ reach) for i in range(count)])
        reach *= 2
    return a


def pick(array, index, axis=0):
    return lax.dynamic_index_in_dim(array, index, axis, keepdims=False)


def toeplitz_tables(rel, count):
    d = jnp.arange(2 * count - 1, dtype=jnp.int32)
    t = jnp.arange(count, dtype=jnp.int32)
    hot = (d[:, None, None] == t[None, None, :] - t[None, :, None] + count - 1).astype(BF)
    return jnp.einsum("hd,dtr->htr", rel.astype(BF), hot, preferred_element_type=F32)


def per_device(
    tokens, time_embed, image_lengths, grid_turns, ln1_gain, w_qkv, w_time_q, time_value_weight,
    rel_rows, rel_cols, output_projection_weight, ln2_gain, w_up, w_down, out_grad,
):
    slots, span, dm = tokens.shape
    heads = rel_rows.shape[0]
    width = dm // heads
    ff = w_up.shape[1]
    scale = width ** (-0.5)
    n_seq = lax.axis_size("seq")
    n_img = lax.axis_size("img")
    cores = n_seq // slots
    own_heads = heads // cores
    cols = own_heads * width
    me_img = lax.axis_index("img")
    me_seq = lax.axis_index("seq")
    y = me_seq // cores
    c = me_seq % cores
    mine = slots * span
    rows = dm // n_img
    over_y = [(s, (slots - 1 - s // cores) * cores + s % cores) for s in range(n_seq)]
    over_core = [(s, s // cores * cores + cores - 1 - s % cores) for s in range(n_seq)]

    def swap_y(a):
        return lax.ppermute(a, "seq", over_y)

    def swap_core(a):
        return lax.ppermute(a, "seq", over_core)

    bits = n_img.bit_length() - 1
    on_y, on_core = bits, bits + 1
    swaps = {
        k: functools.partial(
            lax.ppermute, axis_name="img", perm=[(i, i ^ (1 << k)) for i in range(n_img)]
        )
        for k in range(bits)
    }
    swaps[on_y], swaps[on_core] = swap_y, swap_core

    def across_y(parts):
        part = jnp.concatenate(parts, axis=1)
        return part, swap_y(part)

    def across_core(part, far):
        part = jnp.concatenate([jnp.where(y == 0, part, far), jnp.where(y == 0, far, part)], axis=0)
        return part, swap_core(part)

    def both_cores(part, far):
        return jnp.where(c == 0, part, far).astype(F32), jnp.where(c == 0, far, part).astype(F32)

    def spread(parts):
        return both_cores(*across_core(*across_y(parts)))

    def order(*first):
        return list(first) + [k for k in range(bits) if k not in first]

    tok_own = pick(tokens, y)
    tok_rx = swap_y(pick(tokens, 1 - y))
    tok_own_far = swap_core(tok_own)
    block = lambda yy, cc: (yy * cores + cc) * span
    bases = jnp.stack([block(y, c), block(1 - y, c), block(y, 1 - c), block(1 - y, 1 - c)])
    feats, valid = token_features(
        pick(image_lengths, y), pick(grid_turns, y), bases.astype(jnp.int32), span, mine
    )
    coords = jnp.stack([(me_img >> k) & 1 for k in range(bits)] + [y, c]).astype(jnp.int32)
    core = c.astype(jnp.int32).reshape(1)
    pair = jnp.stack([1 - c, c]).astype(jnp.int32)
    te = pick(time_embed, y)

    def time_terms(w):
        all_heads = dot(te, w, 1, 0)
        return lax.dynamic_slice_in_dim(all_heads, c * cols, cols, 1).T

    time_q = time_terms(w_time_q)
    times = jnp.stack([time_q, jnp.zeros_like(time_q), time_terms(time_value_weight)])
    row_table = toeplitz_tables(lax.dynamic_slice_in_dim(rel_rows, c * own_heads, own_heads), SIDE)
    col_table = toeplitz_tables(lax.dynamic_slice_in_dim(rel_cols, c * own_heads, own_heads), SIDE)
    gap = jnp.zeros_like(row_table)
    tables = jnp.concatenate(
        [
            jnp.concatenate([row_table, gap], axis=2),
            jnp.concatenate([gap, col_table], axis=2),
        ],
        axis=1,
    ).astype(BF)
    ln1_row, ln2_row = ln1_gain.reshape(1, dm), ln2_gain.reshape(1, dm)
    grad_out = pick(out_grad, 1 - y)
    grad_own = pick(out_grad, y)

    clock = Clock(coords)
    clock.passed(feats, times, tables, core, pair, grad_out, grad_own, ln1_row, ln2_row)
    tok_rx = clock.tie(tok_rx)
    grad_rx = swap_y(lax.optimization_barrier((grad_out, tok_rx))[0])
    attn_in, qkv = project(
        core, (tok_own, tok_rx, tok_own_far, swap_core(tok_rx)), ln1_row, times, feats, w_qkv,
        scale, own_heads,
    )
    clock.passed(qkv)
    half_heads = own_heads // 2
    o_a, lse_a = attend_forward(clock.now, qkv, tables, feats, 0, half_heads)
    clock.passed(o_a, grad_rx)
    far_a = swap_core(o_a)
    o_b, lse_b = attend_forward(clock.now, qkv, tables, feats, half_heads, half_heads)
    far_b = swap_core(o_b)

    x = jnp.concatenate([tok_own, tok_rx], axis=0)
    grads_mine = jnp.concatenate([grad_own, grad_rx], axis=0)
    grad_branch = (grads_mine.astype(F32) * valid[:, :1]).astype(BF)
    o_own = jnp.concatenate([o_a, o_b], axis=0)
    lse = jnp.concatenate([lse_a, lse_b], axis=0)
    clock.passed(o_b, grad_branch, x)

    def turned(a):
        a = a.reshape(cols // 2, 2 * mine)
        return jnp.concatenate([a[:, mine:], a[:, :mine]], axis=1)

    o_flat = o_own.reshape(cols, 2 * mine)
    o_far = jnp.concatenate([turned(far_a), turned(far_b)], axis=0)
    attn_all = jnp.concatenate(
        [jnp.where(c == 0, o_flat, o_far), jnp.where(c == 0, o_far, o_flat)], axis=0
    )
    branch_one = dot(attn_all[:, :mine], output_projection_weight, 0, 0)
    hidden_one = x.astype(F32) + branch_one
    mlp_in = (moments(hidden_one)[0] * ln2_gain).astype(BF)

    tile = ff // 6
    two, slope, down, mlp_in_t = mlp_rise(mlp_in, grad_branch, w_up, w_down, tile)
    clock.passed(down)
    img_names = list(range(bits))[::-1]
    twos = (2,) * bits
    low = ff // (8 * n_img)
    down = down.reshape(twos + (2, 2, 2, low, dm))
    jobs_down = [
        Halving(
            img_names + [on_core, on_y], [on_core] + dims, [down], (low, dm), suffix=(k,)
        )
        for k, dims in enumerate([order(0, on_y, 1), order(1, 0, on_y)])
    ]
    step = functools.partial(advance, clock, swaps)

    def finish(jobs):
        while jobs[0].result is None:
            step(jobs)

    step(jobs_down)

    gm, send, own = mlp_fall(
        clock.now, pair, mlp_in_t, grad_branch, w_up, w_down, slope, tile, 0, 1, ()
    )
    clock.passed(gm)
    step(jobs_down)
    gm, send, own = mlp_fall(
        clock.now, pair, mlp_in_t, grad_branch, w_up, w_down, slope, tile, 1, 2, (gm, send, own)
    )
    clock.passed(gm)
    step(jobs_down)
    far_up = swap_core(clock.tie(send))

    output, grad_one, gb_mine, sums = middle(
        clock.now, gm, two, branch_one, hidden_one, grads_mine, valid, ln2_row
    )
    clock.passed(output)
    step(jobs_down)
    gb_all = jnp.concatenate([gb_mine, swap_core(clock.tie(gb_mine))], axis=0)
    w_proj_rows = lax.dynamic_slice_in_dim(output_projection_weight, c * cols, cols, 0)
    do = dot(w_proj_rows, gb_all, 1, 1).astype(BF).reshape(own_heads, width, 2 * mine)
    gb_cols = lax.dynamic_slice_in_dim(gb_all, c * cols, cols, 1)
    proj_part = dot(attn_all, gb_cols, 1, 0).astype(BF)
    clock.passed(do, proj_part)

    def by_row(dims, arrays, columns_of, column=0, prefix=()):
        shape = twos + (2, rows // 2)
        return Halving(
            img_names + [on_y],
            dims,
            [a.reshape(a.shape[: len(prefix)] + shape + a.shape[-1:]) for a in arrays],
            (rows // 2, columns_of),
            prefix=prefix,
            column=column,
        )

    jobs_up = [
        by_row(order(on_y, 0, 1), (own, far_up), ff // 4, 0),
        by_row(order(0, 1, on_y), (own, far_up), ff // 4, 1),
        by_row(order(1, on_y, 0), (proj_part,), cols),
    ]
    step(jobs_down)
    step(jobs_up)
    first = 5 * own_heads // 8
    grads = attend_backward(
        clock.now, qkv, o_own, do, lse, tables, feats, scale, 0, first, ()
    )
    clock.passed(grads[0])
    step(jobs_down)
    step(jobs_up)
    out_far = swap_y(clock.tie(output)[span:])
    finish(jobs_down)
    down_parts, down_far = across_y([job.result for job in jobs_down])
    grads = attend_backward(
        clock.now, qkv, o_own, do, lse, tables, feats, scale, first, own_heads - first, grads
    )
    clock.passed(grads[0], out_far, down_far)
    step(jobs_up)
    d, toe, image_grads = grads
    w_part = project_weights(clock.now, attn_in, d)
    clock.passed(w_part)
    jobs_qkv = [
        by_row(dims, (w_part,), cols, prefix=(p,))
        for p, dims in enumerate([order(0, on_y, 1), order(on_y, 0, 1), order(1, 0, on_y)])
    ]
    step(jobs_qkv)
    step(jobs_up)
    image_grads = clock.tie(image_grads)
    down_part, down_far = across_core(down_parts, down_far)
    back, back_far = project_back(clock.now, core, d, w_qkv, mine)
    clock.passed(back)
    step(jobs_up)
    step(jobs_qkv)
    back_far = swap_core(clock.tie(back_far))
    d0, d1 = (
        a.reshape(2, low, 2, dm).transpose(0, 2, 1, 3).reshape(4 * low, dm)
        for a in both_cores(down_part, clock.tie(down_far))
    )
    w_down_grad = jnp.concatenate([d0, d1], axis=0)
    finish(jobs_up)
    u0, u1 = spread([job.result for job in jobs_up])
    w_up_grad = jnp.concatenate(
        [u[:, k * tile : (k + 1) * tile] for k in range(3) for u in (u0, u1)], axis=1
    )
    w_proj_grad = jnp.concatenate([u[:, ff // 2 :] for u in (u0, u1)], axis=1)
    input_grad, sums_one = last(back, back_far, x, grad_one, ln1_row)
    clock.passed(input_grad)

    part = jnp.transpose(image_grads[:, :, :4], (0, 2, 1, 3)).reshape(8, cols).astype(BF)
    far = swap_core(part)
    part = jnp.concatenate([jnp.where(c == 0, part, far), jnp.where(c == 0, far, part)], axis=1)
    part = jnp.concatenate([part, te], axis=0)[None]
    far = swap_y(part)
    part = jnp.concatenate([jnp.where(y == 0, part, far), jnp.where(y == 0, far, part)], axis=0)
    factors = gather_img(part).reshape(n_img * slots, 12, dm)
    te_rows = lax.dynamic_slice_in_dim(factors[:, 8:], me_img * rows, rows, 2)
    w_time_q_grad, w_time_v_grad = (
        lax.dot_general(
            te_rows.reshape(-1, rows),
            factors[:, 4 * k : 4 * k + 4].reshape(-1, dm),
            (((0,), (0,)), ((), ())),
            preferred_element_type=F32,
        )
        for k in range(2)
    )

    reach = jnp.arange(2 * SIDE - 1, dtype=jnp.int32)
    side = jnp.arange(SIDE, dtype=jnp.int32)
    diag = (reach == side[:, None, None] - side[None, :, None] + SIDE - 1).astype(F32)
    rel = jnp.stack([toe[:, :SIDE, :SIDE], toe[:, SIDE:, SIDE:]])
    rel = jnp.einsum("khrt,rtd->khd", rel, diag, precision=lax.Precision.HIGHEST)
    rel_all = lax.dynamic_update_slice(
        jnp.zeros((2, heads, 2 * SIDE - 1), F32), rel, (0, c * own_heads, 0)
    )
    stats = jnp.concatenate([jnp.sum(sums[1:4], axis=1), jnp.sum(valid[:, 0])[None]])
    small = jnp.concatenate([sums_one[0], sums[0], rel_all.reshape(-1), stats])
    small = sum_all(small, (swap_core, swap_y))
    ln1_gain_grad = lax.dynamic_slice_in_dim(small, me_img * rows, rows)
    ln2_gain_grad = lax.dynamic_slice_in_dim(small, dm + me_img * rows, rows)
    rel_all = small[2 * dm : -4].reshape(2, heads, 2 * SIDE - 1)
    rms_values = jnp.sqrt(small[-4:-1] / (small[-1] * dm))

    step(jobs_qkv)
    in_far = swap_y(clock.tie(input_grad)[span:])
    clock.passed(w_up_grad, w_proj_grad, w_down_grad)
    finish(jobs_qkv)

    q0, q1 = spread([job.result for job in jobs_qkv])
    w_qkv_grad = jnp.concatenate(
        [q[:, p * cols : (p + 1) * cols] for p in range(3) for q in (q0, q1)], axis=1
    )

    def returned(own_rows, far_rows):
        return jnp.stack(
            [jnp.where(y == 0, own_rows, far_rows), jnp.where(y == 0, far_rows, own_rows)]
        )

    return (
        returned(output[:span], out_far),
        returned(input_grad[:span], in_far),
        ln1_gain_grad,
        w_qkv_grad,
        w_time_q_grad,
        w_time_v_grad,
        rel_all[0],
        rel_all[1],
        w_proj_grad,
        ln2_gain_grad,
        w_up_grad,
        w_down_grad,
        rms_values,
    )


def solution(mesh):
    return jax.shard_map(
        per_device,
        mesh=mesh,
        in_specs=(
            P("img", "seq", None),
            P("img", None, None),
            P("img", None),
            P("img", None),
        )
        + (P(),) * 10
        + (P("img", "seq", None),),
        out_specs=(
            P("img", "seq", None),
            P("img", "seq", None),
            P("img"),
            P("img", None),
            P("img", None),
            P("img", None),
            P(),
            P(),
            P("img", None),
            P("img"),
            P("img", None),
            P("img", None),
            P(),
        ),
        check_vma=False,
    )
```

```python
import functools
import math

import jax
import jax.numpy as jnp
from jax import lax
from jax.experimental import pallas as pl
from jax.experimental.pallas import tpu as pltpu
from jax.sharding import PartitionSpec as P

SIDE = 32
EPS = 1e-06
FAR = -1e30
LANES = 128
BF = jnp.bfloat16
F32 = jnp.float32
VMEM_LIMIT = 56 * 2**20
QUERY_BLOCK = 512
FF_STEP = 512

RC = 2 * SIDE
KEY_MASK = RC
QUERY_MASK = KEY_MASK + 16
IMAGE_HOT = QUERY_MASK + 16
FEATURES = IMAGE_HOT + 16
ANYWHERE = pl.BlockSpec(memory_space=pl.ANY)


def dot(a, b, ca, cb):
    return lax.dot_general(a, b, (((ca,), (cb,)), ((), ())), preferred_element_type=F32)


def params(*semantics):
    return pltpu.CompilerParams(dimension_semantics=semantics, vmem_limit_bytes=VMEM_LIMIT)


CHEAP = pl.CostEstimate(flops=10**6, bytes_accessed=10**5, transcendentals=0)


def features_kernel(len_ref, turn_ref, base_ref, feat_ref, valid_ref, *, span):
    tokens = feat_ref.shape[1]

    def describe(shape, axis):
        index = lax.broadcasted_iota(jnp.int32, shape, axis)
        block = index // span
        pos = index - block * span
        for k in range(tokens // span):
            pos = pos + jnp.where(block == k, base_ref[k], 0)
        ends = []
        total = 0
        for j in range(4):
            total = total + len_ref[j]
            ends.append(total)
        segment = sum((pos >= ends[j]).astype(jnp.int32) for j in range(4))
        return pos, ends, segment

    pos, ends, segment = describe((1, tokens), 1)
    picked = jnp.minimum(segment, 3)
    begin = jnp.zeros_like(pos)
    length = jnp.zeros_like(pos)
    turn = jnp.zeros_like(pos)
    for j in range(4):
        here = picked == j
        begin = jnp.where(here, ends[j] - len_ref[j], begin)
        length = jnp.where(here, len_ref[j], length)
        turn = jnp.where(here, turn_ref[j], turn)
    full = length == SIDE * SIDE
    side = jnp.where(full, SIDE, SIDE // 2)
    u = pos - begin
    bits = SIDE.bit_length() - 1
    r0 = jnp.where(full, u >> bits, u >> (bits - 1))
    c0 = u & (side - 1)
    r1 = jnp.where((turn & 1) == 1, side - 1 - r0, r0)
    c1 = jnp.where(((turn >> 1) & 1) == 1, side - 1 - c0, c0)
    valid = pos < ends[3]
    row = jnp.where(valid, jnp.where(turn >= 4, c1, r1), 0)
    col = jnp.where(valid, jnp.where(turn >= 4, r1, c1), 0)
    which = lax.broadcasted_iota(jnp.int32, (SIDE, tokens), 0)
    few = lax.broadcasted_iota(jnp.int32, (16, tokens), 0)

    def put(start, value):
        feat_ref[start : start + value.shape[0], :] = value.astype(BF)

    put(0, jnp.where(which == row, 1.0, 0.0))
    put(SIDE, jnp.where(which == col, 1.0, 0.0))
    put(KEY_MASK, jnp.where(few == segment, 1.0, 0.0))
    put(QUERY_MASK, jnp.where((few < 5) & (few != segment), FAR, 0.0))
    put(IMAGE_HOT, jnp.where(few == picked, 1.0, 0.0))
    down_pos, down_ends, unused = describe(valid_ref.shape, 0)
    valid_ref[...] = jnp.where(down_pos < down_ends[3], 1.0, 0.0)


def token_features(lengths, turns, bases, span, mine):
    tokens = bases.shape[0] * span
    smem = pl.BlockSpec(memory_space=pltpu.SMEM)
    return pl.pallas_call(
        functools.partial(features_kernel, span=span),
        out_shape=(
            jax.ShapeDtypeStruct((FEATURES, tokens), BF),
            jax.ShapeDtypeStruct((mine, LANES), F32),
        ),
        in_specs=[smem, smem, smem],
        cost_estimate=CHEAP,
        name="token_features",
    )(lengths, turns, bases)


def window(cols):
    return -(-(cols + LANES // 2) // LANES) * LANES


def fetch(part, core, w_ref, room, sems, cols, dm):
    start = part * dm + (core * cols) // LANES * LANES
    start = pl.multiple_of(start, LANES)
    return pltpu.make_async_copy(
        w_ref.at[:, pl.ds(start, room.shape[2])], room.at[part], sems.at[part]
    )


def project_kernel(
    core_ref, a_ref, b_ref, c_ref, d_ref, gain_ref, time_ref, feat_ref, w_ref,
    in_ref, x_ref, qkv_ref, room, wide, sems, *, scale, cols,
):
    part = pl.program_id(0)
    core = core_ref[0]
    dm = in_ref.shape[1]
    width = qkv_ref.shape[2]

    @pl.when(part == 0)
    def _():
        for k in range(3):
            fetch(k, core, w_ref, room, sems, cols, dm).start()
        rows = a_ref.shape[0]
        x_ref[:rows, :] = a_ref[...]
        x_ref[rows:, :] = b_ref[...]
        for k, ref in enumerate((a_ref, b_ref, c_ref, d_ref)):
            x = ref[...].astype(F32)
            centre = x - jnp.mean(x, axis=-1, keepdims=True)
            spread = jnp.mean(centre * centre, axis=-1, keepdims=True)
            normed = centre * lax.rsqrt(spread + EPS) * gain_ref[...]
            in_ref[k * rows : (k + 1) * rows, :] = normed.astype(BF)

    fetch(part, core, w_ref, room, sems, cols, dm).wait()
    wide[...] = dot(room[part], in_ref[...], 0, 1)
    shift = core * cols - (core * cols) // LANES * LANES
    factor = jnp.where(part == 0, scale, 1.0)
    hot = feat_ref[IMAGE_HOT:, :].astype(F32)
    for h in range(cols // width):
        at = pl.multiple_of(shift + h * width, 8)
        x = wide[pl.ds(at, width), :]
        t = time_ref[0, h * width : (h + 1) * width, :]
        for j in range(4):
            x = x + t[:, j : j + 1] * hot[j : j + 1]
        qkv_ref[0, h] = (x * factor).astype(BF)


def project(core, blocks, gain, times, feats, w_qkv, scale, heads):
    rows, dm = blocks[0].shape
    tokens = 4 * rows
    cols = times.shape[1]
    width = cols // heads
    whole = lambda p, t: (0, 0)
    room = window(cols)
    return pl.pallas_call(
        functools.partial(project_kernel, scale=scale, cols=cols),
        grid_spec=pltpu.PrefetchScalarGridSpec(
            num_scalar_prefetch=1,
            grid=(3,),
            in_specs=[pl.BlockSpec((rows, dm), whole)] * 4
            + [
                pl.BlockSpec((1, dm), whole),
                pl.BlockSpec((1, cols, 4), lambda p, t: (p, 0, 0)),
                pl.BlockSpec(feats.shape, whole),
                ANYWHERE,
            ],
            out_specs=[
                pl.BlockSpec((tokens, dm), whole),
                pl.BlockSpec((2 * rows, dm), whole),
                pl.BlockSpec((1, heads, width, tokens), lambda p, t: (p, 0, 0, 0)),
            ],
            scratch_shapes=[
                pltpu.VMEM((3, dm, room), BF),
                pltpu.VMEM((room, tokens), F32),
                pltpu.SemaphoreType.DMA((3,)),
            ],
        ),
        out_shape=[
            jax.ShapeDtypeStruct((tokens, dm), BF),
            jax.ShapeDtypeStruct((2 * rows, dm), BF),
            jax.ShapeDtypeStruct((3, heads, width, tokens), BF),
        ],
        compiler_params=params("arbitrary"),
        cost_estimate=CHEAP,
        name="project",
    )(core, *blocks, gain, times, feats, w_qkv)


def weights_kernel(clock_ref, in_ref, d_ref, out_ref):
    d = jnp.concatenate([d_ref[0, h].astype(F32) for h in range(d_ref.shape[1])], axis=0)
    out_ref[0] = dot(in_ref[...], d.astype(BF), 0, 1).astype(BF)


def project_weights(clock, attn_in, d):
    parts, heads, width, tokens = d.shape
    dm = attn_in.shape[1]
    return pl.pallas_call(
        weights_kernel,
        grid_spec=pltpu.PrefetchScalarGridSpec(
            num_scalar_prefetch=1,
            grid=(parts,),
            in_specs=[
                pl.BlockSpec((tokens, dm), lambda p, t: (0, 0)),
                pl.BlockSpec((1, heads, width, tokens), lambda p, t: (p, 0, 0, 0)),
            ],
            out_specs=pl.BlockSpec((1, dm, heads * width), lambda p, t: (p, 0, 0)),
        ),
        out_shape=jax.ShapeDtypeStruct((parts, dm, heads * width), BF),
        compiler_params=params("arbitrary"),
        cost_estimate=CHEAP,
        name="project_weights",
    )(clock, attn_in, d)


def project_back_kernel(
    clock_ref, core_ref, d_ref, w_ref, mine_ref, far_ref, room, wide, total, sems, *, cols
):
    part = pl.program_id(0)
    core = core_ref[0]
    dm = w_ref.shape[0]
    width = d_ref.shape[2]

    @pl.when(part == 0)
    def _():
        for k in range(3):
            fetch(k, core, w_ref, room, sems, cols, dm).start()
        wide[...] = jnp.zeros_like(wide)

    shift = core * cols - (core * cols) // LANES * LANES
    for h in range(cols // width):
        at = pl.multiple_of(shift + h * width, 8)
        wide[pl.ds(at, width), :] = d_ref[0, h].astype(F32)
    fetch(part, core, w_ref, room, sems, cols, dm).wait()
    term = dot(wide[...].astype(BF), room[part], 0, 1)

    @pl.when(part == 0)
    def _():
        total[...] = term

    @pl.when(part == 1)
    def _():
        total[...] += term

    @pl.when(part == 2)
    def _():
        rows = mine_ref.shape[0]
        mine_ref[...] = total[:rows, :] + term[:rows]
        far_ref[...] = (total[rows:, :] + term[rows:]).astype(BF)


def project_back(clock, core, d, w_qkv, mine):
    parts, heads, width, tokens = d.shape
    dm = w_qkv.shape[0]
    cols = heads * width
    room = window(cols)
    whole = lambda p, t, u: (0, 0)
    return pl.pallas_call(
        functools.partial(project_back_kernel, cols=cols),
        grid_spec=pltpu.PrefetchScalarGridSpec(
            num_scalar_prefetch=2,
            grid=(parts,),
            in_specs=[
                pl.BlockSpec((1, heads, width, tokens), lambda p, t, u: (p, 0, 0, 0)),
                ANYWHERE,
            ],
            out_specs=[pl.BlockSpec((mine, dm), whole), pl.BlockSpec((tokens - mine, dm), whole)],
            scratch_shapes=[
                pltpu.VMEM((3, dm, room), BF),
                pltpu.VMEM((room, tokens), F32),
                pltpu.VMEM((tokens, dm), F32),
                pltpu.SemaphoreType.DMA((3,)),
            ],
        ),
        out_shape=[
            jax.ShapeDtypeStruct((mine, dm), F32),
            jax.ShapeDtypeStruct((tokens - mine, dm), BF),
        ],
        compiler_params=params("arbitrary"),
        cost_estimate=CHEAP,
        name="project_back",
    )(clock, core, d, w_qkv)


def query_block(b, bias, feat_ref, q):
    at = slice(b * QUERY_BLOCK, (b + 1) * QUERY_BLOCK)
    return jnp.concatenate([bias[:, at], feat_ref[QUERY_MASK:IMAGE_HOT, at], q[:, at]], axis=0)


def forward_kernel(clock_ref, p_ref, table_ref, feat_ref, o_ref, lse_ref):
    blocks = p_ref.shape[3] // QUERY_BLOCK
    q, k, v = (p_ref[p, 0] for p in range(3))
    bias = jnp.dot(table_ref[0], feat_ref[:RC], preferred_element_type=F32).astype(BF)
    key = jnp.concatenate([feat_ref[:QUERY_MASK], k], axis=0).T

    def scores(b):
        return jnp.dot(key, query_block(b, bias, feat_ref, q), preferred_element_type=F32)

    ahead = scores(0)
    for b in range(blocks):
        at = slice(b * QUERY_BLOCK, (b + 1) * QUERY_BLOCK)
        s = ahead
        top = jnp.max(s, axis=0, keepdims=True)
        if b + 1 < blocks:
            ahead = scores(b + 1)
        e = jnp.exp(s - top)
        total = jnp.sum(e, axis=0, keepdims=True)
        o = jnp.dot(v, e.astype(BF), preferred_element_type=F32) / total
        o_ref[0, :, at] = o.astype(BF)
        lse_ref[0, :, at] = top + jnp.log(total)


def attend_forward(clock, qkv, tables, feats, first, count):
    parts, heads, width, tokens = qkv.shape
    return pl.pallas_call(
        forward_kernel,
        grid_spec=pltpu.PrefetchScalarGridSpec(
            num_scalar_prefetch=1,
            grid=(count,),
            in_specs=[
                pl.BlockSpec((parts, 1, width, tokens), lambda h, t: (0, first + h, 0, 0)),
                pl.BlockSpec((1, RC, RC), lambda h, t: (first + h, 0, 0)),
                pl.BlockSpec(feats.shape, lambda h, t: (0, 0)),
            ],
            out_specs=[
                pl.BlockSpec((1, width, tokens), lambda h, t: (h, 0, 0)),
                pl.BlockSpec((1, 1, tokens), lambda h, t: (h, 0, 0)),
            ],
        ),
        out_shape=[
            jax.ShapeDtypeStruct((count, width, tokens), BF),
            jax.ShapeDtypeStruct((count, 1, tokens), F32),
        ],
        compiler_params=params("arbitrary"),
        cost_estimate=CHEAP,
        name="attention_forward",
    )(clock, qkv, tables, feats)


def backward_kernel(clock_ref, qkv_ref, o_ref, do_ref, lse_ref, table_ref, feat_ref, *rest, scale):
    d_ref, toe_ref, image_ref = rest[-3:]
    width = o_ref.shape[1]
    tokens = o_ref.shape[2]
    q, k, v = (qkv_ref[p, 0] for p in range(3))
    do = do_ref[0]
    delta = jnp.sum(do.astype(F32) * o_ref[0].astype(F32), axis=0, keepdims=True)
    rc = feat_ref[:RC]
    bias = jnp.dot(table_ref[0], rc, preferred_element_type=F32).astype(BF)
    key_t = jnp.concatenate([feat_ref[:QUERY_MASK], k], axis=0)
    key = key_t.T
    value = v.T
    dk = jnp.zeros((tokens, width), F32)
    dv = jnp.zeros((tokens, width), F32)
    dq_parts, bias_parts = [], []

    def first(b):
        at = slice(b * QUERY_BLOCK, (b + 1) * QUERY_BLOCK)
        s = jnp.dot(key, query_block(b, bias, feat_ref, q), preferred_element_type=F32)
        return s, jnp.dot(value, do[:, at], preferred_element_type=F32)

    ahead = first(0)
    for b in range(tokens // QUERY_BLOCK):
        at = slice(b * QUERY_BLOCK, (b + 1) * QUERY_BLOCK)
        s, dp = ahead
        p = jnp.exp(s - lse_ref[0, :, at])
        ds = (p * (dp - delta[:, at])).astype(BF)
        p = p.astype(BF)
        if (b + 1) * QUERY_BLOCK < tokens:
            ahead = first(b + 1)
        dq = jnp.dot(key_t, ds, preferred_element_type=F32)
        dq_parts.append((dq[QUERY_MASK:] * scale).astype(BF))
        bias_parts.append(dq[:RC].astype(BF))
        dk = dk + dot(ds, q[:, at], 1, 1)
        dv = dv + dot(p, do[:, at], 1, 1)
    toe = dot(rc, jnp.concatenate(bias_parts, axis=1), 1, 1)
    dq = jnp.concatenate(dq_parts, axis=1)
    dk = dk.T.astype(BF)
    dv = dv.T.astype(BF)
    d_ref[0, 0] = dq
    d_ref[1, 0] = dk
    d_ref[2, 0] = dv
    toe_ref[0] = toe
    hot = feat_ref[IMAGE_HOT:]
    image_ref[0, 0] = dot(hot, dq, 1, 1)
    image_ref[1, 0] = dot(hot, dv, 1, 1)


def attend_backward(clock, qkv, o, do, lse, tables, feats, scale, first, count, before):
    parts, heads, width, tokens = qkv.shape
    head3 = lambda h, t: (first + h, 0, 0)
    head4 = lambda h, t: (0, first + h, 0, 0)
    return pl.pallas_call(
        functools.partial(backward_kernel, scale=scale),
        grid_spec=pltpu.PrefetchScalarGridSpec(
            num_scalar_prefetch=1,
            grid=(count,),
            in_specs=[
                pl.BlockSpec((parts, 1, width, tokens), head4),
                pl.BlockSpec((1, width, tokens), head3),
                pl.BlockSpec((1, width, tokens), head3),
                pl.BlockSpec((1, 1, tokens), head3),
                pl.BlockSpec((1, RC, RC), head3),
                pl.BlockSpec(feats.shape, lambda h, t: (0, 0)),
            ]
            + [ANYWHERE] * len(before),
            out_specs=[
                pl.BlockSpec((parts, 1, width, tokens), head4),
                pl.BlockSpec((1, RC, RC), head3),
                pl.BlockSpec((2, 1, 16, width), head4),
            ],
        ),
        out_shape=[
            jax.ShapeDtypeStruct((parts, heads, width, tokens), BF),
            jax.ShapeDtypeStruct((heads, RC, RC), F32),
            jax.ShapeDtypeStruct((2, heads, 16, width), F32),
        ],
        input_output_aliases={7 + k: k for k in range(len(before))},
        compiler_params=params("arbitrary"),
        cost_estimate=CHEAP,
        name="attention_backward",
    )(clock, qkv, o, do, lse, tables, feats, *before)


def rise_kernel(
    m_ref, near_ref, far_ref, valid_ref, up_ref, down_ref,
    two_ref, slope_ref, wd_ref, mt_ref, g_ref,
):
    @pl.when(pl.program_id(0) == 0)
    def _():
        two_ref[...] = jnp.zeros_like(two_ref)
        mt_ref[...] = m_ref[...].T
        half = near_ref.shape[0]
        g_ref[:half, :] = (near_ref[...].astype(F32) * valid_ref[:half, :1]).astype(BF)
        g_ref[half:, :] = (far_ref[...].astype(F32) * valid_ref[half:, :1]).astype(BF)

    def up_of(j):
        return jnp.dot(m_ref[...], up_ref[:, j : j + FF_STEP], preferred_element_type=F32)

    acts = []
    tile = up_ref.shape[1]
    ahead = up_of(0)
    for j in range(0, tile, FF_STEP):
        at = slice(j, j + FF_STEP)
        up = ahead
        if j + FF_STEP < tile:
            ahead = up_of(j + FF_STEP)
        half = 0.5 + 0.5 * lax.erf(up * math.sqrt(0.5))
        slope = half + up * (jnp.exp(-0.5 * up * up) * (1.0 / math.sqrt(2.0 * math.pi)))
        slope_ref[:, at] = slope.astype(BF)
        acts.append((up * half).astype(BF))
    act = jnp.concatenate(acts, axis=1)
    wd_ref[...] = dot(act, g_ref[...], 0, 0).astype(BF)
    two_ref[...] += jnp.dot(act, down_ref[...], preferred_element_type=F32)


def mlp_rise(m, near, far, valid, w_up, w_down, tile):
    rows, dm = m.shape
    ff = w_up.shape[1]
    whole = lambda i: (0, 0)
    return pl.pallas_call(
        rise_kernel,
        grid=(ff // tile,),
        in_specs=[
            pl.BlockSpec((rows, dm), whole),
            pl.BlockSpec(near.shape, whole),
            pl.BlockSpec(far.shape, whole),
            pl.BlockSpec(valid.shape, whole),
            pl.BlockSpec((dm, tile), lambda i: (0, i)),
            pl.BlockSpec((tile, dm), lambda i: (i, 0)),
        ],
        out_specs=[
            pl.BlockSpec((rows, dm), whole),
            pl.BlockSpec((rows, tile), lambda i: (0, i)),
            pl.BlockSpec((tile, dm), lambda i: (i, 0)),
            pl.BlockSpec((dm, rows), whole),
            pl.BlockSpec((rows, dm), whole),
        ],
        out_shape=[
            jax.ShapeDtypeStruct((rows, dm), F32),
            jax.ShapeDtypeStruct((rows, ff), BF),
            jax.ShapeDtypeStruct((ff, dm), BF),
            jax.ShapeDtypeStruct((dm, rows), BF),
            jax.ShapeDtypeStruct((rows, dm), BF),
        ],
        compiler_params=params("arbitrary"),
        cost_estimate=CHEAP,
        name="feed_forward_rise",
    )(m, near, far, valid, w_up, w_down)


def fall_kernel(clock_ref, tile_ref, mt_ref, g_ref, up_ref, down_ref, slope_ref, *rest):
    gm_out, send_ref, own_ref = rest[-3:]
    step = pl.program_id(0)

    @pl.when(step == 0)
    def _():
        gm_out[...] = rest[0][...] if len(rest) > 3 else jnp.zeros_like(gm_out)

    du = (dot(g_ref[...], down_ref[...], 1, 1) * slope_ref[...].astype(F32)).astype(BF)
    gm_out[...] += dot(du, up_ref[...], 1, 1)
    wu = jnp.dot(mt_ref[...], du, preferred_element_type=F32).astype(BF)

    @pl.when(step % 2 == 0)
    def _():
        send_ref[...] = wu

    @pl.when(step % 2 == 1)
    def _():
        own_ref[...] = wu


def mlp_fall(clock, tiles, mt, g, w_up, w_down, slope, tile, first, pairs, before):
    dm, rows = mt.shape
    ff = w_up.shape[1]
    whole = lambda i, u, t: (0, 0)
    column = lambda i, u, t: (0, first + i // 2)
    at = lambda i, t: 2 * (first + i // 2) + t[i % 2]
    return pl.pallas_call(
        fall_kernel,
        grid_spec=pltpu.PrefetchScalarGridSpec(
            num_scalar_prefetch=2,
            grid=(2 * pairs,),
            in_specs=[
                pl.BlockSpec((dm, rows), whole),
                pl.BlockSpec((rows, dm), whole),
                pl.BlockSpec((dm, tile), lambda i, u, t: (0, at(i, t))),
                pl.BlockSpec((tile, dm), lambda i, u, t: (at(i, t), 0)),
                pl.BlockSpec((rows, tile), lambda i, u, t: (0, at(i, t))),
            ]
            + ([pl.BlockSpec((rows, dm), whole), ANYWHERE, ANYWHERE] if before else []),
            out_specs=[
                pl.BlockSpec((rows, dm), whole),
                pl.BlockSpec((dm, tile), column),
                pl.BlockSpec((dm, tile), column),
            ],
        ),
        out_shape=[
            jax.ShapeDtypeStruct((rows, dm), F32),
            jax.ShapeDtypeStruct((dm, ff // 2), BF),
            jax.ShapeDtypeStruct((dm, ff // 2), BF),
        ],
        input_output_aliases={8: 1, 9: 2} if before else {},
        compiler_params=params("arbitrary"),
        cost_estimate=CHEAP,
        name="feed_forward_fall",
    )(clock, tiles, mt, g, w_up, w_down, slope, *before)


def moments(x):
    centre = x - jnp.mean(x, axis=-1, keepdims=True)
    root = lax.rsqrt(jnp.mean(centre * centre, axis=-1, keepdims=True) + EPS)
    return centre * root, root


def norm_backward(d, n, root):
    return root * (
        d - jnp.mean(d, axis=-1, keepdims=True) - n * jnp.mean(d * n, axis=-1, keepdims=True)
    )


def columns(x):
    return jnp.sum(x, axis=0, keepdims=True)


def middle_kernel(
    clock_ref, gm_ref, two_ref, one_ref, h_ref, g_ref, valid_ref, gain_ref,
    out_ref, grad_ref, low_ref, sums_ref,
):
    @pl.when(pl.program_id(0) == 0)
    def _():
        sums_ref[...] = jnp.zeros_like(sums_ref)

    valid = valid_ref[:, :1]
    two, one, h = two_ref[...], one_ref[...], h_ref[...]
    h2 = h + two
    out_ref[...] = (h2 * valid).astype(BF)
    n, root = moments(h)
    gm = gm_ref[...]
    grad = g_ref[...].astype(F32) + norm_backward(gm * gain_ref[...], n, root)
    grad_ref[...] = grad
    low_ref[...] = grad.astype(BF)
    sums_ref[0:1, :] += columns(gm * n)
    sums_ref[1:2, :] += columns(valid * h2 * h2)
    sums_ref[2:3, :] += columns(valid * one * one)
    sums_ref[3:4, :] += columns(valid * two * two)


def middle(clock, gm, two, one, hidden, grads, valid, gain):
    rows, dm = gm.shape
    step = rows // 4
    block = pl.BlockSpec((step, dm), lambda i, t: (i, 0))
    return pl.pallas_call(
        middle_kernel,
        grid_spec=pltpu.PrefetchScalarGridSpec(
            num_scalar_prefetch=1,
            grid=(4,),
            in_specs=[block] * 5
            + [
                pl.BlockSpec((step, LANES), lambda i, t: (i, 0)),
                pl.BlockSpec((1, dm), lambda i, t: (0, 0)),
            ],
            out_specs=[block, block, block, pl.BlockSpec((8, dm), lambda i, t: (0, 0))],
        ),
        out_shape=[
            jax.ShapeDtypeStruct((rows, dm), BF),
            jax.ShapeDtypeStruct((rows, dm), F32),
            jax.ShapeDtypeStruct((rows, dm), BF),
            jax.ShapeDtypeStruct((8, dm), F32),
        ],
        compiler_params=params("arbitrary"),
        cost_estimate=CHEAP,
        name="middle",
    )(clock, gm, two, one, hidden, grads, valid, gain)


def last_kernel(back_ref, far_ref, x_ref, grad_ref, gain_ref, out_ref, sums_ref):
    @pl.when(pl.program_id(0) == 0)
    def _():
        sums_ref[...] = jnp.zeros_like(sums_ref)

    back = back_ref[...] + far_ref[...].astype(F32)
    n, root = moments(x_ref[...].astype(F32))
    out_ref[...] = (grad_ref[...] + norm_backward(back * gain_ref[...], n, root)).astype(BF)
    sums_ref[0:1, :] += columns(back * n)


def last(back, far, x, grad, gain):
    rows, dm = back.shape
    step = rows // 4
    block = pl.BlockSpec((step, dm), lambda i: (i, 0))
    return pl.pallas_call(
        last_kernel,
        grid=(4,),
        in_specs=[block] * 4 + [pl.BlockSpec((1, dm), lambda i: (0, 0))],
        out_specs=[block, pl.BlockSpec((8, dm), lambda i: (0, 0))],
        out_shape=[jax.ShapeDtypeStruct((rows, dm), BF), jax.ShapeDtypeStruct((8, dm), F32)],
        compiler_params=params("arbitrary"),
        cost_estimate=CHEAP,
        name="last",
    )(back, far, x, grad, gain)


class Halving:
    def __init__(self, names, dims, base, piece, prefix=(), suffix=(), column=0):
        self.names, self.dims, self.base, self.piece = names, dims, base, piece
        self.prefix, self.suffix, self.column = prefix, suffix, column
        self.stage, self.arrived, self.result = 0, [], None

    def left(self, stage):
        return [d for d in self.names if d in self.dims[stage + 1 :]]

    def specs(self, gridded):
        stage = self.stage
        open_dims = self.left(stage)

        def index(names, prefix, suffix, column):
            def at(*grid):
                t = grid[-1]
                out = list(prefix)
                for d in names:
                    if d in gridded:
                        out.append(grid[gridded.index(d)])
                    elif d in open_dims:
                        out.append(0)
                    elif stage < len(self.dims) and d == self.dims[stage]:
                        out.append(1 - t[d])
                    else:
                        out.append(t[d])
                return tuple(out) + tuple(suffix) + (0, column)

            return at

        def block(names, prefix, suffix):
            sizes = [2 if d in open_dims and d not in gridded else None for d in names]
            return (None,) * len(prefix) + tuple(sizes) + (None,) * len(suffix) + self.piece

        arrays, specs = [], []
        for array in self.base:
            arrays.append(array)
            specs.append(
                pl.BlockSpec(
                    block(self.names, self.prefix, self.suffix),
                    index(self.names, self.prefix, self.suffix, self.column),
                )
            )
        for s, (array, place) in enumerate(self.arrived):
            arrays.append(array)
            names = self.left(s)
            specs.append(pl.BlockSpec(block(names, (place,), ()), index(names, (place,), (), 0)))
        rest = index(open_dims, (), (), 0)
        inner = tuple(2 if d not in gridded else None for d in open_dims) + self.piece
        return arrays, specs, inner, rest, (2,) * len(open_dims) + self.piece


def sum_kernel(coord_ref, *refs, counts, places):
    outs = refs[sum(counts) :]
    at = 0
    for (out, place), count in zip(places, counts):
        total = refs[at][...].astype(F32)
        for k in range(1, count):
            total = total + refs[at + k][...].astype(F32)
        outs[out][place] = total.astype(BF)
        at += count


def advance(clock, swaps, jobs):
    arrays, in_specs, counts, groups, places = [], [], [], [], []
    stage = jobs[0].stage
    steps = min(2, max(0, len(jobs[0].left(stage)) - 1))
    for job in jobs:
        some, their, inner, rest, shape = job.specs(job.left(stage)[:steps])
        arrays, in_specs = arrays + some, in_specs + their
        counts.append(len(some))
        sent = job.dims[stage] if stage < len(job.dims) else None
        key = (sent, shape)
        found = [k for k, g in enumerate(groups) if g[0] == key]
        if not found:
            groups.append((key, inner, rest, []))
        group = found[0] if found else len(groups) - 1
        places.append((group, len(groups[group][3])))
        groups[group][3].append(job)
    out_specs = [
        pl.BlockSpec((len(g[3]),) + g[1], lambda *grid, f=g[2]: (0,) + f(*grid)) for g in groups
    ]
    sums = pl.pallas_call(
        functools.partial(sum_kernel, counts=counts, places=places),
        grid_spec=pltpu.PrefetchScalarGridSpec(
            num_scalar_prefetch=1,
            grid=(2,) * steps if steps else (1,),
            in_specs=in_specs,
            out_specs=out_specs,
        ),
        out_shape=[jax.ShapeDtypeStruct((len(g[3]),) + g[0][1], BF) for g in groups],
        compiler_params=params(*("arbitrary",) * max(steps, 1)),
        cost_estimate=CHEAP,
        name="sum_pieces",
    )(clock.now, *arrays)
    for (key, inner, rest, members), total in zip(groups, sums):
        if key[0] is not None:
            total = swaps[key[0]](total)
        for k, job in enumerate(members):
            if key[0] is None:
                job.result = total[k]
            else:
                job.arrived.append((total, k))
                job.stage += 1
    clock.passed(*sums)


class Clock:
    def __init__(self, now):
        self.now = now

    def passed(self, *results):
        self.now = lax.optimization_barrier((self.now, *results))[0]

    def tie(self, x):
        return lax.optimization_barrier((x, self.now))[0]


class Gather:
    def __init__(self, clock, part, swaps):
        self.clock, self.part, self.swaps, self.far = clock, part, list(swaps), None

    def tick(self):
        if self.far is not None:
            bit, axis = self.put
            low, high = jnp.where(bit, self.far, self.part), jnp.where(bit, self.part, self.far)
            self.part = jnp.concatenate([low, high], axis=axis)
            self.clock.passed(self.part)
            self.far = None
        if self.swaps:
            swap, bit, axis = self.swaps.pop(0)
            self.put = (bit, axis)
            self.far = swap(self.clock.tie(self.part))

    def finish(self):
        while self.far is not None or self.swaps:
            self.tick()
        return self.part


class Total:
    def __init__(self, clock, part, swaps):
        self.clock, self.part, self.swaps, self.far = clock, part, list(swaps), None

    def tick(self):
        if self.far is not None:
            self.part = self.part + self.far
            self.clock.passed(self.part)
            self.far = None
        if self.swaps:
            self.far = self.swaps.pop(0)(self.clock.tie(self.part))

    def finish(self):
        while self.far is not None or self.swaps:
            self.tick()
        return self.part


def pick(array, index, axis=0):
    return lax.dynamic_index_in_dim(array, index, axis, keepdims=False)


def toeplitz_tables(rel, count):
    d = jnp.arange(2 * count - 1, dtype=jnp.int32)
    t = jnp.arange(count, dtype=jnp.int32)
    hot = (d[:, None, None] == t[None, None, :] - t[None, :, None] + count - 1).astype(BF)
    return jnp.einsum("hd,dtr->htr", rel.astype(BF), hot, preferred_element_type=F32)


def per_device(
    tokens, time_embed, image_lengths, grid_turns, ln1_gain, w_qkv, w_time_q, time_value_weight,
    rel_rows, rel_cols, output_projection_weight, ln2_gain, w_up, w_down, out_grad,
):
    slots, span, dm = tokens.shape
    heads = rel_rows.shape[0]
    width = dm // heads
    ff = w_up.shape[1]
    scale = width ** (-0.5)
    n_seq = lax.axis_size("seq")
    n_img = lax.axis_size("img")
    cores = n_seq // slots
    own_heads = heads // cores
    cols = own_heads * width
    me_img = lax.axis_index("img")
    me_seq = lax.axis_index("seq")
    y = me_seq // cores
    c = me_seq % cores
    mine = slots * span
    rows = dm // n_img
    over_y = [(s, (slots - 1 - s // cores) * cores + s % cores) for s in range(n_seq)]
    over_core = [(s, s // cores * cores + cores - 1 - s % cores) for s in range(n_seq)]

    def swap_y(a):
        return lax.ppermute(a, "seq", over_y)

    def swap_core(a):
        return lax.ppermute(a, "seq", over_core)

    bits = n_img.bit_length() - 1
    on_y, on_core = bits, bits + 1
    swaps = {
        k: functools.partial(
            lax.ppermute, axis_name="img", perm=[(i, i ^ (1 << k)) for i in range(n_img)]
        )
        for k in range(bits)
    }
    swaps[on_y], swaps[on_core] = swap_y, swap_core

    def across_y(parts):
        part = jnp.concatenate(parts, axis=1)
        return part, swap_y(part)

    def across_core(part, far):
        part = jnp.concatenate([jnp.where(y == 0, part, far), jnp.where(y == 0, far, part)], axis=0)
        return part, swap_core(part)

    def both_cores(part, far):
        return jnp.where(c == 0, part, far).astype(F32), jnp.where(c == 0, far, part).astype(F32)

    def order(*first):
        return list(first) + [k for k in range(bits) if k not in first]

    tok_own = pick(tokens, y)
    tok_rx = swap_y(pick(tokens, 1 - y))
    tok_own_far = swap_core(tok_own)
    block = lambda yy, cc: (yy * cores + cc) * span
    bases = jnp.stack([block(y, c), block(1 - y, c), block(y, 1 - c), block(1 - y, 1 - c)])
    feats, valid = token_features(
        pick(image_lengths, y), pick(grid_turns, y), bases.astype(jnp.int32), span, mine
    )
    coords = jnp.stack([(me_img >> k) & 1 for k in range(bits)] + [y, c]).astype(jnp.int32)
    core = c.astype(jnp.int32).reshape(1)
    pair = jnp.stack([1 - c, c]).astype(jnp.int32)
    te = pick(time_embed, y)

    def time_terms(w):
        all_heads = dot(te, w, 1, 0)
        return lax.dynamic_slice_in_dim(all_heads, c * cols, cols, 1).T

    time_q = time_terms(w_time_q)
    times = jnp.stack([time_q, jnp.zeros_like(time_q), time_terms(time_value_weight)])
    row_table = toeplitz_tables(lax.dynamic_slice_in_dim(rel_rows, c * own_heads, own_heads), SIDE)
    col_table = toeplitz_tables(lax.dynamic_slice_in_dim(rel_cols, c * own_heads, own_heads), SIDE)
    gap = jnp.zeros_like(row_table)
    tables = jnp.concatenate(
        [
            jnp.concatenate([row_table, gap], axis=2),
            jnp.concatenate([gap, col_table], axis=2),
        ],
        axis=1,
    ).astype(BF)
    ln1_row, ln2_row = ln1_gain.reshape(1, dm), ln2_gain.reshape(1, dm)
    grad_out = pick(out_grad, 1 - y)
    grad_own = pick(out_grad, y)

    img_bits = [((me_img >> k) & 1) == 1 for k in range(bits)]
    clock = Clock(coords)
    times_all = Gather(
        clock,
        lax.optimization_barrier((time_embed, feats))[0][None],
        [(swaps[k], img_bits[k], 0) for k in range(bits)],
    ).finish()
    clock.passed(feats, times, tables, core, pair, grad_out, grad_own, ln1_row, ln2_row)
    tok_rx = clock.tie(tok_rx)
    grad_rx = swap_y(lax.optimization_barrier((grad_out, tok_rx))[0])
    attn_in, x, qkv = project(
        core, (tok_own, tok_rx, tok_own_far, swap_core(tok_rx)), ln1_row, times, feats, w_qkv,
        scale, own_heads,
    )
    clock.passed(qkv)
    half_heads = own_heads // 2
    o_a, lse_a = attend_forward(clock.now, qkv, tables, feats, 0, half_heads)
    clock.passed(o_a, grad_rx)
    far_a = swap_core(o_a)
    o_b, lse_b = attend_forward(clock.now, qkv, tables, feats, half_heads, half_heads)
    far_b = swap_core(o_b)

    o_own = jnp.concatenate([o_a, o_b], axis=0)
    lse = jnp.concatenate([lse_a, lse_b], axis=0)
    clock.passed(o_b)

    def turned(a):
        a = a.reshape(cols // 2, 2 * mine)
        return jnp.concatenate([a[:, mine:], a[:, :mine]], axis=1)

    o_flat = o_own.reshape(cols, 2 * mine)
    o_far = jnp.concatenate([turned(far_a), turned(far_b)], axis=0)
    attn_all = jnp.concatenate(
        [jnp.where(c == 0, o_flat, o_far), jnp.where(c == 0, o_far, o_flat)], axis=0
    )
    branch_one = dot(attn_all[:, :mine], output_projection_weight, 0, 0)
    hidden_one = x.astype(F32) + branch_one
    mlp_in = (moments(hidden_one)[0] * ln2_gain).astype(BF)

    tile = ff // 6
    two, slope, down, mlp_in_t, grad_branch = mlp_rise(
        mlp_in, grad_own, grad_rx, valid, w_up, w_down, ff // 3
    )
    clock.passed(two)
    down = lax.psum_scatter(down, ("img", "seq"), scatter_dimension=0, tiled=True)
    img_names = list(range(bits))[::-1]
    twos = (2,) * bits
    step = functools.partial(advance, clock, swaps)

    def finish(jobs):
        while jobs[0].result is None:
            step(jobs)

    gm, send, own = mlp_fall(
        clock.now, pair, mlp_in_t, grad_branch, w_up, w_down, slope, tile, 0, 3, ()
    )
    clock.passed(gm)
    output, grad_one, gb_mine, sums = middle(
        clock.now, gm, two, branch_one, hidden_one, grad_branch, valid, ln2_row
    )
    clock.passed(output)
    far_up = swap_core(clock.tie(send))
    gb_all = jnp.concatenate([gb_mine, swap_core(gb_mine)], axis=0)
    out_far = swap_y(output[span:])
    w_proj_rows = lax.dynamic_slice_in_dim(output_projection_weight, c * cols, cols, 0)
    do = dot(w_proj_rows, gb_all, 1, 1).astype(BF).reshape(own_heads, width, 2 * mine)
    gb_cols = lax.dynamic_slice_in_dim(gb_all, c * cols, cols, 1)
    proj_part = dot(attn_all, gb_cols, 1, 0).astype(BF)
    clock.passed(do, proj_part)

    def by_row(dims, arrays, columns_of, column=0, prefix=()):
        shape = twos + (2, rows // 2)
        return Halving(
            img_names + [on_y],
            dims,
            [a.reshape(a.shape[: len(prefix)] + shape + a.shape[-1:]) for a in arrays],
            (rows // 2, columns_of),
            prefix=prefix,
            column=column,
        )

    orders = [order(0, on_y, 1), order(on_y, 1, 0), order(1, 0, on_y)]
    up_half = ff // 4
    jobs_up = [
        by_row(dims, (own, far_up), up_half, k)
        for k, dims in enumerate([order(0, on_y, 1), order(on_y, 0, 1)])
    ]
    job_proj = by_row(orders[2], (proj_part,), cols)
    step(jobs_up + [job_proj])
    grads = attend_backward(
        clock.now, qkv, o_own, do, lse, tables, feats, scale, 0, own_heads, ()
    )
    d, toe, image_grads = grads
    clock.passed(d)
    step(jobs_up)
    part = jnp.transpose(image_grads[:, :, :4], (0, 2, 1, 3)).reshape(8, cols).astype(BF)
    gather = Gather(
        clock,
        part[None, None],
        [(swap_core, c == 1, 3), (swap_y, y == 1, 1)]
        + [(swaps[k], img_bits[k], 0) for k in range(bits)],
    )
    gather.tick()
    w_part = project_weights(clock.now, attn_in, d)
    clock.passed(w_part, out_far)
    jobs_qkv = [by_row(dims, (w_part,), cols, prefix=(p,)) for p, dims in enumerate(orders)]
    step(jobs_qkv)
    jobs_qkv.append(job_proj)
    back, back_far = project_back(clock.now, core, d, w_qkv, mine)
    clock.passed(back)
    step(jobs_up)
    clock.passed(down)
    back_far = swap_core(clock.tie(back_far))
    step(jobs_qkv)
    input_grad, sums_one = last(back, back_far, x, grad_one, ln1_row)
    clock.passed(input_grad)
    reach = jnp.arange(2 * SIDE - 1, dtype=jnp.int32)
    side = jnp.arange(SIDE, dtype=jnp.int32)
    diag = (reach == side[:, None, None] - side[None, :, None] + SIDE - 1).astype(F32)
    rel = jnp.stack([toe[:, :SIDE, :SIDE], toe[:, SIDE:, SIDE:]])
    rel = jnp.einsum("khrt,rtd->khd", rel, diag, precision=lax.Precision.HIGHEST)
    rel_all = lax.dynamic_update_slice(
        jnp.zeros((2, heads, 2 * SIDE - 1), F32), rel, (0, c * own_heads, 0)
    )
    stats = jnp.concatenate([jnp.sum(sums[1:4], axis=1), jnp.sum(valid[:, 0])[None]])
    small = jnp.concatenate([sums_one[0], sums[0], rel_all.reshape(-1), stats])
    def returned(own_rows, far_rows):
        return jnp.stack(
            [jnp.where(y == 0, own_rows, far_rows), jnp.where(y == 0, far_rows, own_rows)]
        )

    small = Total(clock, small, [swap_core, swap_y] + [swaps[k] for k in range(bits)])

    step(jobs_qkv)
    gather.tick()
    output = returned(output[:span], out_far)
    clock.passed(output)
    step(jobs_up)
    small.tick()
    gather.tick()
    down = clock.tie(down)
    step(jobs_qkv)
    in_far = swap_y(clock.tie(input_grad)[span:])
    down_far = swap_y(down)
    small.tick()
    gather.tick()
    finish(jobs_up)
    up_parts, up_far = across_y([clock.tie(job.result) for job in jobs_up])
    finish(jobs_qkv)
    qkv_parts, qkv_far = across_y([job.result for job in jobs_qkv])
    down, down_far = clock.tie(down), clock.tie(down_far)
    down = jnp.where(y == 0, jnp.stack([down, down_far]), jnp.stack([down_far, down]))
    down_far = swap_core(down)
    small.tick()
    gather.tick()
    up_part, up_far = across_core(up_parts, clock.tie(up_far))
    h0, h1 = both_cores(down, down_far)
    w_down_grad = jnp.concatenate([h0[0], h1[0], h0[1], h1[1]], axis=0)
    clock.passed(w_down_grad)
    small.tick()
    gather.tick()
    qkv_part, qkv_far = across_core(qkv_parts, clock.tie(qkv_far))
    u0, u1 = both_cores(up_part, clock.tie(up_far))
    w_up_grad = jnp.concatenate(
        [u[:, k * tile : (k + 1) * tile] for k in range(3) for u in (u0, u1)], axis=1
    )
    clock.passed(w_up_grad)
    small = small.finish()
    factors = gather.finish().reshape(n_img * slots, 8, dm)
    in_far = clock.tie(in_far)

    te_rows = lax.dynamic_slice_in_dim(times_all, me_img * rows, rows, 3)
    w_time_q_grad, w_time_v_grad = (
        lax.dot_general(
            te_rows.reshape(-1, rows),
            factors[:, 4 * k : 4 * k + 4].reshape(-1, dm),
            (((0,), (0,)), ((), ())),
            preferred_element_type=F32,
        )
        for k in range(2)
    )
    ln1_gain_grad = lax.dynamic_slice_in_dim(small, me_img * rows, rows)
    ln2_gain_grad = lax.dynamic_slice_in_dim(small, dm + me_img * rows, rows)
    rel_all = small[2 * dm : -4].reshape(2, heads, 2 * SIDE - 1)
    rms_values = jnp.sqrt(small[-4:-1] / (small[-1] * dm))
    q0, q1 = both_cores(qkv_part, qkv_far)
    w_proj_grad = jnp.concatenate([q[:, 3 * cols :] for q in (q0, q1)], axis=1)
    w_qkv_grad = jnp.concatenate(
        [q[:, p * cols : (p + 1) * cols] for p in range(3) for q in (q0, q1)], axis=1
    )

    return (
        output,
        returned(input_grad[:span], in_far),
        ln1_gain_grad,
        w_qkv_grad,
        w_time_q_grad,
        w_time_v_grad,
        rel_all[0],
        rel_all[1],
        w_proj_grad,
        ln2_gain_grad,
        w_up_grad,
        w_down_grad,
        rms_values,
    )


def solution(mesh):
    return jax.shard_map(
        per_device,
        mesh=mesh,
        in_specs=(
            P("img", "seq", None),
            P("img", None, None),
            P("img", None),
            P("img", None),
        )
        + (P(),) * 10
        + (P("img", "seq", None),),
        out_specs=(
            P("img", "seq", None),
            P("img", "seq", None),
            P("img"),
            P("img", None),
            P("img", None),
            P("img", None),
            P(),
            P(),
            P("img", None),
            P("img"),
            P("img", None),
            P("img", None),
            P(),
        ),
        check_vma=False,
    )
```

```python
import functools
import math

import jax
import jax.numpy as jnp
from jax import lax
from jax.experimental import pallas as pl
from jax.experimental.pallas import tpu as pltpu
from jax.sharding import PartitionSpec as P

SIDE = 32
EPS = 1e-06
FAR = -1e30
LANES = 128
BF = jnp.bfloat16
F32 = jnp.float32
VMEM_LIMIT = 56 * 2**20
QUERY_BLOCK = 512
FF_STEP = 512

RC = 2 * SIDE
KEY_MASK = RC
QUERY_MASK = KEY_MASK + 16
IMAGE_HOT = QUERY_MASK + 16
FEATURES = IMAGE_HOT + 16
ANYWHERE = pl.BlockSpec(memory_space=pl.ANY)


def dot(a, b, ca, cb):
    return lax.dot_general(a, b, (((ca,), (cb,)), ((), ())), preferred_element_type=F32)


def params(*semantics):
    return pltpu.CompilerParams(dimension_semantics=semantics, vmem_limit_bytes=VMEM_LIMIT)


CHEAP = pl.CostEstimate(flops=10**6, bytes_accessed=10**5, transcendentals=0)


def features_kernel(len_ref, turn_ref, base_ref, feat_ref, valid_ref, *, span):
    tokens = feat_ref.shape[1]

    def describe(shape, axis):
        index = lax.broadcasted_iota(jnp.int32, shape, axis)
        block = index // span
        pos = index - block * span
        for k in range(tokens // span):
            pos = pos + jnp.where(block == k, base_ref[k], 0)
        ends = []
        total = 0
        for j in range(4):
            total = total + len_ref[j]
            ends.append(total)
        segment = sum((pos >= ends[j]).astype(jnp.int32) for j in range(4))
        return pos, ends, segment

    pos, ends, segment = describe((1, tokens), 1)
    picked = jnp.minimum(segment, 3)
    begin = jnp.zeros_like(pos)
    length = jnp.zeros_like(pos)
    turn = jnp.zeros_like(pos)
    for j in range(4):
        here = picked == j
        begin = jnp.where(here, ends[j] - len_ref[j], begin)
        length = jnp.where(here, len_ref[j], length)
        turn = jnp.where(here, turn_ref[j], turn)
    full = length == SIDE * SIDE
    side = jnp.where(full, SIDE, SIDE // 2)
    u = pos - begin
    bits = SIDE.bit_length() - 1
    r0 = jnp.where(full, u >> bits, u >> (bits - 1))
    c0 = u & (side - 1)
    r1 = jnp.where((turn & 1) == 1, side - 1 - r0, r0)
    c1 = jnp.where(((turn >> 1) & 1) == 1, side - 1 - c0, c0)
    valid = pos < ends[3]
    row = jnp.where(valid, jnp.where(turn >= 4, c1, r1), 0)
    col = jnp.where(valid, jnp.where(turn >= 4, r1, c1), 0)
    which = lax.broadcasted_iota(jnp.int32, (SIDE, tokens), 0)
    few = lax.broadcasted_iota(jnp.int32, (16, tokens), 0)

    def put(start, value):
        feat_ref[start : start + value.shape[0], :] = value.astype(BF)

    put(0, jnp.where(which == row, 1.0, 0.0))
    put(SIDE, jnp.where(which == col, 1.0, 0.0))
    put(KEY_MASK, jnp.where(few == segment, 1.0, 0.0))
    put(QUERY_MASK, jnp.where((few < 5) & (few != segment), FAR, 0.0))
    put(IMAGE_HOT, jnp.where(few == picked, 1.0, 0.0))
    down_pos, down_ends, unused = describe(valid_ref.shape, 0)
    valid_ref[...] = jnp.where(down_pos < down_ends[3], 1.0, 0.0)


def token_features(lengths, turns, bases, span, mine):
    tokens = bases.shape[0] * span
    smem = pl.BlockSpec(memory_space=pltpu.SMEM)
    return pl.pallas_call(
        functools.partial(features_kernel, span=span),
        out_shape=(
            jax.ShapeDtypeStruct((FEATURES, tokens), BF),
            jax.ShapeDtypeStruct((mine, LANES), F32),
        ),
        in_specs=[smem, smem, smem],
        cost_estimate=CHEAP,
        name="token_features",
    )(lengths, turns, bases)


def window(cols):
    return -(-(cols + LANES // 2) // LANES) * LANES


def fetch(part, core, w_ref, room, sems, cols, dm):
    start = part * dm + (core * cols) // LANES * LANES
    start = pl.multiple_of(start, LANES)
    return pltpu.make_async_copy(
        w_ref.at[:, pl.ds(start, room.shape[2])], room.at[part], sems.at[part]
    )


def project_kernel(
    core_ref, a_ref, b_ref, c_ref, d_ref, gain_ref, time_ref, feat_ref, w_ref,
    in_ref, x_ref, qkv_ref, room, wide, sems, *, scale, cols,
):
    part = pl.program_id(0)
    core = core_ref[0]
    dm = in_ref.shape[1]
    width = qkv_ref.shape[2]

    @pl.when(part == 0)
    def _():
        for k in range(3):
            fetch(k, core, w_ref, room, sems, cols, dm).start()
        rows = a_ref.shape[0]
        x_ref[:rows, :] = a_ref[...]
        x_ref[rows:, :] = b_ref[...]
        for k, ref in enumerate((a_ref, b_ref, c_ref, d_ref)):
            x = ref[...].astype(F32)
            centre = x - jnp.mean(x, axis=-1, keepdims=True)
            spread = jnp.mean(centre * centre, axis=-1, keepdims=True)
            normed = centre * lax.rsqrt(spread + EPS) * gain_ref[...]
            in_ref[k * rows : (k + 1) * rows, :] = normed.astype(BF)

    fetch(part, core, w_ref, room, sems, cols, dm).wait()
    wide[...] = dot(room[part], in_ref[...], 0, 1)
    shift = core * cols - (core * cols) // LANES * LANES
    factor = jnp.where(part == 0, scale, 1.0)
    hot = feat_ref[IMAGE_HOT:, :].astype(F32)
    for h in range(cols // width):
        at = pl.multiple_of(shift + h * width, 8)
        x = wide[pl.ds(at, width), :]
        t = time_ref[0, h * width : (h + 1) * width, :]
        for j in range(4):
            x = x + t[:, j : j + 1] * hot[j : j + 1]
        qkv_ref[0, h] = (x * factor).astype(BF)


def project(core, blocks, gain, times, feats, w_qkv, scale, heads):
    rows, dm = blocks[0].shape
    tokens = 4 * rows
    cols = times.shape[1]
    width = cols // heads
    whole = lambda p, t: (0, 0)
    room = window(cols)
    return pl.pallas_call(
        functools.partial(project_kernel, scale=scale, cols=cols),
        grid_spec=pltpu.PrefetchScalarGridSpec(
            num_scalar_prefetch=1,
            grid=(3,),
            in_specs=[pl.BlockSpec((rows, dm), whole)] * 4
            + [
                pl.BlockSpec((1, dm), whole),
                pl.BlockSpec((1, cols, 4), lambda p, t: (p, 0, 0)),
                pl.BlockSpec(feats.shape, whole),
                ANYWHERE,
            ],
            out_specs=[
                pl.BlockSpec((tokens, dm), whole),
                pl.BlockSpec((2 * rows, dm), whole),
                pl.BlockSpec((1, heads, width, tokens), lambda p, t: (p, 0, 0, 0)),
            ],
            scratch_shapes=[
                pltpu.VMEM((3, dm, room), BF),
                pltpu.VMEM((room, tokens), F32),
                pltpu.SemaphoreType.DMA((3,)),
            ],
        ),
        out_shape=[
            jax.ShapeDtypeStruct((tokens, dm), BF),
            jax.ShapeDtypeStruct((2 * rows, dm), BF),
            jax.ShapeDtypeStruct((3, heads, width, tokens), BF),
        ],
        compiler_params=params("arbitrary"),
        cost_estimate=CHEAP,
        name="project",
    )(core, *blocks, gain, times, feats, w_qkv)


def weights_kernel(clock_ref, in_ref, d_ref, out_ref):
    d = jnp.concatenate([d_ref[0, h].astype(F32) for h in range(d_ref.shape[1])], axis=0)
    out_ref[0] = dot(in_ref[...], d.astype(BF), 0, 1).astype(BF)


def project_weights(clock, attn_in, d):
    parts, heads, width, tokens = d.shape
    dm = attn_in.shape[1]
    return pl.pallas_call(
        weights_kernel,
        grid_spec=pltpu.PrefetchScalarGridSpec(
            num_scalar_prefetch=1,
            grid=(parts,),
            in_specs=[
                pl.BlockSpec((tokens, dm), lambda p, t: (0, 0)),
                pl.BlockSpec((1, heads, width, tokens), lambda p, t: (p, 0, 0, 0)),
            ],
            out_specs=pl.BlockSpec((1, dm, heads * width), lambda p, t: (p, 0, 0)),
        ),
        out_shape=jax.ShapeDtypeStruct((parts, dm, heads * width), BF),
        compiler_params=params("arbitrary"),
        cost_estimate=CHEAP,
        name="project_weights",
    )(clock, attn_in, d)


def project_back_kernel(
    clock_ref, core_ref, d_ref, w_ref, mine_ref, far_ref, room, wide, total, sems, *, cols
):
    part = pl.program_id(0)
    core = core_ref[0]
    dm = w_ref.shape[0]
    width = d_ref.shape[2]

    @pl.when(part == 0)
    def _():
        for k in range(3):
            fetch(k, core, w_ref, room, sems, cols, dm).start()
        wide[...] = jnp.zeros_like(wide)

    shift = core * cols - (core * cols) // LANES * LANES
    for h in range(cols // width):
        at = pl.multiple_of(shift + h * width, 8)
        wide[pl.ds(at, width), :] = d_ref[0, h].astype(F32)
    fetch(part, core, w_ref, room, sems, cols, dm).wait()
    term = dot(wide[...].astype(BF), room[part], 0, 1)

    @pl.when(part == 0)
    def _():
        total[...] = term

    @pl.when(part == 1)
    def _():
        total[...] += term

    @pl.when(part == 2)
    def _():
        rows = mine_ref.shape[0]
        mine_ref[...] = total[:rows, :] + term[:rows]
        far_ref[...] = (total[rows:, :] + term[rows:]).astype(BF)


def project_back(clock, core, d, w_qkv, mine):
    parts, heads, width, tokens = d.shape
    dm = w_qkv.shape[0]
    cols = heads * width
    room = window(cols)
    whole = lambda p, t, u: (0, 0)
    return pl.pallas_call(
        functools.partial(project_back_kernel, cols=cols),
        grid_spec=pltpu.PrefetchScalarGridSpec(
            num_scalar_prefetch=2,
            grid=(parts,),
            in_specs=[
                pl.BlockSpec((1, heads, width, tokens), lambda p, t, u: (p, 0, 0, 0)),
                ANYWHERE,
            ],
            out_specs=[pl.BlockSpec((mine, dm), whole), pl.BlockSpec((tokens - mine, dm), whole)],
            scratch_shapes=[
                pltpu.VMEM((3, dm, room), BF),
                pltpu.VMEM((room, tokens), F32),
                pltpu.VMEM((tokens, dm), F32),
                pltpu.SemaphoreType.DMA((3,)),
            ],
        ),
        out_shape=[
            jax.ShapeDtypeStruct((mine, dm), F32),
            jax.ShapeDtypeStruct((tokens - mine, dm), BF),
        ],
        compiler_params=params("arbitrary"),
        cost_estimate=CHEAP,
        name="project_back",
    )(clock, core, d, w_qkv)


def query_block(b, bias, feat_ref, q):
    at = slice(b * QUERY_BLOCK, (b + 1) * QUERY_BLOCK)
    return jnp.concatenate([bias[:, at], feat_ref[QUERY_MASK:IMAGE_HOT, at], q[:, at]], axis=0)


def forward_kernel(clock_ref, p_ref, table_ref, feat_ref, o_ref, lse_ref):
    blocks = p_ref.shape[3] // QUERY_BLOCK
    q, k, v = (p_ref[p, 0] for p in range(3))
    bias = jnp.dot(table_ref[0], feat_ref[:RC], preferred_element_type=F32).astype(BF)
    key = jnp.concatenate([feat_ref[:QUERY_MASK], k], axis=0).T

    def scores(b):
        return jnp.dot(key, query_block(b, bias, feat_ref, q), preferred_element_type=F32)

    ahead = scores(0)
    for b in range(blocks):
        at = slice(b * QUERY_BLOCK, (b + 1) * QUERY_BLOCK)
        s = ahead
        top = jnp.max(s, axis=0, keepdims=True)
        if b + 1 < blocks:
            ahead = scores(b + 1)
        e = jnp.exp(s - top)
        total = jnp.sum(e, axis=0, keepdims=True)
        o = jnp.dot(v, e.astype(BF), preferred_element_type=F32) / total
        o_ref[0, :, at] = o.astype(BF)
        lse_ref[0, :, at] = top + jnp.log(total)


def attend_forward(clock, qkv, tables, feats, first, count):
    parts, heads, width, tokens = qkv.shape
    return pl.pallas_call(
        forward_kernel,
        grid_spec=pltpu.PrefetchScalarGridSpec(
            num_scalar_prefetch=1,
            grid=(count,),
            in_specs=[
                pl.BlockSpec((parts, 1, width, tokens), lambda h, t: (0, first + h, 0, 0)),
                pl.BlockSpec((1, RC, RC), lambda h, t: (first + h, 0, 0)),
                pl.BlockSpec(feats.shape, lambda h, t: (0, 0)),
            ],
            out_specs=[
                pl.BlockSpec((1, width, tokens), lambda h, t: (h, 0, 0)),
                pl.BlockSpec((1, 1, tokens), lambda h, t: (h, 0, 0)),
            ],
        ),
        out_shape=[
            jax.ShapeDtypeStruct((count, width, tokens), BF),
            jax.ShapeDtypeStruct((count, 1, tokens), F32),
        ],
        compiler_params=params("arbitrary"),
        cost_estimate=CHEAP,
        name="attention_forward",
    )(clock, qkv, tables, feats)


def backward_kernel(clock_ref, qkv_ref, o_ref, do_ref, lse_ref, table_ref, feat_ref, *rest, scale):
    d_ref, toe_ref, image_ref = rest[-3:]
    width = o_ref.shape[1]
    tokens = o_ref.shape[2]
    q, k, v = (qkv_ref[p, 0] for p in range(3))
    do = do_ref[0]
    delta = jnp.sum(do.astype(F32) * o_ref[0].astype(F32), axis=0, keepdims=True)
    rc = feat_ref[:RC]
    bias = jnp.dot(table_ref[0], rc, preferred_element_type=F32).astype(BF)
    key_t = jnp.concatenate([feat_ref[:QUERY_MASK], k], axis=0)
    key = key_t.T
    value = v.T
    dk = jnp.zeros((tokens, width), F32)
    dv = jnp.zeros((tokens, width), F32)
    dq_parts, bias_parts = [], []

    def first(b):
        at = slice(b * QUERY_BLOCK, (b + 1) * QUERY_BLOCK)
        s = jnp.dot(key, query_block(b, bias, feat_ref, q), preferred_element_type=F32)
        return s, jnp.dot(value, do[:, at], preferred_element_type=F32)

    ahead = first(0)
    for b in range(tokens // QUERY_BLOCK):
        at = slice(b * QUERY_BLOCK, (b + 1) * QUERY_BLOCK)
        s, dp = ahead
        p = jnp.exp(s - lse_ref[0, :, at])
        ds = (p * (dp - delta[:, at])).astype(BF)
        p = p.astype(BF)
        if (b + 1) * QUERY_BLOCK < tokens:
            ahead = first(b + 1)
        dq = jnp.dot(key_t, ds, preferred_element_type=F32)
        dq_parts.append((dq[QUERY_MASK:] * scale).astype(BF))
        bias_parts.append(dq[:RC].astype(BF))
        dk = dk + dot(ds, q[:, at], 1, 1)
        dv = dv + dot(p, do[:, at], 1, 1)
    toe = dot(rc, jnp.concatenate(bias_parts, axis=1), 1, 1)
    dq = jnp.concatenate(dq_parts, axis=1)
    dk = dk.T.astype(BF)
    dv = dv.T.astype(BF)
    d_ref[0, 0] = dq
    d_ref[1, 0] = dk
    d_ref[2, 0] = dv
    toe_ref[0] = toe
    hot = feat_ref[IMAGE_HOT:]
    image_ref[0, 0] = dot(hot, dq, 1, 1)
    image_ref[1, 0] = dot(hot, dv, 1, 1)


def attend_backward(clock, qkv, o, do, lse, tables, feats, scale, first, count, before):
    parts, heads, width, tokens = qkv.shape
    head3 = lambda h, t: (first + h, 0, 0)
    head4 = lambda h, t: (0, first + h, 0, 0)
    return pl.pallas_call(
        functools.partial(backward_kernel, scale=scale),
        grid_spec=pltpu.PrefetchScalarGridSpec(
            num_scalar_prefetch=1,
            grid=(count,),
            in_specs=[
                pl.BlockSpec((parts, 1, width, tokens), head4),
                pl.BlockSpec((1, width, tokens), head3),
                pl.BlockSpec((1, width, tokens), head3),
                pl.BlockSpec((1, 1, tokens), head3),
                pl.BlockSpec((1, RC, RC), head3),
                pl.BlockSpec(feats.shape, lambda h, t: (0, 0)),
            ]
            + [ANYWHERE] * len(before),
            out_specs=[
                pl.BlockSpec((parts, 1, width, tokens), head4),
                pl.BlockSpec((1, RC, RC), head3),
                pl.BlockSpec((2, 1, 16, width), head4),
            ],
        ),
        out_shape=[
            jax.ShapeDtypeStruct((parts, heads, width, tokens), BF),
            jax.ShapeDtypeStruct((heads, RC, RC), F32),
            jax.ShapeDtypeStruct((2, heads, 16, width), F32),
        ],
        input_output_aliases={7 + k: k for k in range(len(before))},
        compiler_params=params("arbitrary"),
        cost_estimate=CHEAP,
        name="attention_backward",
    )(clock, qkv, o, do, lse, tables, feats, *before)


def rise_kernel(
    m_ref, near_ref, far_ref, valid_ref, up_ref, down_ref,
    two_ref, slope_ref, wd_ref, mt_ref, g_ref,
):
    @pl.when(pl.program_id(0) == 0)
    def _():
        two_ref[...] = jnp.zeros_like(two_ref)
        mt_ref[...] = m_ref[...].T
        half = near_ref.shape[0]
        g_ref[:half, :] = (near_ref[...].astype(F32) * valid_ref[:half, :1]).astype(BF)
        g_ref[half:, :] = (far_ref[...].astype(F32) * valid_ref[half:, :1]).astype(BF)

    def up_of(j):
        return jnp.dot(m_ref[...], up_ref[:, j : j + FF_STEP], preferred_element_type=F32)

    acts = []
    tile = up_ref.shape[1]
    ahead = up_of(0)
    for j in range(0, tile, FF_STEP):
        at = slice(j, j + FF_STEP)
        up = ahead
        if j + FF_STEP < tile:
            ahead = up_of(j + FF_STEP)
        half = 0.5 + 0.5 * lax.erf(up * math.sqrt(0.5))
        slope = half + up * (jnp.exp(-0.5 * up * up) * (1.0 / math.sqrt(2.0 * math.pi)))
        slope_ref[:, at] = slope.astype(BF)
        acts.append((up * half).astype(BF))
    act = jnp.concatenate(acts, axis=1)
    wd_ref[...] = dot(act, g_ref[...], 0, 0).astype(BF)
    two_ref[...] += jnp.dot(act, down_ref[...], preferred_element_type=F32)


def mlp_rise(m, near, far, valid, w_up, w_down, tile):
    rows, dm = m.shape
    ff = w_up.shape[1]
    whole = lambda i: (0, 0)
    return pl.pallas_call(
        rise_kernel,
        grid=(ff // tile,),
        in_specs=[
            pl.BlockSpec((rows, dm), whole),
            pl.BlockSpec(near.shape, whole),
            pl.BlockSpec(far.shape, whole),
            pl.BlockSpec(valid.shape, whole),
            pl.BlockSpec((dm, tile), lambda i: (0, i)),
            pl.BlockSpec((tile, dm), lambda i: (i, 0)),
        ],
        out_specs=[
            pl.BlockSpec((rows, dm), whole),
            pl.BlockSpec((rows, tile), lambda i: (0, i)),
            pl.BlockSpec((tile, dm), lambda i: (i, 0)),
            pl.BlockSpec((dm, rows), whole),
            pl.BlockSpec((rows, dm), whole),
        ],
        out_shape=[
            jax.ShapeDtypeStruct((rows, dm), F32),
            jax.ShapeDtypeStruct((rows, ff), BF),
            jax.ShapeDtypeStruct((ff, dm), BF),
            jax.ShapeDtypeStruct((dm, rows), BF),
            jax.ShapeDtypeStruct((rows, dm), BF),
        ],
        compiler_params=params("arbitrary"),
        cost_estimate=CHEAP,
        name="feed_forward_rise",
    )(m, near, far, valid, w_up, w_down)


def fall_kernel(clock_ref, tile_ref, mt_ref, g_ref, up_ref, down_ref, slope_ref, *rest):
    gm_out, send_ref, own_ref = rest[-3:]
    step = pl.program_id(0)

    @pl.when(step == 0)
    def _():
        gm_out[...] = rest[0][...] if len(rest) > 3 else jnp.zeros_like(gm_out)

    du = (dot(g_ref[...], down_ref[...], 1, 1) * slope_ref[...].astype(F32)).astype(BF)
    gm_out[...] += dot(du, up_ref[...], 1, 1)
    wu = jnp.dot(mt_ref[...], du, preferred_element_type=F32).astype(BF)

    @pl.when(step % 2 == 0)
    def _():
        send_ref[...] = wu

    @pl.when(step % 2 == 1)
    def _():
        own_ref[...] = wu


def mlp_fall(clock, tiles, mt, g, w_up, w_down, slope, tile, first, pairs, before):
    dm, rows = mt.shape
    ff = w_up.shape[1]
    whole = lambda i, u, t: (0, 0)
    column = lambda i, u, t: (0, first + i // 2)
    at = lambda i, t: 2 * (first + i // 2) + t[i % 2]
    return pl.pallas_call(
        fall_kernel,
        grid_spec=pltpu.PrefetchScalarGridSpec(
            num_scalar_prefetch=2,
            grid=(2 * pairs,),
            in_specs=[
                pl.BlockSpec((dm, rows), whole),
                pl.BlockSpec((rows, dm), whole),
                pl.BlockSpec((dm, tile), lambda i, u, t: (0, at(i, t))),
                pl.BlockSpec((tile, dm), lambda i, u, t: (at(i, t), 0)),
                pl.BlockSpec((rows, tile), lambda i, u, t: (0, at(i, t))),
            ]
            + ([pl.BlockSpec((rows, dm), whole), ANYWHERE, ANYWHERE] if before else []),
            out_specs=[
                pl.BlockSpec((rows, dm), whole),
                pl.BlockSpec((dm, tile), column),
                pl.BlockSpec((dm, tile), column),
            ],
        ),
        out_shape=[
            jax.ShapeDtypeStruct((rows, dm), F32),
            jax.ShapeDtypeStruct((dm, ff // 2), BF),
            jax.ShapeDtypeStruct((dm, ff // 2), BF),
        ],
        input_output_aliases={8: 1, 9: 2} if before else {},
        compiler_params=params("arbitrary"),
        cost_estimate=CHEAP,
        name="feed_forward_fall",
    )(clock, tiles, mt, g, w_up, w_down, slope, *before)


def moments(x):
    centre = x - jnp.mean(x, axis=-1, keepdims=True)
    root = lax.rsqrt(jnp.mean(centre * centre, axis=-1, keepdims=True) + EPS)
    return centre * root, root


def norm_backward(d, n, root):
    return root * (
        d - jnp.mean(d, axis=-1, keepdims=True) - n * jnp.mean(d * n, axis=-1, keepdims=True)
    )


def columns(x):
    return jnp.sum(x, axis=0, keepdims=True)


def middle_kernel(
    clock_ref, gm_ref, two_ref, one_ref, h_ref, g_ref, valid_ref, gain_ref,
    out_ref, grad_ref, low_ref, sums_ref,
):
    @pl.when(pl.program_id(0) == 0)
    def _():
        sums_ref[...] = jnp.zeros_like(sums_ref)

    valid = valid_ref[:, :1]
    two, one, h = two_ref[...], one_ref[...], h_ref[...]
    h2 = h + two
    out_ref[...] = (h2 * valid).astype(BF)
    n, root = moments(h)
    gm = gm_ref[...]
    grad = g_ref[...].astype(F32) + norm_backward(gm * gain_ref[...], n, root)
    grad_ref[...] = grad
    low_ref[...] = grad.astype(BF)
    sums_ref[0:1, :] += columns(gm * n)
    sums_ref[1:2, :] += columns(valid * h2 * h2)
    sums_ref[2:3, :] += columns(valid * one * one)
    sums_ref[3:4, :] += columns(valid * two * two)


def middle(clock, gm, two, one, hidden, grads, valid, gain):
    rows, dm = gm.shape
    step = rows // 4
    block = pl.BlockSpec((step, dm), lambda i, t: (i, 0))
    return pl.pallas_call(
        middle_kernel,
        grid_spec=pltpu.PrefetchScalarGridSpec(
            num_scalar_prefetch=1,
            grid=(4,),
            in_specs=[block] * 5
            + [
                pl.BlockSpec((step, LANES), lambda i, t: (i, 0)),
                pl.BlockSpec((1, dm), lambda i, t: (0, 0)),
            ],
            out_specs=[block, block, block, pl.BlockSpec((8, dm), lambda i, t: (0, 0))],
        ),
        out_shape=[
            jax.ShapeDtypeStruct((rows, dm), BF),
            jax.ShapeDtypeStruct((rows, dm), F32),
            jax.ShapeDtypeStruct((rows, dm), BF),
            jax.ShapeDtypeStruct((8, dm), F32),
        ],
        compiler_params=params("arbitrary"),
        cost_estimate=CHEAP,
        name="middle",
    )(clock, gm, two, one, hidden, grads, valid, gain)


def last_kernel(back_ref, far_ref, x_ref, grad_ref, gain_ref, out_ref, sums_ref):
    @pl.when(pl.program_id(0) == 0)
    def _():
        sums_ref[...] = jnp.zeros_like(sums_ref)

    back = back_ref[...] + far_ref[...].astype(F32)
    n, root = moments(x_ref[...].astype(F32))
    out_ref[...] = (grad_ref[...] + norm_backward(back * gain_ref[...], n, root)).astype(BF)
    sums_ref[0:1, :] += columns(back * n)


def last(back, far, x, grad, gain):
    rows, dm = back.shape
    step = rows // 4
    block = pl.BlockSpec((step, dm), lambda i: (i, 0))
    return pl.pallas_call(
        last_kernel,
        grid=(4,),
        in_specs=[block] * 4 + [pl.BlockSpec((1, dm), lambda i: (0, 0))],
        out_specs=[block, pl.BlockSpec((8, dm), lambda i: (0, 0))],
        out_shape=[jax.ShapeDtypeStruct((rows, dm), BF), jax.ShapeDtypeStruct((8, dm), F32)],
        compiler_params=params("arbitrary"),
        cost_estimate=CHEAP,
        name="last",
    )(back, far, x, grad, gain)


class Halving:
    def __init__(self, names, dims, base, piece, prefix=(), suffix=(), column=0):
        self.names, self.dims, self.base, self.piece = names, dims, base, piece
        self.prefix, self.suffix, self.column = prefix, suffix, column
        self.stage, self.arrived, self.result = 0, [], None

    def left(self, stage):
        return [d for d in self.names if d in self.dims[stage + 1 :]]

    def specs(self, gridded):
        stage = self.stage
        open_dims = self.left(stage)

        def index(names, prefix, suffix, column):
            def at(*grid):
                t = grid[-1]
                out = list(prefix)
                for d in names:
                    if d in gridded:
                        out.append(grid[gridded.index(d)])
                    elif d in open_dims:
                        out.append(0)
                    elif stage < len(self.dims) and d == self.dims[stage]:
                        out.append(1 - t[d])
                    else:
                        out.append(t[d])
                return tuple(out) + tuple(suffix) + (0, column)

            return at

        def block(names, prefix, suffix):
            sizes = [2 if d in open_dims and d not in gridded else None for d in names]
            return (None,) * len(prefix) + tuple(sizes) + (None,) * len(suffix) + self.piece

        arrays, specs = [], []
        for array in self.base:
            arrays.append(array)
            specs.append(
                pl.BlockSpec(
                    block(self.names, self.prefix, self.suffix),
                    index(self.names, self.prefix, self.suffix, self.column),
                )
            )
        for s, (array, place) in enumerate(self.arrived):
            arrays.append(array)
            names = self.left(s)
            specs.append(pl.BlockSpec(block(names, (place,), ()), index(names, (place,), (), 0)))
        rest = index(open_dims, (), (), 0)
        inner = tuple(2 if d not in gridded else None for d in open_dims) + self.piece
        return arrays, specs, inner, rest, (2,) * len(open_dims) + self.piece


def sum_kernel(coord_ref, *refs, counts, places):
    outs = refs[sum(counts) :]
    at = 0
    for (out, place), count in zip(places, counts):
        total = refs[at][...].astype(F32)
        for k in range(1, count):
            total = total + refs[at + k][...].astype(F32)
        outs[out][place] = total.astype(BF)
        at += count


def advance(clock, swaps, jobs):
    arrays, in_specs, counts, groups, places = [], [], [], [], []
    stage = jobs[0].stage
    steps = min(2, max(0, len(jobs[0].left(stage)) - 1))
    for job in jobs:
        some, their, inner, rest, shape = job.specs(job.left(stage)[:steps])
        arrays, in_specs = arrays + some, in_specs + their
        counts.append(len(some))
        sent = job.dims[stage] if stage < len(job.dims) else None
        key = (sent, shape)
        found = [k for k, g in enumerate(groups) if g[0] == key]
        if not found:
            groups.append((key, inner, rest, []))
        group = found[0] if found else len(groups) - 1
        places.append((group, len(groups[group][3])))
        groups[group][3].append(job)
    out_specs = [
        pl.BlockSpec((len(g[3]),) + g[1], lambda *grid, f=g[2]: (0,) + f(*grid)) for g in groups
    ]
    sums = pl.pallas_call(
        functools.partial(sum_kernel, counts=counts, places=places),
        grid_spec=pltpu.PrefetchScalarGridSpec(
            num_scalar_prefetch=1,
            grid=(2,) * steps if steps else (1,),
            in_specs=in_specs,
            out_specs=out_specs,
        ),
        out_shape=[jax.ShapeDtypeStruct((len(g[3]),) + g[0][1], BF) for g in groups],
        compiler_params=params(*("arbitrary",) * max(steps, 1)),
        cost_estimate=CHEAP,
        name="sum_pieces",
    )(clock.now, *arrays)
    for (key, inner, rest, members), total in zip(groups, sums):
        if key[0] is not None:
            total = swaps[key[0]](total)
        for k, job in enumerate(members):
            if key[0] is None:
                job.result = total[k]
            else:
                job.arrived.append((total, k))
                job.stage += 1
    clock.passed(*sums)


class Clock:
    def __init__(self, now):
        self.now = now

    def passed(self, *results):
        self.now = lax.optimization_barrier((self.now, *results))[0]

    def tie(self, x):
        return lax.optimization_barrier((x, self.now))[0]


class Gather:
    def __init__(self, clock, part, swaps):
        self.clock, self.part, self.swaps, self.far = clock, part, list(swaps), None

    def land(self):
        if self.far is not None:
            bit, axis = self.put
            low, high = jnp.where(bit, self.far, self.part), jnp.where(bit, self.part, self.far)
            self.part = jnp.concatenate([low, high], axis=axis)
            self.clock.passed(self.part)
            self.far = None

    def tick(self):
        self.land()
        if self.swaps:
            swap, bit, axis = self.swaps.pop(0)
            self.put = (bit, axis)
            self.far = swap(self.clock.tie(self.part))

    def finish(self):
        while self.far is not None or self.swaps:
            self.tick()
        return self.part


class Total:
    def __init__(self, clock, part, swaps):
        self.clock, self.part, self.swaps, self.far = clock, part, list(swaps), None

    def tick(self):
        if self.far is not None:
            self.part = self.part + self.far
            self.clock.passed(self.part)
            self.far = None
        if self.swaps:
            self.far = self.swaps.pop(0)(self.clock.tie(self.part))

    def finish(self):
        while self.far is not None or self.swaps:
            self.tick()
        return self.part


def pick(array, index, axis=0):
    return lax.dynamic_index_in_dim(array, index, axis, keepdims=False)


def toeplitz_tables(rel, count):
    d = jnp.arange(2 * count - 1, dtype=jnp.int32)
    t = jnp.arange(count, dtype=jnp.int32)
    hot = (d[:, None, None] == t[None, None, :] - t[None, :, None] + count - 1).astype(BF)
    return jnp.einsum("hd,dtr->htr", rel.astype(BF), hot, preferred_element_type=F32)


def per_device(
    tokens, time_embed, image_lengths, grid_turns, ln1_gain, w_qkv, w_time_q, time_value_weight,
    rel_rows, rel_cols, output_projection_weight, ln2_gain, w_up, w_down, out_grad,
):
    slots, span, dm = tokens.shape
    heads = rel_rows.shape[0]
    width = dm // heads
    ff = w_up.shape[1]
    scale = width ** (-0.5)
    n_seq = lax.axis_size("seq")
    n_img = lax.axis_size("img")
    cores = n_seq // slots
    own_heads = heads // cores
    cols = own_heads * width
    me_img = lax.axis_index("img")
    me_seq = lax.axis_index("seq")
    y = me_seq // cores
    c = me_seq % cores
    mine = slots * span
    rows = dm // n_img
    over_y = [(s, (slots - 1 - s // cores) * cores + s % cores) for s in range(n_seq)]
    over_core = [(s, s // cores * cores + cores - 1 - s % cores) for s in range(n_seq)]

    def swap_y(a):
        return lax.ppermute(a, "seq", over_y)

    def swap_core(a):
        return lax.ppermute(a, "seq", over_core)

    bits = n_img.bit_length() - 1
    on_y, on_core = bits, bits + 1
    swaps = {
        k: functools.partial(
            lax.ppermute, axis_name="img", perm=[(i, i ^ (1 << k)) for i in range(n_img)]
        )
        for k in range(bits)
    }
    swaps[on_y], swaps[on_core] = swap_y, swap_core

    def across_y(parts):
        part = jnp.concatenate(parts, axis=1)
        return part, swap_y(part)

    def across_core(part, far):
        part = jnp.concatenate([jnp.where(y == 0, part, far), jnp.where(y == 0, far, part)], axis=0)
        return part, swap_core(part)

    def both_cores(part, far):
        return jnp.where(c == 0, part, far).astype(F32), jnp.where(c == 0, far, part).astype(F32)

    def order(*first):
        return list(first) + [k for k in range(bits) if k not in first]

    tok_own = pick(tokens, y)
    tok_rx = swap_y(pick(tokens, 1 - y))
    tok_own_far = swap_core(tok_own)
    block = lambda yy, cc: (yy * cores + cc) * span
    bases = jnp.stack([block(y, c), block(1 - y, c), block(y, 1 - c), block(1 - y, 1 - c)])
    feats, valid = token_features(
        pick(image_lengths, y), pick(grid_turns, y), bases.astype(jnp.int32), span, mine
    )
    coords = jnp.stack([(me_img >> k) & 1 for k in range(bits)] + [y, c]).astype(jnp.int32)
    core = c.astype(jnp.int32).reshape(1)
    pair = jnp.stack([1 - c, c]).astype(jnp.int32)
    te = pick(time_embed, y)

    def time_terms(w):
        all_heads = dot(te, w, 1, 0)
        return lax.dynamic_slice_in_dim(all_heads, c * cols, cols, 1).T

    time_q = time_terms(w_time_q)
    times = jnp.stack([time_q, jnp.zeros_like(time_q), time_terms(time_value_weight)])
    row_table = toeplitz_tables(lax.dynamic_slice_in_dim(rel_rows, c * own_heads, own_heads), SIDE)
    col_table = toeplitz_tables(lax.dynamic_slice_in_dim(rel_cols, c * own_heads, own_heads), SIDE)
    gap = jnp.zeros_like(row_table)
    tables = jnp.concatenate(
        [
            jnp.concatenate([row_table, gap], axis=2),
            jnp.concatenate([gap, col_table], axis=2),
        ],
        axis=1,
    ).astype(BF)
    ln1_row, ln2_row = ln1_gain.reshape(1, dm), ln2_gain.reshape(1, dm)
    grad_out = pick(out_grad, 1 - y)
    grad_own = pick(out_grad, y)

    img_bits = [((me_img >> k) & 1) == 1 for k in range(bits)]
    clock = Clock(coords)
    clock.passed(feats, times, tables, core, pair, grad_out, grad_own, ln1_row, ln2_row)
    tok_rx = clock.tie(tok_rx)
    grad_rx = swap_y(lax.optimization_barrier((grad_out, tok_rx))[0])
    attn_in, x, qkv = project(
        core, (tok_own, tok_rx, tok_own_far, swap_core(tok_rx)), ln1_row, times, feats, w_qkv,
        scale, own_heads,
    )
    clock.passed(qkv)
    times_all = Gather(
        clock, time_embed[None], [(swaps[k], img_bits[k], 0) for k in range(bits)]
    )
    times_all.tick()
    half_heads = own_heads // 2
    o_a, lse_a = attend_forward(clock.now, qkv, tables, feats, 0, half_heads)
    clock.passed(o_a, grad_rx)
    times_all.tick()
    far_a = swap_core(o_a)
    o_b, lse_b = attend_forward(clock.now, qkv, tables, feats, half_heads, half_heads)
    far_b = swap_core(o_b)

    o_own = jnp.concatenate([o_a, o_b], axis=0)
    lse = jnp.concatenate([lse_a, lse_b], axis=0)
    clock.passed(o_b)

    def turned(a):
        a = a.reshape(cols // 2, 2 * mine)
        return jnp.concatenate([a[:, mine:], a[:, :mine]], axis=1)

    o_flat = o_own.reshape(cols, 2 * mine)
    o_far = jnp.concatenate([turned(far_a), turned(far_b)], axis=0)
    attn_all = jnp.concatenate(
        [jnp.where(c == 0, o_flat, o_far), jnp.where(c == 0, o_far, o_flat)], axis=0
    )
    branch_one = dot(attn_all[:, :mine], output_projection_weight, 0, 0)
    hidden_one = x.astype(F32) + branch_one
    times_all.tick()
    mlp_in = clock.tie((moments(hidden_one)[0] * ln2_gain).astype(BF))

    tile = ff // 6
    two, slope, down, mlp_in_t, grad_branch = mlp_rise(
        mlp_in, grad_own, grad_rx, valid, w_up, w_down, ff // 3
    )
    clock.passed(two)
    down = lax.psum_scatter(down, ("img", "seq"), scatter_dimension=0, tiled=True)
    img_names = list(range(bits))[::-1]
    twos = (2,) * bits
    step = functools.partial(advance, clock, swaps)

    def finish(jobs):
        while jobs[0].result is None:
            step(jobs)

    gm, send, own = mlp_fall(
        clock.now, pair, mlp_in_t, grad_branch, w_up, w_down, slope, tile, 0, 3, ()
    )
    clock.passed(gm)
    output, grad_one, gb_mine, sums = middle(
        clock.now, gm, two, branch_one, hidden_one, grad_branch, valid, ln2_row
    )
    clock.passed(output)
    gb_far = swap_core(gb_mine)
    far_up = swap_core(lax.optimization_barrier((send, gb_far))[0])
    gb_all = jnp.concatenate([gb_mine, gb_far], axis=0)
    out_far = swap_y(output[span:])
    w_proj_rows = lax.dynamic_slice_in_dim(output_projection_weight, c * cols, cols, 0)
    do = dot(w_proj_rows, gb_all, 1, 1).astype(BF).reshape(own_heads, width, 2 * mine)
    gb_cols = lax.dynamic_slice_in_dim(gb_all, c * cols, cols, 1)
    proj_part = dot(attn_all, gb_cols, 1, 0).astype(BF)
    clock.passed(do, proj_part)

    def by_row(dims, arrays, columns_of, column=0, prefix=()):
        shape = twos + (2, rows // 2)
        return Halving(
            img_names + [on_y],
            dims,
            [a.reshape(a.shape[: len(prefix)] + shape + a.shape[-1:]) for a in arrays],
            (rows // 2, columns_of),
            prefix=prefix,
            column=column,
        )

    orders = [order(0, on_y, 1), order(on_y, 1, 0), order(1, 0, on_y)]
    up_half = ff // 4
    jobs_up = [
        by_row(dims, (own, far_up), up_half, k)
        for k, dims in enumerate([order(0, 1, on_y), order(on_y, 0, 1)])
    ]
    job_proj = by_row(orders[2], (proj_part,), cols)
    clock.passed(out_far)
    step(jobs_up + [job_proj])
    grads = attend_backward(
        clock.now, qkv, o_own, do, lse, tables, feats, scale, 0, own_heads, ()
    )
    d, toe, image_grads = grads
    clock.passed(d)
    step(jobs_up)
    part = jnp.transpose(image_grads[:, :, :4], (0, 2, 1, 3)).reshape(8, cols).astype(BF)
    gather = Gather(
        clock,
        part[None, None],
        [(swap_core, c == 1, 3), (swap_y, y == 1, 1)]
        + [(swaps[k], img_bits[k], 0) for k in range(bits)],
    )
    gather.tick()
    w_part = project_weights(clock.now, attn_in, d)
    clock.passed(w_part, job_proj.arrived[0][0])
    gather.land()
    times_all = times_all.finish()
    jobs_qkv = [by_row(dims, (w_part,), cols, prefix=(p,)) for p, dims in enumerate(orders)]
    step(jobs_qkv)
    jobs_qkv.append(job_proj)
    back, back_far = project_back(clock.now, core, d, w_qkv, mine)
    clock.passed(back)
    step(jobs_up)
    back_far = swap_core(clock.tie(back_far))
    step(jobs_qkv)
    clock.passed(down)
    down_far = swap_y(clock.tie(down))
    input_grad, sums_one = last(back, back_far, x, grad_one, ln1_row)
    clock.passed(input_grad)
    reach = jnp.arange(2 * SIDE - 1, dtype=jnp.int32)
    side = jnp.arange(SIDE, dtype=jnp.int32)
    diag = (reach == side[:, None, None] - side[None, :, None] + SIDE - 1).astype(F32)
    rel = jnp.stack([toe[:, :SIDE, :SIDE], toe[:, SIDE:, SIDE:]])
    rel = jnp.einsum("khrt,rtd->khd", rel, diag, precision=lax.Precision.HIGHEST)
    rel_all = lax.dynamic_update_slice(
        jnp.zeros((2, heads, 2 * SIDE - 1), F32), rel, (0, c * own_heads, 0)
    )
    stats = jnp.concatenate([jnp.sum(sums[1:4], axis=1), jnp.sum(valid[:, 0])[None]])
    small = jnp.concatenate([sums_one[0], sums[0], rel_all.reshape(-1), stats])
    def returned(own_rows, far_rows):
        return jnp.stack(
            [jnp.where(y == 0, own_rows, far_rows), jnp.where(y == 0, far_rows, own_rows)]
        )

    small = Total(clock, small, [swap_core, swap_y] + [swaps[k] for k in range(bits)])

    small.tick()
    step(jobs_qkv)
    gather.tick()
    down = jnp.where(y == 0, jnp.stack([down, down_far]), jnp.stack([down_far, down]))
    output = returned(output[:span], out_far)
    in_far = swap_y(clock.tie(input_grad)[span:])
    clock.passed(output)
    step(jobs_up)
    small.tick()
    gather.tick()
    down_far = swap_core(down)
    step(jobs_qkv)
    small.tick()
    gather.tick()
    h0, h1 = both_cores(down, down_far)
    w_down_grad = jnp.concatenate([h0[0], h1[0], h0[1], h1[1]], axis=0)
    clock.passed(w_down_grad)
    finish(jobs_up)
    up_parts, up_far = across_y([clock.tie(job.result) for job in jobs_up])
    finish(jobs_qkv)
    qkv_parts, qkv_far = across_y([job.result for job in jobs_qkv])
    small.tick()
    gather.tick()
    clock.passed(qkv_far, up_far)
    qkv_part, qkv_far = across_core(qkv_parts, clock.tie(qkv_far))
    up_part, up_far = across_core(up_parts, clock.tie(up_far))
    clock.passed(in_far)
    in_far = clock.tie(in_far)
    small.tick()
    gather.tick()
    u0, u1 = both_cores(up_part, up_far)
    w_up_grad = jnp.concatenate(
        [u[:, k * tile : (k + 1) * tile] for k in range(3) for u in (u0, u1)], axis=1
    )
    clock.passed(w_up_grad)
    small = small.finish()
    factors = gather.finish().reshape(n_img * slots, 8, dm)

    te_rows = lax.dynamic_slice_in_dim(times_all, me_img * rows, rows, 3)
    w_time_q_grad, w_time_v_grad = (
        lax.dot_general(
            te_rows.reshape(-1, rows),
            factors[:, 4 * k : 4 * k + 4].reshape(-1, dm),
            (((0,), (0,)), ((), ())),
            preferred_element_type=F32,
        )
        for k in range(2)
    )
    ln1_gain_grad = lax.dynamic_slice_in_dim(small, me_img * rows, rows)
    ln2_gain_grad = lax.dynamic_slice_in_dim(small, dm + me_img * rows, rows)
    rel_all = small[2 * dm : -4].reshape(2, heads, 2 * SIDE - 1)
    rms_values = jnp.sqrt(small[-4:-1] / (small[-1] * dm))
    q0, q1 = both_cores(qkv_part, qkv_far)
    w_proj_grad = jnp.concatenate([q[:, 3 * cols :] for q in (q0, q1)], axis=1)
    w_qkv_grad = jnp.concatenate(
        [q[:, p * cols : (p + 1) * cols] for p in range(3) for q in (q0, q1)], axis=1
    )

    return (
        output,
        returned(input_grad[:span], in_far),
        ln1_gain_grad,
        w_qkv_grad,
        w_time_q_grad,
        w_time_v_grad,
        rel_all[0],
        rel_all[1],
        w_proj_grad,
        ln2_gain_grad,
        w_up_grad,
        w_down_grad,
        rms_values,
    )


def solution(mesh):
    return jax.shard_map(
        per_device,
        mesh=mesh,
        in_specs=(
            P("img", "seq", None),
            P("img", None, None),
            P("img", None),
            P("img", None),
        )
        + (P(),) * 10
        + (P("img", "seq", None),),
        out_specs=(
            P("img", "seq", None),
            P("img", "seq", None),
            P("img"),
            P("img", None),
            P("img", None),
            P("img", None),
            P(),
            P(),
            P("img", None),
            P("img"),
            P("img", None),
            P("img", None),
            P(),
        ),
        check_vma=False,
    )
```

```python
import functools
import math

import jax
import jax.numpy as jnp
from jax import lax
from jax.experimental import pallas as pl
from jax.experimental.pallas import tpu as pltpu
from jax.sharding import PartitionSpec as P

SIDE = 32
EPS = 1e-06
FAR = -1e30
LANES = 128
BF = jnp.bfloat16
F32 = jnp.float32
VMEM_LIMIT = 56 * 2**20
QUERY_BLOCK = 512
FF_STEP = 512

RC = 2 * SIDE
KEY_MASK = RC
QUERY_MASK = KEY_MASK + 16
IMAGE_HOT = QUERY_MASK + 16
FEATURES = IMAGE_HOT + 16
ANYWHERE = pl.BlockSpec(memory_space=pl.ANY)


def dot(a, b, ca, cb):
    return lax.dot_general(a, b, (((ca,), (cb,)), ((), ())), preferred_element_type=F32)


def params(*semantics):
    return pltpu.CompilerParams(dimension_semantics=semantics, vmem_limit_bytes=VMEM_LIMIT)


CHEAP = pl.CostEstimate(flops=10**6, bytes_accessed=10**5, transcendentals=0)


def features_kernel(len_ref, turn_ref, base_ref, feat_ref, valid_ref, *, span):
    tokens = feat_ref.shape[1]

    def describe(shape, axis):
        index = lax.broadcasted_iota(jnp.int32, shape, axis)
        block = index // span
        pos = index - block * span
        for k in range(tokens // span):
            pos = pos + jnp.where(block == k, base_ref[k], 0)
        ends = []
        total = 0
        for j in range(4):
            total = total + len_ref[j]
            ends.append(total)
        segment = sum((pos >= ends[j]).astype(jnp.int32) for j in range(4))
        return pos, ends, segment

    pos, ends, segment = describe((1, tokens), 1)
    picked = jnp.minimum(segment, 3)
    begin = jnp.zeros_like(pos)
    length = jnp.zeros_like(pos)
    turn = jnp.zeros_like(pos)
    for j in range(4):
        here = picked == j
        begin = jnp.where(here, ends[j] - len_ref[j], begin)
        length = jnp.where(here, len_ref[j], length)
        turn = jnp.where(here, turn_ref[j], turn)
    full = length == SIDE * SIDE
    side = jnp.where(full, SIDE, SIDE // 2)
    u = pos - begin
    bits = SIDE.bit_length() - 1
    r0 = jnp.where(full, u >> bits, u >> (bits - 1))
    c0 = u & (side - 1)
    r1 = jnp.where((turn & 1) == 1, side - 1 - r0, r0)
    c1 = jnp.where(((turn >> 1) & 1) == 1, side - 1 - c0, c0)
    valid = pos < ends[3]
    row = jnp.where(valid, jnp.where(turn >= 4, c1, r1), 0)
    col = jnp.where(valid, jnp.where(turn >= 4, r1, c1), 0)
    which = lax.broadcasted_iota(jnp.int32, (SIDE, tokens), 0)
    few = lax.broadcasted_iota(jnp.int32, (16, tokens), 0)

    def put(start, value):
        feat_ref[start : start + value.shape[0], :] = value.astype(BF)

    put(0, jnp.where(which == row, 1.0, 0.0))
    put(SIDE, jnp.where(which == col, 1.0, 0.0))
    put(KEY_MASK, jnp.where(few == segment, 1.0, 0.0))
    put(QUERY_MASK, jnp.where((few < 5) & (few != segment), FAR, 0.0))
    put(IMAGE_HOT, jnp.where(few == picked, 1.0, 0.0))
    down_pos, down_ends, unused = describe(valid_ref.shape, 0)
    valid_ref[...] = jnp.where(down_pos < down_ends[3], 1.0, 0.0)


def token_features(lengths, turns, bases, span, mine):
    tokens = bases.shape[0] * span
    smem = pl.BlockSpec(memory_space=pltpu.SMEM)
    return pl.pallas_call(
        functools.partial(features_kernel, span=span),
        out_shape=(
            jax.ShapeDtypeStruct((FEATURES, tokens), BF),
            jax.ShapeDtypeStruct((mine, LANES), F32),
        ),
        in_specs=[smem, smem, smem],
        cost_estimate=CHEAP,
        name="token_features",
    )(lengths, turns, bases)


def window(cols):
    return -(-(cols + LANES // 2) // LANES) * LANES


def fetch(part, core, w_ref, room, sems, cols, dm):
    start = part * dm + (core * cols) // LANES * LANES
    start = pl.multiple_of(start, LANES)
    return pltpu.make_async_copy(
        w_ref.at[:, pl.ds(start, room.shape[2])], room.at[part], sems.at[part]
    )


def project_kernel(
    core_ref, a_ref, b_ref, c_ref, d_ref, gain_ref, time_ref, feat_ref, w_ref,
    in_ref, x_ref, qkv_ref, room, wide, sems, *, scale, cols,
):
    part = pl.program_id(0)
    core = core_ref[0]
    dm = in_ref.shape[1]
    width = qkv_ref.shape[2]

    @pl.when(part == 0)
    def _():
        for k in range(3):
            fetch(k, core, w_ref, room, sems, cols, dm).start()
        rows = a_ref.shape[0]
        x_ref[:rows, :] = a_ref[...]
        x_ref[rows:, :] = b_ref[...]
        for k, ref in enumerate((a_ref, b_ref, c_ref, d_ref)):
            x = ref[...].astype(F32)
            centre = x - jnp.mean(x, axis=-1, keepdims=True)
            spread = jnp.mean(centre * centre, axis=-1, keepdims=True)
            normed = centre * lax.rsqrt(spread + EPS) * gain_ref[...]
            in_ref[k * rows : (k + 1) * rows, :] = normed.astype(BF)

    fetch(part, core, w_ref, room, sems, cols, dm).wait()
    wide[...] = dot(room[part], in_ref[...], 0, 1)
    shift = core * cols - (core * cols) // LANES * LANES
    factor = jnp.where(part == 0, scale, 1.0)
    hot = feat_ref[IMAGE_HOT:, :].astype(F32)
    for h in range(cols // width):
        at = pl.multiple_of(shift + h * width, 8)
        x = wide[pl.ds(at, width), :]
        t = time_ref[0, h * width : (h + 1) * width, :]
        for j in range(4):
            x = x + t[:, j : j + 1] * hot[j : j + 1]
        qkv_ref[0, h] = (x * factor).astype(BF)


def project(core, blocks, gain, times, feats, w_qkv, scale, heads):
    rows, dm = blocks[0].shape
    tokens = 4 * rows
    cols = times.shape[1]
    width = cols // heads
    whole = lambda p, t: (0, 0)
    room = window(cols)
    return pl.pallas_call(
        functools.partial(project_kernel, scale=scale, cols=cols),
        grid_spec=pltpu.PrefetchScalarGridSpec(
            num_scalar_prefetch=1,
            grid=(3,),
            in_specs=[pl.BlockSpec((rows, dm), whole)] * 4
            + [
                pl.BlockSpec((1, dm), whole),
                pl.BlockSpec((1, cols, 4), lambda p, t: (p, 0, 0)),
                pl.BlockSpec(feats.shape, whole),
                ANYWHERE,
            ],
            out_specs=[
                pl.BlockSpec((tokens, dm), whole),
                pl.BlockSpec((2 * rows, dm), whole),
                pl.BlockSpec((1, heads, width, tokens), lambda p, t: (p, 0, 0, 0)),
            ],
            scratch_shapes=[
                pltpu.VMEM((3, dm, room), BF),
                pltpu.VMEM((room, tokens), F32),
                pltpu.SemaphoreType.DMA((3,)),
            ],
        ),
        out_shape=[
            jax.ShapeDtypeStruct((tokens, dm), BF),
            jax.ShapeDtypeStruct((2 * rows, dm), BF),
            jax.ShapeDtypeStruct((3, heads, width, tokens), BF),
        ],
        compiler_params=params("arbitrary"),
        cost_estimate=CHEAP,
        name="project",
    )(core, *blocks, gain, times, feats, w_qkv)


def weights_kernel(clock_ref, in_ref, d_ref, out_ref):
    d = jnp.concatenate([d_ref[0, h].astype(F32) for h in range(d_ref.shape[1])], axis=0)
    out_ref[0] = dot(in_ref[...], d.astype(BF), 0, 1).astype(BF)


def project_weights(clock, attn_in, d):
    parts, heads, width, tokens = d.shape
    dm = attn_in.shape[1]
    return pl.pallas_call(
        weights_kernel,
        grid_spec=pltpu.PrefetchScalarGridSpec(
            num_scalar_prefetch=1,
            grid=(parts,),
            in_specs=[
                pl.BlockSpec((tokens, dm), lambda p, t: (0, 0)),
                pl.BlockSpec((1, heads, width, tokens), lambda p, t: (p, 0, 0, 0)),
            ],
            out_specs=pl.BlockSpec((1, dm, heads * width), lambda p, t: (p, 0, 0)),
        ),
        out_shape=jax.ShapeDtypeStruct((parts, dm, heads * width), BF),
        compiler_params=params("arbitrary"),
        cost_estimate=CHEAP,
        name="project_weights",
    )(clock, attn_in, d)


def project_back_kernel(
    clock_ref, core_ref, d_ref, w_ref, mine_ref, far_ref, room, wide, total, sems, *, cols
):
    part = pl.program_id(0)
    core = core_ref[0]
    dm = w_ref.shape[0]
    width = d_ref.shape[2]

    @pl.when(part == 0)
    def _():
        for k in range(3):
            fetch(k, core, w_ref, room, sems, cols, dm).start()
        wide[...] = jnp.zeros_like(wide)

    shift = core * cols - (core * cols) // LANES * LANES
    for h in range(cols // width):
        at = pl.multiple_of(shift + h * width, 8)
        wide[pl.ds(at, width), :] = d_ref[0, h].astype(F32)
    fetch(part, core, w_ref, room, sems, cols, dm).wait()
    term = dot(wide[...].astype(BF), room[part], 0, 1)

    @pl.when(part == 0)
    def _():
        total[...] = term

    @pl.when(part == 1)
    def _():
        total[...] += term

    @pl.when(part == 2)
    def _():
        rows = mine_ref.shape[0]
        mine_ref[...] = total[:rows, :] + term[:rows]
        far_ref[...] = (total[rows:, :] + term[rows:]).astype(BF)


def project_back(clock, core, d, w_qkv, mine):
    parts, heads, width, tokens = d.shape
    dm = w_qkv.shape[0]
    cols = heads * width
    room = window(cols)
    whole = lambda p, t, u: (0, 0)
    return pl.pallas_call(
        functools.partial(project_back_kernel, cols=cols),
        grid_spec=pltpu.PrefetchScalarGridSpec(
            num_scalar_prefetch=2,
            grid=(parts,),
            in_specs=[
                pl.BlockSpec((1, heads, width, tokens), lambda p, t, u: (p, 0, 0, 0)),
                ANYWHERE,
            ],
            out_specs=[pl.BlockSpec((mine, dm), whole), pl.BlockSpec((tokens - mine, dm), whole)],
            scratch_shapes=[
                pltpu.VMEM((3, dm, room), BF),
                pltpu.VMEM((room, tokens), F32),
                pltpu.VMEM((tokens, dm), F32),
                pltpu.SemaphoreType.DMA((3,)),
            ],
        ),
        out_shape=[
            jax.ShapeDtypeStruct((mine, dm), F32),
            jax.ShapeDtypeStruct((tokens - mine, dm), BF),
        ],
        compiler_params=params("arbitrary"),
        cost_estimate=CHEAP,
        name="project_back",
    )(clock, core, d, w_qkv)


def query_block(b, bias, feat_ref, q):
    at = slice(b * QUERY_BLOCK, (b + 1) * QUERY_BLOCK)
    return jnp.concatenate([bias[:, at], feat_ref[QUERY_MASK:IMAGE_HOT, at], q[:, at]], axis=0)


def forward_kernel(clock_ref, p_ref, table_ref, feat_ref, o_ref, lse_ref):
    blocks = p_ref.shape[3] // QUERY_BLOCK
    q, k, v = (p_ref[p, 0] for p in range(3))
    bias = jnp.dot(table_ref[0], feat_ref[:RC], preferred_element_type=F32).astype(BF)
    key = jnp.concatenate([feat_ref[:QUERY_MASK], k], axis=0).T

    def scores(b):
        return jnp.dot(key, query_block(b, bias, feat_ref, q), preferred_element_type=F32)

    ahead = scores(0)
    for b in range(blocks):
        at = slice(b * QUERY_BLOCK, (b + 1) * QUERY_BLOCK)
        s = ahead
        top = jnp.max(s, axis=0, keepdims=True)
        if b + 1 < blocks:
            ahead = scores(b + 1)
        e = jnp.exp(s - top)
        total = jnp.sum(e, axis=0, keepdims=True)
        o = jnp.dot(v, e.astype(BF), preferred_element_type=F32) / total
        o_ref[0, :, at] = o.astype(BF)
        lse_ref[0, :, at] = top + jnp.log(total)


def attend_forward(clock, qkv, tables, feats, first, count):
    parts, heads, width, tokens = qkv.shape
    return pl.pallas_call(
        forward_kernel,
        grid_spec=pltpu.PrefetchScalarGridSpec(
            num_scalar_prefetch=1,
            grid=(count,),
            in_specs=[
                pl.BlockSpec((parts, 1, width, tokens), lambda h, t: (0, first + h, 0, 0)),
                pl.BlockSpec((1, RC, RC), lambda h, t: (first + h, 0, 0)),
                pl.BlockSpec(feats.shape, lambda h, t: (0, 0)),
            ],
            out_specs=[
                pl.BlockSpec((1, width, tokens), lambda h, t: (h, 0, 0)),
                pl.BlockSpec((1, 1, tokens), lambda h, t: (h, 0, 0)),
            ],
        ),
        out_shape=[
            jax.ShapeDtypeStruct((count, width, tokens), BF),
            jax.ShapeDtypeStruct((count, 1, tokens), F32),
        ],
        compiler_params=params("arbitrary"),
        cost_estimate=CHEAP,
        name="attention_forward",
    )(clock, qkv, tables, feats)


def backward_kernel(clock_ref, qkv_ref, o_ref, do_ref, lse_ref, table_ref, feat_ref, *rest, scale):
    d_ref, toe_ref, image_ref = rest[-3:]
    width = o_ref.shape[1]
    tokens = o_ref.shape[2]
    q, k, v = (qkv_ref[p, 0] for p in range(3))
    do = do_ref[0]
    delta = jnp.sum(do.astype(F32) * o_ref[0].astype(F32), axis=0, keepdims=True)
    rc = feat_ref[:RC]
    bias = jnp.dot(table_ref[0], rc, preferred_element_type=F32).astype(BF)
    key_t = jnp.concatenate([feat_ref[:QUERY_MASK], k], axis=0)
    key = key_t.T
    value = v.T
    dk = jnp.zeros((tokens, width), F32)
    dv = jnp.zeros((tokens, width), F32)
    dq_parts, bias_parts = [], []

    def first(b):
        at = slice(b * QUERY_BLOCK, (b + 1) * QUERY_BLOCK)
        s = jnp.dot(key, query_block(b, bias, feat_ref, q), preferred_element_type=F32)
        return s, jnp.dot(value, do[:, at], preferred_element_type=F32)

    ahead = first(0)
    for b in range(tokens // QUERY_BLOCK):
        at = slice(b * QUERY_BLOCK, (b + 1) * QUERY_BLOCK)
        s, dp = ahead
        p = jnp.exp(s - lse_ref[0, :, at])
        ds = (p * (dp - delta[:, at])).astype(BF)
        p = p.astype(BF)
        if (b + 1) * QUERY_BLOCK < tokens:
            ahead = first(b + 1)
        dq = jnp.dot(key_t, ds, preferred_element_type=F32)
        dq_parts.append((dq[QUERY_MASK:] * scale).astype(BF))
        bias_parts.append(dq[:RC].astype(BF))
        dk = dk + dot(ds, q[:, at], 1, 1)
        dv = dv + dot(p, do[:, at], 1, 1)
    toe = dot(rc, jnp.concatenate(bias_parts, axis=1), 1, 1)
    dq = jnp.concatenate(dq_parts, axis=1)
    dk = dk.T.astype(BF)
    dv = dv.T.astype(BF)
    d_ref[0, 0] = dq
    d_ref[1, 0] = dk
    d_ref[2, 0] = dv
    toe_ref[0] = toe
    hot = feat_ref[IMAGE_HOT:]
    image_ref[0, 0] = dot(hot, dq, 1, 1)
    image_ref[1, 0] = dot(hot, dv, 1, 1)


def attend_backward(clock, qkv, o, do, lse, tables, feats, scale, first, count, before):
    parts, heads, width, tokens = qkv.shape
    head3 = lambda h, t: (first + h, 0, 0)
    head4 = lambda h, t: (0, first + h, 0, 0)
    return pl.pallas_call(
        functools.partial(backward_kernel, scale=scale),
        grid_spec=pltpu.PrefetchScalarGridSpec(
            num_scalar_prefetch=1,
            grid=(count,),
            in_specs=[
                pl.BlockSpec((parts, 1, width, tokens), head4),
                pl.BlockSpec((1, width, tokens), head3),
                pl.BlockSpec((1, width, tokens), head3),
                pl.BlockSpec((1, 1, tokens), head3),
                pl.BlockSpec((1, RC, RC), head3),
                pl.BlockSpec(feats.shape, lambda h, t: (0, 0)),
            ]
            + [ANYWHERE] * len(before),
            out_specs=[
                pl.BlockSpec((parts, 1, width, tokens), head4),
                pl.BlockSpec((1, RC, RC), head3),
                pl.BlockSpec((2, 1, 16, width), head4),
            ],
        ),
        out_shape=[
            jax.ShapeDtypeStruct((parts, heads, width, tokens), BF),
            jax.ShapeDtypeStruct((heads, RC, RC), F32),
            jax.ShapeDtypeStruct((2, heads, 16, width), F32),
        ],
        input_output_aliases={7 + k: k for k in range(len(before))},
        compiler_params=params("arbitrary"),
        cost_estimate=CHEAP,
        name="attention_backward",
    )(clock, qkv, o, do, lse, tables, feats, *before)


def rise_kernel(
    m_ref, near_ref, far_ref, valid_ref, up_ref, down_ref,
    two_ref, slope_ref, wd_ref, mt_ref, g_ref,
):
    @pl.when(pl.program_id(0) == 0)
    def _():
        two_ref[...] = jnp.zeros_like(two_ref)
        mt_ref[...] = m_ref[...].T
        half = near_ref.shape[0]
        g_ref[:half, :] = (near_ref[...].astype(F32) * valid_ref[:half, :1]).astype(BF)
        g_ref[half:, :] = (far_ref[...].astype(F32) * valid_ref[half:, :1]).astype(BF)

    def up_of(j):
        return jnp.dot(m_ref[...], up_ref[:, j : j + FF_STEP], preferred_element_type=F32)

    acts = []
    tile = up_ref.shape[1]
    ahead = up_of(0)
    for j in range(0, tile, FF_STEP):
        at = slice(j, j + FF_STEP)
        up = ahead
        if j + FF_STEP < tile:
            ahead = up_of(j + FF_STEP)
        half = 0.5 + 0.5 * lax.erf(up * math.sqrt(0.5))
        slope = half + up * (jnp.exp(-0.5 * up * up) * (1.0 / math.sqrt(2.0 * math.pi)))
        slope_ref[:, at] = slope.astype(BF)
        acts.append((up * half).astype(BF))
    act = jnp.concatenate(acts, axis=1)
    wd_ref[...] = dot(act, g_ref[...], 0, 0).astype(BF)
    two_ref[...] += jnp.dot(act, down_ref[...], preferred_element_type=F32)


def mlp_rise(m, near, far, valid, w_up, w_down, tile):
    rows, dm = m.shape
    ff = w_up.shape[1]
    whole = lambda i: (0, 0)
    return pl.pallas_call(
        rise_kernel,
        grid=(ff // tile,),
        in_specs=[
            pl.BlockSpec((rows, dm), whole),
            pl.BlockSpec(near.shape, whole),
            pl.BlockSpec(far.shape, whole),
            pl.BlockSpec(valid.shape, whole),
            pl.BlockSpec((dm, tile), lambda i: (0, i)),
            pl.BlockSpec((tile, dm), lambda i: (i, 0)),
        ],
        out_specs=[
            pl.BlockSpec((rows, dm), whole),
            pl.BlockSpec((rows, tile), lambda i: (0, i)),
            pl.BlockSpec((tile, dm), lambda i: (i, 0)),
            pl.BlockSpec((dm, rows), whole),
            pl.BlockSpec((rows, dm), whole),
        ],
        out_shape=[
            jax.ShapeDtypeStruct((rows, dm), F32),
            jax.ShapeDtypeStruct((rows, ff), BF),
            jax.ShapeDtypeStruct((ff, dm), BF),
            jax.ShapeDtypeStruct((dm, rows), BF),
            jax.ShapeDtypeStruct((rows, dm), BF),
        ],
        compiler_params=params("arbitrary"),
        cost_estimate=CHEAP,
        name="feed_forward_rise",
    )(m, near, far, valid, w_up, w_down)


def fall_kernel(clock_ref, tile_ref, mt_ref, g_ref, up_ref, down_ref, slope_ref, *rest):
    gm_out, send_ref, own_ref = rest[-3:]
    step = pl.program_id(0)

    @pl.when(step == 0)
    def _():
        gm_out[...] = rest[0][...] if len(rest) > 3 else jnp.zeros_like(gm_out)

    du = (dot(g_ref[...], down_ref[...], 1, 1) * slope_ref[...].astype(F32)).astype(BF)
    gm_out[...] += dot(du, up_ref[...], 1, 1)
    wu = jnp.dot(mt_ref[...], du, preferred_element_type=F32).astype(BF)

    @pl.when(step % 2 == 0)
    def _():
        send_ref[...] = wu

    @pl.when(step % 2 == 1)
    def _():
        own_ref[...] = wu


def mlp_fall(clock, tiles, mt, g, w_up, w_down, slope, tile, first, pairs, before):
    dm, rows = mt.shape
    ff = w_up.shape[1]
    whole = lambda i, u, t: (0, 0)
    column = lambda i, u, t: (0, first + i // 2)
    at = lambda i, t: 2 * (first + i // 2) + t[i % 2]
    return pl.pallas_call(
        fall_kernel,
        grid_spec=pltpu.PrefetchScalarGridSpec(
            num_scalar_prefetch=2,
            grid=(2 * pairs,),
            in_specs=[
                pl.BlockSpec((dm, rows), whole),
                pl.BlockSpec((rows, dm), whole),
                pl.BlockSpec((dm, tile), lambda i, u, t: (0, at(i, t))),
                pl.BlockSpec((tile, dm), lambda i, u, t: (at(i, t), 0)),
                pl.BlockSpec((rows, tile), lambda i, u, t: (0, at(i, t))),
            ]
            + ([pl.BlockSpec((rows, dm), whole), ANYWHERE, ANYWHERE] if before else []),
            out_specs=[
                pl.BlockSpec((rows, dm), whole),
                pl.BlockSpec((dm, tile), column),
                pl.BlockSpec((dm, tile), column),
            ],
        ),
        out_shape=[
            jax.ShapeDtypeStruct((rows, dm), F32),
            jax.ShapeDtypeStruct((dm, ff // 2), BF),
            jax.ShapeDtypeStruct((dm, ff // 2), BF),
        ],
        input_output_aliases={8: 1, 9: 2} if before else {},
        compiler_params=params("arbitrary"),
        cost_estimate=CHEAP,
        name="feed_forward_fall",
    )(clock, tiles, mt, g, w_up, w_down, slope, *before)


def moments(x):
    centre = x - jnp.mean(x, axis=-1, keepdims=True)
    root = lax.rsqrt(jnp.mean(centre * centre, axis=-1, keepdims=True) + EPS)
    return centre * root, root


def norm_backward(d, n, root):
    return root * (
        d - jnp.mean(d, axis=-1, keepdims=True) - n * jnp.mean(d * n, axis=-1, keepdims=True)
    )


def columns(x):
    return jnp.sum(x, axis=0, keepdims=True)


def middle_kernel(
    clock_ref, gm_ref, two_ref, one_ref, h_ref, g_ref, valid_ref, gain_ref,
    out_ref, grad_ref, low_ref, sums_ref,
):
    @pl.when(pl.program_id(0) == 0)
    def _():
        sums_ref[...] = jnp.zeros_like(sums_ref)

    valid = valid_ref[:, :1]
    two, one, h = two_ref[...], one_ref[...], h_ref[...]
    h2 = h + two
    out_ref[...] = (h2 * valid).astype(BF)
    n, root = moments(h)
    gm = gm_ref[...]
    grad = g_ref[...].astype(F32) + norm_backward(gm * gain_ref[...], n, root)
    grad_ref[...] = grad
    low_ref[...] = grad.astype(BF)
    sums_ref[0:1, :] += columns(gm * n)
    sums_ref[1:2, :] += columns(valid * h2 * h2)
    sums_ref[2:3, :] += columns(valid * one * one)
    sums_ref[3:4, :] += columns(valid * two * two)


def middle(clock, gm, two, one, hidden, grads, valid, gain):
    rows, dm = gm.shape
    step = rows // 4
    block = pl.BlockSpec((step, dm), lambda i, t: (i, 0))
    return pl.pallas_call(
        middle_kernel,
        grid_spec=pltpu.PrefetchScalarGridSpec(
            num_scalar_prefetch=1,
            grid=(4,),
            in_specs=[block] * 5
            + [
                pl.BlockSpec((step, LANES), lambda i, t: (i, 0)),
                pl.BlockSpec((1, dm), lambda i, t: (0, 0)),
            ],
            out_specs=[block, block, block, pl.BlockSpec((8, dm), lambda i, t: (0, 0))],
        ),
        out_shape=[
            jax.ShapeDtypeStruct((rows, dm), BF),
            jax.ShapeDtypeStruct((rows, dm), F32),
            jax.ShapeDtypeStruct((rows, dm), BF),
            jax.ShapeDtypeStruct((8, dm), F32),
        ],
        compiler_params=params("arbitrary"),
        cost_estimate=CHEAP,
        name="middle",
    )(clock, gm, two, one, hidden, grads, valid, gain)


def last_kernel(back_ref, far_ref, x_ref, grad_ref, gain_ref, out_ref, sums_ref):
    @pl.when(pl.program_id(0) == 0)
    def _():
        sums_ref[...] = jnp.zeros_like(sums_ref)

    back = back_ref[...] + far_ref[...].astype(F32)
    n, root = moments(x_ref[...].astype(F32))
    out_ref[...] = (grad_ref[...] + norm_backward(back * gain_ref[...], n, root)).astype(BF)
    sums_ref[0:1, :] += columns(back * n)


def last(back, far, x, grad, gain):
    rows, dm = back.shape
    step = rows // 4
    block = pl.BlockSpec((step, dm), lambda i: (i, 0))
    return pl.pallas_call(
        last_kernel,
        grid=(4,),
        in_specs=[block] * 4 + [pl.BlockSpec((1, dm), lambda i: (0, 0))],
        out_specs=[block, pl.BlockSpec((8, dm), lambda i: (0, 0))],
        out_shape=[jax.ShapeDtypeStruct((rows, dm), BF), jax.ShapeDtypeStruct((8, dm), F32)],
        compiler_params=params("arbitrary"),
        cost_estimate=CHEAP,
        name="last",
    )(back, far, x, grad, gain)


class Halving:
    def __init__(self, names, dims, base, piece, prefix=(), suffix=(), column=0):
        self.names, self.dims, self.base, self.piece = names, dims, base, piece
        self.prefix, self.suffix, self.column = prefix, suffix, column
        self.stage, self.arrived, self.result = 0, [], None

    def left(self, stage):
        return [d for d in self.names if d in self.dims[stage + 1 :]]

    def specs(self, gridded):
        stage = self.stage
        open_dims = self.left(stage)

        def index(names, prefix, suffix, column):
            def at(*grid):
                t = grid[-1]
                out = list(prefix)
                for d in names:
                    if d in gridded:
                        out.append(grid[gridded.index(d)])
                    elif d in open_dims:
                        out.append(0)
                    elif stage < len(self.dims) and d == self.dims[stage]:
                        out.append(1 - t[d])
                    else:
                        out.append(t[d])
                return tuple(out) + tuple(suffix) + (0, column)

            return at

        def block(names, prefix, suffix):
            sizes = [2 if d in open_dims and d not in gridded else None for d in names]
            return (None,) * len(prefix) + tuple(sizes) + (None,) * len(suffix) + self.piece

        arrays, specs = [], []
        for array in self.base:
            arrays.append(array)
            specs.append(
                pl.BlockSpec(
                    block(self.names, self.prefix, self.suffix),
                    index(self.names, self.prefix, self.suffix, self.column),
                )
            )
        for s, (array, place) in enumerate(self.arrived):
            arrays.append(array)
            names = self.left(s)
            specs.append(pl.BlockSpec(block(names, (place,), ()), index(names, (place,), (), 0)))
        rest = index(open_dims, (), (), 0)
        inner = tuple(2 if d not in gridded else None for d in open_dims) + self.piece
        return arrays, specs, inner, rest, (2,) * len(open_dims) + self.piece


def sum_kernel(coord_ref, *refs, counts, places):
    outs = refs[sum(counts) :]
    at = 0
    for (out, place), count in zip(places, counts):
        total = refs[at][...].astype(F32)
        for k in range(1, count):
            total = total + refs[at + k][...].astype(F32)
        outs[out][place] = total.astype(BF)
        at += count


def advance(clock, swaps, jobs):
    arrays, in_specs, counts, groups, places = [], [], [], [], []
    stage = jobs[0].stage
    steps = min(2, max(0, len(jobs[0].left(stage)) - 1))
    for job in jobs:
        some, their, inner, rest, shape = job.specs(job.left(stage)[:steps])
        arrays, in_specs = arrays + some, in_specs + their
        counts.append(len(some))
        sent = job.dims[stage] if stage < len(job.dims) else None
        key = (sent, shape)
        found = [k for k, g in enumerate(groups) if g[0] == key]
        if not found:
            groups.append((key, inner, rest, []))
        group = found[0] if found else len(groups) - 1
        places.append((group, len(groups[group][3])))
        groups[group][3].append(job)
    out_specs = [
        pl.BlockSpec((len(g[3]),) + g[1], lambda *grid, f=g[2]: (0,) + f(*grid)) for g in groups
    ]
    sums = pl.pallas_call(
        functools.partial(sum_kernel, counts=counts, places=places),
        grid_spec=pltpu.PrefetchScalarGridSpec(
            num_scalar_prefetch=1,
            grid=(2,) * steps if steps else (1,),
            in_specs=in_specs,
            out_specs=out_specs,
        ),
        out_shape=[jax.ShapeDtypeStruct((len(g[3]),) + g[0][1], BF) for g in groups],
        compiler_params=params(*("arbitrary",) * max(steps, 1)),
        cost_estimate=CHEAP,
        name="sum_pieces",
    )(clock.now, *arrays)
    for (key, inner, rest, members), total in zip(groups, sums):
        if key[0] is not None:
            total = swaps[key[0]](total)
        for k, job in enumerate(members):
            if key[0] is None:
                job.result = total[k]
            else:
                job.arrived.append((total, k))
                job.stage += 1
    clock.passed(*sums)


class Clock:
    def __init__(self, now):
        self.now = now

    def passed(self, *results):
        self.now = lax.optimization_barrier((self.now, *results))[0]

    def tie(self, x):
        return lax.optimization_barrier((x, self.now))[0]


class Gather:
    def __init__(self, clock, part, swaps):
        self.clock, self.part, self.swaps, self.far = clock, part, list(swaps), None

    def land(self):
        if self.far is not None:
            bit, axis = self.put
            low, high = jnp.where(bit, self.far, self.part), jnp.where(bit, self.part, self.far)
            self.part = jnp.concatenate([low, high], axis=axis)
            self.clock.passed(self.part)
            self.far = None

    def tick(self):
        self.land()
        if self.swaps:
            swap, bit, axis = self.swaps.pop(0)
            self.put = (bit, axis)
            self.far = swap(self.clock.tie(self.part))

    def finish(self):
        while self.far is not None or self.swaps:
            self.tick()
        return self.part


class Total:
    def __init__(self, clock, part, swaps):
        self.clock, self.part, self.swaps, self.far = clock, part, list(swaps), None

    def tick(self):
        if self.far is not None:
            self.part = self.part + self.far
            self.clock.passed(self.part)
            self.far = None
        if self.swaps:
            self.far = self.swaps.pop(0)(self.clock.tie(self.part))

    def finish(self):
        while self.far is not None or self.swaps:
            self.tick()
        return self.part


def pick(array, index, axis=0):
    return lax.dynamic_index_in_dim(array, index, axis, keepdims=False)


def toeplitz_tables(rel, count):
    d = jnp.arange(2 * count - 1, dtype=jnp.int32)
    t = jnp.arange(count, dtype=jnp.int32)
    hot = (d[:, None, None] == t[None, None, :] - t[None, :, None] + count - 1).astype(BF)
    return jnp.einsum("hd,dtr->htr", rel.astype(BF), hot, preferred_element_type=F32)


def per_device(
    tokens, time_embed, image_lengths, grid_turns, ln1_gain, w_qkv, w_time_q, time_value_weight,
    rel_rows, rel_cols, output_projection_weight, ln2_gain, w_up, w_down, out_grad,
):
    slots, span, dm = tokens.shape
    heads = rel_rows.shape[0]
    width = dm // heads
    ff = w_up.shape[1]
    scale = width ** (-0.5)
    n_seq = lax.axis_size("seq")
    n_img = lax.axis_size("img")
    cores = n_seq // slots
    own_heads = heads // cores
    cols = own_heads * width
    me_img = lax.axis_index("img")
    me_seq = lax.axis_index("seq")
    y = me_seq // cores
    c = me_seq % cores
    mine = slots * span
    rows = dm // n_img
    over_y = [(s, (slots - 1 - s // cores) * cores + s % cores) for s in range(n_seq)]
    over_core = [(s, s // cores * cores + cores - 1 - s % cores) for s in range(n_seq)]

    def swap_y(a):
        return lax.ppermute(a, "seq", over_y)

    def swap_core(a):
        return lax.ppermute(a, "seq", over_core)

    bits = n_img.bit_length() - 1
    on_y, on_core = bits, bits + 1
    swaps = {
        k: functools.partial(
            lax.ppermute, axis_name="img", perm=[(i, i ^ (1 << k)) for i in range(n_img)]
        )
        for k in range(bits)
    }
    swaps[on_y], swaps[on_core] = swap_y, swap_core

    def across_y(parts):
        part = jnp.concatenate(parts, axis=1)
        return part, swap_y(part)

    def across_core(part, far):
        part = jnp.concatenate([jnp.where(y == 0, part, far), jnp.where(y == 0, far, part)], axis=0)
        return part, swap_core(part)

    def both_cores(part, far):
        return jnp.where(c == 0, part, far).astype(F32), jnp.where(c == 0, far, part).astype(F32)

    def order(*first):
        return list(first) + [k for k in range(bits) if k not in first]

    tok_own = pick(tokens, y)
    tok_rx = swap_y(pick(tokens, 1 - y))
    tok_own_far = swap_core(tok_own)
    block = lambda yy, cc: (yy * cores + cc) * span
    bases = jnp.stack([block(y, c), block(1 - y, c), block(y, 1 - c), block(1 - y, 1 - c)])
    feats, valid = token_features(
        pick(image_lengths, y), pick(grid_turns, y), bases.astype(jnp.int32), span, mine
    )
    coords = jnp.stack([(me_img >> k) & 1 for k in range(bits)] + [y, c]).astype(jnp.int32)
    core = c.astype(jnp.int32).reshape(1)
    pair = jnp.stack([1 - c, c]).astype(jnp.int32)
    te = pick(time_embed, y)

    def time_terms(w):
        all_heads = dot(te, w, 1, 0)
        return lax.dynamic_slice_in_dim(all_heads, c * cols, cols, 1).T

    time_q = time_terms(w_time_q)
    times = jnp.stack([time_q, jnp.zeros_like(time_q), time_terms(time_value_weight)])
    row_table = toeplitz_tables(lax.dynamic_slice_in_dim(rel_rows, c * own_heads, own_heads), SIDE)
    col_table = toeplitz_tables(lax.dynamic_slice_in_dim(rel_cols, c * own_heads, own_heads), SIDE)
    gap = jnp.zeros_like(row_table)
    tables = jnp.concatenate(
        [
            jnp.concatenate([row_table, gap], axis=2),
            jnp.concatenate([gap, col_table], axis=2),
        ],
        axis=1,
    ).astype(BF)
    ln1_row, ln2_row = ln1_gain.reshape(1, dm), ln2_gain.reshape(1, dm)
    grad_out = pick(out_grad, 1 - y)
    grad_own = pick(out_grad, y)

    img_bits = [((me_img >> k) & 1) == 1 for k in range(bits)]
    clock = Clock(coords)
    clock.passed(feats, times, tables, core, pair, grad_out, grad_own, ln1_row, ln2_row)
    tok_rx = clock.tie(tok_rx)
    grad_rx = swap_y(lax.optimization_barrier((grad_out, tok_rx))[0])
    attn_in, x, qkv = project(
        core, (tok_own, tok_rx, tok_own_far, swap_core(tok_rx)), ln1_row, times, feats, w_qkv,
        scale, own_heads,
    )
    clock.passed(qkv)
    half_heads = own_heads // 2
    o_a, lse_a = attend_forward(clock.now, qkv, tables, feats, 0, half_heads)
    clock.passed(o_a, grad_rx)
    far_a = swap_core(o_a)
    o_b, lse_b = attend_forward(clock.now, qkv, tables, feats, half_heads, half_heads)
    far_b = swap_core(o_b)

    o_own = jnp.concatenate([o_a, o_b], axis=0)
    lse = jnp.concatenate([lse_a, lse_b], axis=0)
    clock.passed(o_b)

    def turned(a):
        a = a.reshape(cols // 2, 2 * mine)
        return jnp.concatenate([a[:, mine:], a[:, :mine]], axis=1)

    o_flat = o_own.reshape(cols, 2 * mine)
    o_far = jnp.concatenate([turned(far_a), turned(far_b)], axis=0)
    attn_all = jnp.concatenate(
        [jnp.where(c == 0, o_flat, o_far), jnp.where(c == 0, o_far, o_flat)], axis=0
    )
    branch_one = dot(attn_all[:, :mine], output_projection_weight, 0, 0)
    hidden_one = x.astype(F32) + branch_one
    mlp_in = clock.tie((moments(hidden_one)[0] * ln2_gain).astype(BF))

    tile = ff // 6
    two, slope, down, mlp_in_t, grad_branch = mlp_rise(
        mlp_in, grad_own, grad_rx, valid, w_up, w_down, ff // 3
    )
    clock.passed(two)
    down = lax.psum_scatter(down, ("img", "seq"), scatter_dimension=0, tiled=True)
    img_names = list(range(bits))[::-1]
    twos = (2,) * bits
    step = functools.partial(advance, clock, swaps)

    def finish(jobs):
        while jobs[0].result is None:
            step(jobs)

    gm, send, own = mlp_fall(
        clock.now, pair, mlp_in_t, grad_branch, w_up, w_down, slope, tile, 0, 3, ()
    )
    clock.passed(gm)
    output, grad_one, gb_mine, sums = middle(
        clock.now, gm, two, branch_one, hidden_one, grad_branch, valid, ln2_row
    )
    clock.passed(output)
    gb_far = swap_core(gb_mine)
    far_up = swap_core(lax.optimization_barrier((send, gb_far))[0])
    gb_all = jnp.concatenate([gb_mine, gb_far], axis=0)
    out_far = swap_y(output[span:])
    w_proj_rows = lax.dynamic_slice_in_dim(output_projection_weight, c * cols, cols, 0)
    do = dot(w_proj_rows, gb_all, 1, 1).astype(BF).reshape(own_heads, width, 2 * mine)
    gb_cols = lax.dynamic_slice_in_dim(gb_all, c * cols, cols, 1)
    proj_part = dot(attn_all, gb_cols, 1, 0).astype(BF)
    clock.passed(do, proj_part)

    def by_row(dims, arrays, columns_of, column=0, prefix=()):
        shape = twos + (2, rows // 2)
        return Halving(
            img_names + [on_y],
            dims,
            [a.reshape(a.shape[: len(prefix)] + shape + a.shape[-1:]) for a in arrays],
            (rows // 2, columns_of),
            prefix=prefix,
            column=column,
        )

    orders = [order(0, on_y, 1), order(on_y, 1, 0), order(1, 0, on_y)]
    up_half = ff // 4
    jobs_up = [
        by_row(dims, (own, far_up), up_half, k)
        for k, dims in enumerate([order(0, 1, on_y), order(on_y, 0, 1)])
    ]
    job_proj = by_row(orders[2], (proj_part,), cols)
    clock.passed(out_far)
    step(jobs_up + [job_proj])
    grads = attend_backward(
        clock.now, qkv, o_own, do, lse, tables, feats, scale, 0, own_heads, ()
    )
    d, toe, image_grads = grads
    clock.passed(d)
    step(jobs_up)
    part = jnp.transpose(image_grads[:, :, :4], (0, 2, 1, 3)).reshape(8, cols).astype(BF)
    gather = Gather(
        clock,
        part[None, None],
        [(swap_core, c == 1, 3), (swap_y, y == 1, 1)]
        + [(swaps[k], img_bits[k], 0) for k in [*range(1, bits), 0]],
    )
    gather.tick()
    w_part = project_weights(clock.now, attn_in, d)
    clock.passed(w_part, job_proj.arrived[0][0])
    gather.land()
    gather.part = jnp.concatenate([gather.part, te[None, None]], axis=2)
    jobs_qkv = [by_row(dims, (w_part,), cols, prefix=(p,)) for p, dims in enumerate(orders)]
    step(jobs_qkv)
    jobs_qkv.append(job_proj)
    back, back_far = project_back(clock.now, core, d, w_qkv, mine)
    clock.passed(back)
    step(jobs_up)
    back_far = swap_core(clock.tie(back_far))
    step(jobs_qkv)
    clock.passed(down)
    down_far = swap_y(clock.tie(down))
    input_grad, sums_one = last(back, back_far, x, grad_one, ln1_row)
    clock.passed(input_grad)
    reach = jnp.arange(2 * SIDE - 1, dtype=jnp.int32)
    side = jnp.arange(SIDE, dtype=jnp.int32)
    diag = (reach == side[:, None, None] - side[None, :, None] + SIDE - 1).astype(F32)
    rel = jnp.stack([toe[:, :SIDE, :SIDE], toe[:, SIDE:, SIDE:]])
    rel = jnp.einsum("khrt,rtd->khd", rel, diag, precision=lax.Precision.HIGHEST)
    rel_all = lax.dynamic_update_slice(
        jnp.zeros((2, heads, 2 * SIDE - 1), F32), rel, (0, c * own_heads, 0)
    )
    stats = jnp.concatenate([jnp.sum(sums[1:4], axis=1), jnp.sum(valid[:, 0])[None]])
    small = jnp.concatenate([sums_one[0], sums[0], rel_all.reshape(-1), stats])
    def returned(own_rows, far_rows):
        return jnp.stack(
            [jnp.where(y == 0, own_rows, far_rows), jnp.where(y == 0, far_rows, own_rows)]
        )

    small = Total(clock, small, [swap_core, swap_y] + [swaps[k] for k in range(bits)])

    small.tick()
    step(jobs_qkv)
    gather.tick()
    down = jnp.where(y == 0, jnp.stack([down, down_far]), jnp.stack([down_far, down]))
    output = returned(output[:span], out_far)
    in_far = swap_y(clock.tie(input_grad)[span:])
    clock.passed(output)
    step(jobs_up)
    small.tick()
    gather.tick()
    down_far = swap_core(down)
    step(jobs_qkv)
    small.tick()
    gather.tick()
    h0, h1 = both_cores(down, down_far)
    w_down_grad = jnp.concatenate([h0[0], h1[0], h0[1], h1[1]], axis=0)
    clock.passed(w_down_grad)
    finish(jobs_up)
    up_parts, up_far = across_y([clock.tie(job.result) for job in jobs_up])
    finish(jobs_qkv)
    qkv_parts, qkv_far = across_y([job.result for job in jobs_qkv])
    small.tick()
    gather.tick()
    clock.passed(qkv_far, up_far)
    qkv_part, qkv_far = across_core(qkv_parts, clock.tie(qkv_far))
    up_part, up_far = across_core(up_parts, clock.tie(up_far))
    clock.passed(in_far)
    in_far = clock.tie(in_far)
    small.tick()
    gather.tick()
    u0, u1 = both_cores(up_part, up_far)
    w_up_grad = jnp.concatenate(
        [u[:, k * tile : (k + 1) * tile] for k in range(3) for u in (u0, u1)], axis=1
    )
    clock.passed(w_up_grad)
    small = small.finish()
    factors = gather.finish().reshape(n_img * slots, 12, dm)

    te_rows = lax.dynamic_slice_in_dim(factors[:, 8:], me_img * rows, rows, 2)
    w_time_q_grad, w_time_v_grad = (
        lax.dot_general(
            te_rows.reshape(-1, rows),
            factors[:, 4 * k : 4 * k + 4].reshape(-1, dm),
            (((0,), (0,)), ((), ())),
            preferred_element_type=F32,
        )
        for k in range(2)
    )
    ln1_gain_grad = lax.dynamic_slice_in_dim(small, me_img * rows, rows)
    ln2_gain_grad = lax.dynamic_slice_in_dim(small, dm + me_img * rows, rows)
    rel_all = small[2 * dm : -4].reshape(2, heads, 2 * SIDE - 1)
    rms_values = jnp.sqrt(small[-4:-1] / (small[-1] * dm))
    q0, q1 = both_cores(qkv_part, qkv_far)
    w_proj_grad = jnp.concatenate([q[:, 3 * cols :] for q in (q0, q1)], axis=1)
    w_qkv_grad = jnp.concatenate(
        [q[:, p * cols : (p + 1) * cols] for p in range(3) for q in (q0, q1)], axis=1
    )

    return (
        output,
        returned(input_grad[:span], in_far),
        ln1_gain_grad,
        w_qkv_grad,
        w_time_q_grad,
        w_time_v_grad,
        rel_all[0],
        rel_all[1],
        w_proj_grad,
        ln2_gain_grad,
        w_up_grad,
        w_down_grad,
        rms_values,
    )


def solution(mesh):
    return jax.shard_map(
        per_device,
        mesh=mesh,
        in_specs=(
            P("img", "seq", None),
            P("img", None, None),
            P("img", None),
            P("img", None),
        )
        + (P(),) * 10
        + (P("img", "seq", None),),
        out_specs=(
            P("img", "seq", None),
            P("img", "seq", None),
            P("img"),
            P("img", None),
            P("img", None),
            P("img", None),
            P(),
            P(),
            P("img", None),
            P("img"),
            P("img", None),
            P("img", None),
            P(),
        ),
        check_vma=False,
    )
```

```python
import functools
import math

import jax
import jax.numpy as jnp
from jax import lax
from jax.experimental import pallas as pl
from jax.experimental.pallas import tpu as pltpu
from jax.sharding import PartitionSpec as P

SIDE = 32
EPS = 1e-06
FAR = -1e30
LANES = 128
BF = jnp.bfloat16
F32 = jnp.float32
VMEM_LIMIT = 56 * 2**20
QUERY_BLOCK = 512
FF_STEP = 512

RC = 2 * SIDE
KEY_MASK = RC
QUERY_MASK = KEY_MASK + 16
IMAGE_HOT = QUERY_MASK + 16
FEATURES = IMAGE_HOT + 16
ANYWHERE = pl.BlockSpec(memory_space=pl.ANY)


def dot(a, b, ca, cb):
    return lax.dot_general(a, b, (((ca,), (cb,)), ((), ())), preferred_element_type=F32)


def params(*semantics):
    return pltpu.CompilerParams(dimension_semantics=semantics, vmem_limit_bytes=VMEM_LIMIT)


CHEAP = pl.CostEstimate(flops=10**6, bytes_accessed=10**5, transcendentals=0)


def features_kernel(len_ref, turn_ref, base_ref, feat_ref, valid_ref, *, span):
    tokens = feat_ref.shape[1]

    def describe(shape, axis):
        index = lax.broadcasted_iota(jnp.int32, shape, axis)
        block = index // span
        pos = index - block * span
        for k in range(tokens // span):
            pos = pos + jnp.where(block == k, base_ref[k], 0)
        ends = []
        total = 0
        for j in range(4):
            total = total + len_ref[j]
            ends.append(total)
        segment = sum((pos >= ends[j]).astype(jnp.int32) for j in range(4))
        return pos, ends, segment

    pos, ends, segment = describe((1, tokens), 1)
    picked = jnp.minimum(segment, 3)
    begin = jnp.zeros_like(pos)
    length = jnp.zeros_like(pos)
    turn = jnp.zeros_like(pos)
    for j in range(4):
        here = picked == j
        begin = jnp.where(here, ends[j] - len_ref[j], begin)
        length = jnp.where(here, len_ref[j], length)
        turn = jnp.where(here, turn_ref[j], turn)
    full = length == SIDE * SIDE
    side = jnp.where(full, SIDE, SIDE // 2)
    u = pos - begin
    bits = SIDE.bit_length() - 1
    r0 = jnp.where(full, u >> bits, u >> (bits - 1))
    c0 = u & (side - 1)
    r1 = jnp.where((turn & 1) == 1, side - 1 - r0, r0)
    c1 = jnp.where(((turn >> 1) & 1) == 1, side - 1 - c0, c0)
    valid = pos < ends[3]
    row = jnp.where(valid, jnp.where(turn >= 4, c1, r1), 0)
    col = jnp.where(valid, jnp.where(turn >= 4, r1, c1), 0)
    which = lax.broadcasted_iota(jnp.int32, (SIDE, tokens), 0)
    few = lax.broadcasted_iota(jnp.int32, (16, tokens), 0)

    def put(start, value):
        feat_ref[start : start + value.shape[0], :] = value.astype(BF)

    put(0, jnp.where(which == row, 1.0, 0.0))
    put(SIDE, jnp.where(which == col, 1.0, 0.0))
    put(KEY_MASK, jnp.where(few == segment, 1.0, 0.0))
    put(QUERY_MASK, jnp.where((few < 5) & (few != segment), FAR, 0.0))
    put(IMAGE_HOT, jnp.where(few == picked, 1.0, 0.0))
    down_pos, down_ends, unused = describe(valid_ref.shape, 0)
    valid_ref[...] = jnp.where(down_pos < down_ends[3], 1.0, 0.0)


def token_features(lengths, turns, bases, span, mine):
    tokens = bases.shape[0] * span
    smem = pl.BlockSpec(memory_space=pltpu.SMEM)
    return pl.pallas_call(
        functools.partial(features_kernel, span=span),
        out_shape=(
            jax.ShapeDtypeStruct((FEATURES, tokens), BF),
            jax.ShapeDtypeStruct((mine, LANES), F32),
        ),
        in_specs=[smem, smem, smem],
        cost_estimate=CHEAP,
        name="token_features",
    )(lengths, turns, bases)


def window(cols):
    return -(-(cols + LANES // 2) // LANES) * LANES


def fetch(part, core, w_ref, room, sems, cols, dm):
    start = part * dm + (core * cols) // LANES * LANES
    start = pl.multiple_of(start, LANES)
    return pltpu.make_async_copy(
        w_ref.at[:, pl.ds(start, room.shape[2])], room.at[part], sems.at[part]
    )


def project_kernel(
    core_ref, a_ref, b_ref, c_ref, d_ref, gain_ref, time_ref, feat_ref, w_ref,
    in_ref, x_ref, qkv_ref, room, wide, sems, *, scale, cols,
):
    part = pl.program_id(0)
    core = core_ref[0]
    dm = in_ref.shape[1]
    width = qkv_ref.shape[2]

    @pl.when(part == 0)
    def _():
        for k in range(3):
            fetch(k, core, w_ref, room, sems, cols, dm).start()
        rows = a_ref.shape[0]
        x_ref[:rows, :] = a_ref[...]
        x_ref[rows:, :] = b_ref[...]
        for k, ref in enumerate((a_ref, b_ref, c_ref, d_ref)):
            x = ref[...].astype(F32)
            centre = x - jnp.mean(x, axis=-1, keepdims=True)
            spread = jnp.mean(centre * centre, axis=-1, keepdims=True)
            normed = centre * lax.rsqrt(spread + EPS) * gain_ref[...]
            in_ref[k * rows : (k + 1) * rows, :] = normed.astype(BF)

    fetch(part, core, w_ref, room, sems, cols, dm).wait()
    wide[...] = dot(room[part], in_ref[...], 0, 1)
    shift = core * cols - (core * cols) // LANES * LANES
    factor = jnp.where(part == 0, scale, 1.0)
    hot = feat_ref[IMAGE_HOT:, :].astype(F32)
    for h in range(cols // width):
        at = pl.multiple_of(shift + h * width, 8)
        x = wide[pl.ds(at, width), :]
        t = time_ref[0, h * width : (h + 1) * width, :]
        for j in range(4):
            x = x + t[:, j : j + 1] * hot[j : j + 1]
        qkv_ref[0, h] = (x * factor).astype(BF)


def project(core, blocks, gain, times, feats, w_qkv, scale, heads):
    rows, dm = blocks[0].shape
    tokens = 4 * rows
    cols = times.shape[1]
    width = cols // heads
    whole = lambda p, t: (0, 0)
    room = window(cols)
    return pl.pallas_call(
        functools.partial(project_kernel, scale=scale, cols=cols),
        grid_spec=pltpu.PrefetchScalarGridSpec(
            num_scalar_prefetch=1,
            grid=(3,),
            in_specs=[pl.BlockSpec((rows, dm), whole)] * 4
            + [
                pl.BlockSpec((1, dm), whole),
                pl.BlockSpec((1, cols, 4), lambda p, t: (p, 0, 0)),
                pl.BlockSpec(feats.shape, whole),
                ANYWHERE,
            ],
            out_specs=[
                pl.BlockSpec((tokens, dm), whole),
                pl.BlockSpec((2 * rows, dm), whole),
                pl.BlockSpec((1, heads, width, tokens), lambda p, t: (p, 0, 0, 0)),
            ],
            scratch_shapes=[
                pltpu.VMEM((3, dm, room), BF),
                pltpu.VMEM((room, tokens), F32),
                pltpu.SemaphoreType.DMA((3,)),
            ],
        ),
        out_shape=[
            jax.ShapeDtypeStruct((tokens, dm), BF),
            jax.ShapeDtypeStruct((2 * rows, dm), BF),
            jax.ShapeDtypeStruct((3, heads, width, tokens), BF),
        ],
        compiler_params=params("arbitrary"),
        cost_estimate=CHEAP,
        name="project",
    )(core, *blocks, gain, times, feats, w_qkv)


def weights_kernel(clock_ref, in_ref, d_ref, out_ref):
    d = jnp.concatenate([d_ref[0, h].astype(F32) for h in range(d_ref.shape[1])], axis=0)
    out_ref[0] = dot(in_ref[...], d.astype(BF), 0, 1).astype(BF)


def project_weights(clock, attn_in, d):
    parts, heads, width, tokens = d.shape
    dm = attn_in.shape[1]
    return pl.pallas_call(
        weights_kernel,
        grid_spec=pltpu.PrefetchScalarGridSpec(
            num_scalar_prefetch=1,
            grid=(parts,),
            in_specs=[
                pl.BlockSpec((tokens, dm), lambda p, t: (0, 0)),
                pl.BlockSpec((1, heads, width, tokens), lambda p, t: (p, 0, 0, 0)),
            ],
            out_specs=pl.BlockSpec((1, dm, heads * width), lambda p, t: (p, 0, 0)),
        ),
        out_shape=jax.ShapeDtypeStruct((parts, dm, heads * width), BF),
        compiler_params=params("arbitrary"),
        cost_estimate=CHEAP,
        name="project_weights",
    )(clock, attn_in, d)


def project_back_kernel(
    clock_ref, core_ref, d_ref, w_ref, mine_ref, far_ref, room, wide, total, sems, *, cols
):
    part = pl.program_id(0)
    core = core_ref[0]
    dm = w_ref.shape[0]
    width = d_ref.shape[2]

    @pl.when(part == 0)
    def _():
        for k in range(3):
            fetch(k, core, w_ref, room, sems, cols, dm).start()
        wide[...] = jnp.zeros_like(wide)

    shift = core * cols - (core * cols) // LANES * LANES
    for h in range(cols // width):
        at = pl.multiple_of(shift + h * width, 8)
        wide[pl.ds(at, width), :] = d_ref[0, h].astype(F32)
    fetch(part, core, w_ref, room, sems, cols, dm).wait()
    term = dot(wide[...].astype(BF), room[part], 0, 1)

    @pl.when(part == 0)
    def _():
        total[...] = term

    @pl.when(part == 1)
    def _():
        total[...] += term

    @pl.when(part == 2)
    def _():
        rows = mine_ref.shape[0]
        mine_ref[...] = total[:rows, :] + term[:rows]
        far_ref[...] = (total[rows:, :] + term[rows:]).astype(BF)


def project_back(clock, core, d, w_qkv, mine):
    parts, heads, width, tokens = d.shape
    dm = w_qkv.shape[0]
    cols = heads * width
    room = window(cols)
    whole = lambda p, t, u: (0, 0)
    return pl.pallas_call(
        functools.partial(project_back_kernel, cols=cols),
        grid_spec=pltpu.PrefetchScalarGridSpec(
            num_scalar_prefetch=2,
            grid=(parts,),
            in_specs=[
                pl.BlockSpec((1, heads, width, tokens), lambda p, t, u: (p, 0, 0, 0)),
                ANYWHERE,
            ],
            out_specs=[pl.BlockSpec((mine, dm), whole), pl.BlockSpec((tokens - mine, dm), whole)],
            scratch_shapes=[
                pltpu.VMEM((3, dm, room), BF),
                pltpu.VMEM((room, tokens), F32),
                pltpu.VMEM((tokens, dm), F32),
                pltpu.SemaphoreType.DMA((3,)),
            ],
        ),
        out_shape=[
            jax.ShapeDtypeStruct((mine, dm), F32),
            jax.ShapeDtypeStruct((tokens - mine, dm), BF),
        ],
        compiler_params=params("arbitrary"),
        cost_estimate=CHEAP,
        name="project_back",
    )(clock, core, d, w_qkv)


def query_block(b, bias, feat_ref, q):
    at = slice(b * QUERY_BLOCK, (b + 1) * QUERY_BLOCK)
    return jnp.concatenate([bias[:, at], feat_ref[QUERY_MASK:IMAGE_HOT, at], q[:, at]], axis=0)


def forward_kernel(clock_ref, p_ref, table_ref, feat_ref, o_ref, lse_ref):
    blocks = p_ref.shape[3] // QUERY_BLOCK
    q, k, v = (p_ref[p, 0] for p in range(3))
    bias = jnp.dot(table_ref[0], feat_ref[:RC], preferred_element_type=F32).astype(BF)
    key = jnp.concatenate([feat_ref[:QUERY_MASK], k], axis=0).T

    def scores(b):
        return jnp.dot(key, query_block(b, bias, feat_ref, q), preferred_element_type=F32)

    ahead = scores(0)
    for b in range(blocks):
        at = slice(b * QUERY_BLOCK, (b + 1) * QUERY_BLOCK)
        s = ahead
        top = jnp.max(s, axis=0, keepdims=True)
        if b + 1 < blocks:
            ahead = scores(b + 1)
        e = jnp.exp(s - top)
        total = jnp.sum(e, axis=0, keepdims=True)
        o = jnp.dot(v, e.astype(BF), preferred_element_type=F32) / total
        o_ref[0, :, at] = o.astype(BF)
        lse_ref[0, :, at] = top + jnp.log(total)


def attend_forward(clock, qkv, tables, feats, first, count):
    parts, heads, width, tokens = qkv.shape
    return pl.pallas_call(
        forward_kernel,
        grid_spec=pltpu.PrefetchScalarGridSpec(
            num_scalar_prefetch=1,
            grid=(count,),
            in_specs=[
                pl.BlockSpec((parts, 1, width, tokens), lambda h, t: (0, first + h, 0, 0)),
                pl.BlockSpec((1, RC, RC), lambda h, t: (first + h, 0, 0)),
                pl.BlockSpec(feats.shape, lambda h, t: (0, 0)),
            ],
            out_specs=[
                pl.BlockSpec((1, width, tokens), lambda h, t: (h, 0, 0)),
                pl.BlockSpec((1, 1, tokens), lambda h, t: (h, 0, 0)),
            ],
        ),
        out_shape=[
            jax.ShapeDtypeStruct((count, width, tokens), BF),
            jax.ShapeDtypeStruct((count, 1, tokens), F32),
        ],
        compiler_params=params("arbitrary"),
        cost_estimate=CHEAP,
        name="attention_forward",
    )(clock, qkv, tables, feats)


def backward_kernel(clock_ref, qkv_ref, o_ref, do_ref, lse_ref, table_ref, feat_ref, *rest, scale):
    d_ref, toe_ref, image_ref = rest[-3:]
    width = o_ref.shape[1]
    tokens = o_ref.shape[2]
    q, k, v = (qkv_ref[p, 0] for p in range(3))
    do = do_ref[0]
    delta = jnp.sum(do.astype(F32) * o_ref[0].astype(F32), axis=0, keepdims=True)
    rc = feat_ref[:RC]
    bias = jnp.dot(table_ref[0], rc, preferred_element_type=F32).astype(BF)
    key_t = jnp.concatenate([feat_ref[:QUERY_MASK], k], axis=0)
    key = key_t.T
    value = v.T
    dk = jnp.zeros((tokens, width), F32)
    dv = jnp.zeros((tokens, width), F32)
    dq_parts, bias_parts = [], []

    def first(b):
        at = slice(b * QUERY_BLOCK, (b + 1) * QUERY_BLOCK)
        s = jnp.dot(key, query_block(b, bias, feat_ref, q), preferred_element_type=F32)
        return s, jnp.dot(value, do[:, at], preferred_element_type=F32)

    ahead = first(0)
    for b in range(tokens // QUERY_BLOCK):
        at = slice(b * QUERY_BLOCK, (b + 1) * QUERY_BLOCK)
        s, dp = ahead
        p = jnp.exp(s - lse_ref[0, :, at])
        ds = (p * (dp - delta[:, at])).astype(BF)
        p = p.astype(BF)
        if (b + 1) * QUERY_BLOCK < tokens:
            ahead = first(b + 1)
        dq = jnp.dot(key_t, ds, preferred_element_type=F32)
        dq_parts.append((dq[QUERY_MASK:] * scale).astype(BF))
        bias_parts.append(dq[:RC].astype(BF))
        dk = dk + dot(ds, q[:, at], 1, 1)
        dv = dv + dot(p, do[:, at], 1, 1)
    toe = dot(rc, jnp.concatenate(bias_parts, axis=1), 1, 1)
    dq = jnp.concatenate(dq_parts, axis=1)
    dk = dk.T.astype(BF)
    dv = dv.T.astype(BF)
    d_ref[0, 0] = dq
    d_ref[1, 0] = dk
    d_ref[2, 0] = dv
    toe_ref[0] = toe
    hot = feat_ref[IMAGE_HOT:]
    image_ref[0, 0] = dot(hot, dq, 1, 1)
    image_ref[1, 0] = dot(hot, dv, 1, 1)


def attend_backward(clock, qkv, o, do, lse, tables, feats, scale, first, count, before):
    parts, heads, width, tokens = qkv.shape
    head3 = lambda h, t: (first + h, 0, 0)
    head4 = lambda h, t: (0, first + h, 0, 0)
    return pl.pallas_call(
        functools.partial(backward_kernel, scale=scale),
        grid_spec=pltpu.PrefetchScalarGridSpec(
            num_scalar_prefetch=1,
            grid=(count,),
            in_specs=[
                pl.BlockSpec((parts, 1, width, tokens), head4),
                pl.BlockSpec((1, width, tokens), head3),
                pl.BlockSpec((1, width, tokens), head3),
                pl.BlockSpec((1, 1, tokens), head3),
                pl.BlockSpec((1, RC, RC), head3),
                pl.BlockSpec(feats.shape, lambda h, t: (0, 0)),
            ]
            + [ANYWHERE] * len(before),
            out_specs=[
                pl.BlockSpec((parts, 1, width, tokens), head4),
                pl.BlockSpec((1, RC, RC), head3),
                pl.BlockSpec((2, 1, 16, width), head4),
            ],
        ),
        out_shape=[
            jax.ShapeDtypeStruct((parts, heads, width, tokens), BF),
            jax.ShapeDtypeStruct((heads, RC, RC), F32),
            jax.ShapeDtypeStruct((2, heads, 16, width), F32),
        ],
        input_output_aliases={7 + k: k for k in range(len(before))},
        compiler_params=params("arbitrary"),
        cost_estimate=CHEAP,
        name="attention_backward",
    )(clock, qkv, o, do, lse, tables, feats, *before)


def rise_kernel(
    m_ref, near_ref, far_ref, valid_ref, up_ref, down_ref,
    two_ref, slope_ref, wd_ref, mt_ref, g_ref,
):
    @pl.when(pl.program_id(0) == 0)
    def _():
        two_ref[...] = jnp.zeros_like(two_ref)
        mt_ref[...] = m_ref[...].T
        half = near_ref.shape[0]
        g_ref[:half, :] = (near_ref[...].astype(F32) * valid_ref[:half, :1]).astype(BF)
        g_ref[half:, :] = (far_ref[...].astype(F32) * valid_ref[half:, :1]).astype(BF)

    def up_of(j):
        return jnp.dot(m_ref[...], up_ref[:, j : j + FF_STEP], preferred_element_type=F32)

    acts = []
    tile = up_ref.shape[1]
    ahead = up_of(0)
    for j in range(0, tile, FF_STEP):
        at = slice(j, j + FF_STEP)
        up = ahead
        if j + FF_STEP < tile:
            ahead = up_of(j + FF_STEP)
        half = 0.5 + 0.5 * lax.erf(up * math.sqrt(0.5))
        slope = half + up * (jnp.exp(-0.5 * up * up) * (1.0 / math.sqrt(2.0 * math.pi)))
        slope_ref[:, at] = slope.astype(BF)
        acts.append((up * half).astype(BF))
    act = jnp.concatenate(acts, axis=1)
    wd_ref[...] = dot(act, g_ref[...], 0, 0).astype(BF)
    two_ref[...] += jnp.dot(act, down_ref[...], preferred_element_type=F32)


def mlp_rise(m, near, far, valid, w_up, w_down, tile):
    rows, dm = m.shape
    ff = w_up.shape[1]
    whole = lambda i: (0, 0)
    return pl.pallas_call(
        rise_kernel,
        grid=(ff // tile,),
        in_specs=[
            pl.BlockSpec((rows, dm), whole),
            pl.BlockSpec(near.shape, whole),
            pl.BlockSpec(far.shape, whole),
            pl.BlockSpec(valid.shape, whole),
            pl.BlockSpec((dm, tile), lambda i: (0, i)),
            pl.BlockSpec((tile, dm), lambda i: (i, 0)),
        ],
        out_specs=[
            pl.BlockSpec((rows, dm), whole),
            pl.BlockSpec((rows, tile), lambda i: (0, i)),
            pl.BlockSpec((tile, dm), lambda i: (i, 0)),
            pl.BlockSpec((dm, rows), whole),
            pl.BlockSpec((rows, dm), whole),
        ],
        out_shape=[
            jax.ShapeDtypeStruct((rows, dm), F32),
            jax.ShapeDtypeStruct((rows, ff), BF),
            jax.ShapeDtypeStruct((ff, dm), BF),
            jax.ShapeDtypeStruct((dm, rows), BF),
            jax.ShapeDtypeStruct((rows, dm), BF),
        ],
        compiler_params=params("arbitrary"),
        cost_estimate=CHEAP,
        name="feed_forward_rise",
    )(m, near, far, valid, w_up, w_down)


def fall_kernel(clock_ref, tile_ref, mt_ref, g_ref, up_ref, down_ref, slope_ref, *rest):
    gm_out, send_ref, own_ref = rest[-3:]
    step = pl.program_id(0)

    @pl.when(step == 0)
    def _():
        gm_out[...] = rest[0][...] if len(rest) > 3 else jnp.zeros_like(gm_out)

    du = (dot(g_ref[...], down_ref[...], 1, 1) * slope_ref[...].astype(F32)).astype(BF)
    gm_out[...] += dot(du, up_ref[...], 1, 1)
    wu = jnp.dot(mt_ref[...], du, preferred_element_type=F32).astype(BF)

    @pl.when(step % 2 == 0)
    def _():
        send_ref[...] = wu

    @pl.when(step % 2 == 1)
    def _():
        own_ref[...] = wu


def mlp_fall(clock, tiles, mt, g, w_up, w_down, slope, tile, first, pairs, before):
    dm, rows = mt.shape
    ff = w_up.shape[1]
    whole = lambda i, u, t: (0, 0)
    column = lambda i, u, t: (0, first + i // 2)
    at = lambda i, t: 2 * (first + i // 2) + t[i % 2]
    return pl.pallas_call(
        fall_kernel,
        grid_spec=pltpu.PrefetchScalarGridSpec(
            num_scalar_prefetch=2,
            grid=(2 * pairs,),
            in_specs=[
                pl.BlockSpec((dm, rows), whole),
                pl.BlockSpec((rows, dm), whole),
                pl.BlockSpec((dm, tile), lambda i, u, t: (0, at(i, t))),
                pl.BlockSpec((tile, dm), lambda i, u, t: (at(i, t), 0)),
                pl.BlockSpec((rows, tile), lambda i, u, t: (0, at(i, t))),
            ]
            + ([pl.BlockSpec((rows, dm), whole), ANYWHERE, ANYWHERE] if before else []),
            out_specs=[
                pl.BlockSpec((rows, dm), whole),
                pl.BlockSpec((dm, tile), column),
                pl.BlockSpec((dm, tile), column),
            ],
        ),
        out_shape=[
            jax.ShapeDtypeStruct((rows, dm), F32),
            jax.ShapeDtypeStruct((dm, ff // 2), BF),
            jax.ShapeDtypeStruct((dm, ff // 2), BF),
        ],
        input_output_aliases={8: 1, 9: 2} if before else {},
        compiler_params=params("arbitrary"),
        cost_estimate=CHEAP,
        name="feed_forward_fall",
    )(clock, tiles, mt, g, w_up, w_down, slope, *before)


def moments(x):
    centre = x - jnp.mean(x, axis=-1, keepdims=True)
    root = lax.rsqrt(jnp.mean(centre * centre, axis=-1, keepdims=True) + EPS)
    return centre * root, root


def norm_backward(d, n, root):
    return root * (
        d - jnp.mean(d, axis=-1, keepdims=True) - n * jnp.mean(d * n, axis=-1, keepdims=True)
    )


def columns(x):
    return jnp.sum(x, axis=0, keepdims=True)


def middle_kernel(
    clock_ref, gm_ref, two_ref, one_ref, h_ref, g_ref, valid_ref, gain_ref,
    out_ref, grad_ref, low_ref, sums_ref,
):
    @pl.when(pl.program_id(0) == 0)
    def _():
        sums_ref[...] = jnp.zeros_like(sums_ref)

    valid = valid_ref[:, :1]
    two, one, h = two_ref[...], one_ref[...], h_ref[...]
    h2 = h + two
    out_ref[...] = (h2 * valid).astype(BF)
    n, root = moments(h)
    gm = gm_ref[...]
    grad = g_ref[...].astype(F32) + norm_backward(gm * gain_ref[...], n, root)
    grad_ref[...] = grad
    low_ref[...] = grad.astype(BF)
    sums_ref[0:1, :] += columns(gm * n)
    sums_ref[1:2, :] += columns(valid * h2 * h2)
    sums_ref[2:3, :] += columns(valid * one * one)
    sums_ref[3:4, :] += columns(valid * two * two)


def middle(clock, gm, two, one, hidden, grads, valid, gain):
    rows, dm = gm.shape
    step = rows // 4
    block = pl.BlockSpec((step, dm), lambda i, t: (i, 0))
    return pl.pallas_call(
        middle_kernel,
        grid_spec=pltpu.PrefetchScalarGridSpec(
            num_scalar_prefetch=1,
            grid=(4,),
            in_specs=[block] * 5
            + [
                pl.BlockSpec((step, LANES), lambda i, t: (i, 0)),
                pl.BlockSpec((1, dm), lambda i, t: (0, 0)),
            ],
            out_specs=[block, block, block, pl.BlockSpec((8, dm), lambda i, t: (0, 0))],
        ),
        out_shape=[
            jax.ShapeDtypeStruct((rows, dm), BF),
            jax.ShapeDtypeStruct((rows, dm), F32),
            jax.ShapeDtypeStruct((rows, dm), BF),
            jax.ShapeDtypeStruct((8, dm), F32),
        ],
        compiler_params=params("arbitrary"),
        cost_estimate=CHEAP,
        name="middle",
    )(clock, gm, two, one, hidden, grads, valid, gain)


def last_kernel(back_ref, far_ref, x_ref, grad_ref, gain_ref, out_ref, sums_ref):
    @pl.when(pl.program_id(0) == 0)
    def _():
        sums_ref[...] = jnp.zeros_like(sums_ref)

    back = back_ref[...] + far_ref[...].astype(F32)
    n, root = moments(x_ref[...].astype(F32))
    out_ref[...] = (grad_ref[...] + norm_backward(back * gain_ref[...], n, root)).astype(BF)
    sums_ref[0:1, :] += columns(back * n)


def last(back, far, x, grad, gain):
    rows, dm = back.shape
    step = rows // 4
    block = pl.BlockSpec((step, dm), lambda i: (i, 0))
    return pl.pallas_call(
        last_kernel,
        grid=(4,),
        in_specs=[block] * 4 + [pl.BlockSpec((1, dm), lambda i: (0, 0))],
        out_specs=[block, pl.BlockSpec((8, dm), lambda i: (0, 0))],
        out_shape=[jax.ShapeDtypeStruct((rows, dm), BF), jax.ShapeDtypeStruct((8, dm), F32)],
        compiler_params=params("arbitrary"),
        cost_estimate=CHEAP,
        name="last",
    )(back, far, x, grad, gain)


class Halving:
    def __init__(self, names, dims, base, piece, prefix=(), suffix=(), column=0):
        self.names, self.dims, self.base, self.piece = names, dims, base, piece
        self.prefix, self.suffix, self.column = prefix, suffix, column
        self.stage, self.arrived, self.result = 0, [], None

    def left(self, stage):
        return [d for d in self.names if d in self.dims[stage + 1 :]]

    def specs(self, gridded):
        stage = self.stage
        open_dims = self.left(stage)

        def index(names, prefix, suffix, column):
            def at(*grid):
                t = grid[-1]
                out = list(prefix)
                for d in names:
                    if d in gridded:
                        out.append(grid[gridded.index(d)])
                    elif d in open_dims:
                        out.append(0)
                    elif stage < len(self.dims) and d == self.dims[stage]:
                        out.append(1 - t[d])
                    else:
                        out.append(t[d])
                return tuple(out) + tuple(suffix) + (0, column)

            return at

        def block(names, prefix, suffix):
            sizes = [2 if d in open_dims and d not in gridded else None for d in names]
            return (None,) * len(prefix) + tuple(sizes) + (None,) * len(suffix) + self.piece

        arrays, specs = [], []
        for array in self.base:
            arrays.append(array)
            specs.append(
                pl.BlockSpec(
                    block(self.names, self.prefix, self.suffix),
                    index(self.names, self.prefix, self.suffix, self.column),
                )
            )
        for s, (array, place) in enumerate(self.arrived):
            arrays.append(array)
            names = self.left(s)
            specs.append(pl.BlockSpec(block(names, (place,), ()), index(names, (place,), (), 0)))
        rest = index(open_dims, (), (), 0)
        inner = tuple(2 if d not in gridded else None for d in open_dims) + self.piece
        return arrays, specs, inner, rest, (2,) * len(open_dims) + self.piece


def sum_kernel(coord_ref, *refs, counts, places):
    outs = refs[sum(counts) :]
    at = 0
    for (out, place), count in zip(places, counts):
        total = refs[at][...].astype(F32)
        for k in range(1, count):
            total = total + refs[at + k][...].astype(F32)
        outs[out][place] = total.astype(BF)
        at += count


def advance(clock, swaps, jobs):
    arrays, in_specs, counts, groups, places = [], [], [], [], []
    stage = jobs[0].stage
    steps = min(2, max(0, len(jobs[0].left(stage)) - 1))
    for job in jobs:
        some, their, inner, rest, shape = job.specs(job.left(stage)[:steps])
        arrays, in_specs = arrays + some, in_specs + their
        counts.append(len(some))
        sent = job.dims[stage] if stage < len(job.dims) else None
        key = (sent, shape)
        found = [k for k, g in enumerate(groups) if g[0] == key]
        if not found:
            groups.append((key, inner, rest, []))
        group = found[0] if found else len(groups) - 1
        places.append((group, len(groups[group][3])))
        groups[group][3].append(job)
    out_specs = [
        pl.BlockSpec((len(g[3]),) + g[1], lambda *grid, f=g[2]: (0,) + f(*grid)) for g in groups
    ]
    sums = pl.pallas_call(
        functools.partial(sum_kernel, counts=counts, places=places),
        grid_spec=pltpu.PrefetchScalarGridSpec(
            num_scalar_prefetch=1,
            grid=(2,) * steps if steps else (1,),
            in_specs=in_specs,
            out_specs=out_specs,
        ),
        out_shape=[jax.ShapeDtypeStruct((len(g[3]),) + g[0][1], BF) for g in groups],
        compiler_params=params(*("arbitrary",) * max(steps, 1)),
        cost_estimate=CHEAP,
        name="sum_pieces",
    )(clock.now, *arrays)
    for (key, inner, rest, members), total in zip(groups, sums):
        if key[0] is not None:
            total = swaps[key[0]](total)
        for k, job in enumerate(members):
            if key[0] is None:
                job.result = total[k]
            else:
                job.arrived.append((total, k))
                job.stage += 1
    clock.passed(*sums)


class Clock:
    def __init__(self, now):
        self.now = now

    def passed(self, *results):
        self.now = lax.optimization_barrier((self.now, *results))[0]

    def tie(self, x):
        return lax.optimization_barrier((x, self.now))[0]


class Gather:
    def __init__(self, clock, part, swaps):
        self.clock, self.part, self.swaps, self.far = clock, part, list(swaps), None

    def land(self):
        if self.far is not None:
            bit, axis = self.put
            low, high = jnp.where(bit, self.far, self.part), jnp.where(bit, self.part, self.far)
            self.part = jnp.concatenate([low, high], axis=axis)
            self.clock.passed(self.part)
            self.far = None

    def tick(self):
        self.land()
        if self.swaps:
            swap, bit, axis = self.swaps.pop(0)
            self.put = (bit, axis)
            self.far = swap(self.clock.tie(self.part))

    def finish(self):
        while self.far is not None or self.swaps:
            self.tick()
        return self.part


class Total:
    def __init__(self, clock, part, swaps):
        self.clock, self.part, self.swaps, self.far = clock, part, list(swaps), None

    def tick(self):
        if self.far is not None:
            self.part = self.part + self.far
            self.clock.passed(self.part)
            self.far = None
        if self.swaps:
            self.far = self.swaps.pop(0)(self.clock.tie(self.part))

    def finish(self):
        while self.far is not None or self.swaps:
            self.tick()
        return self.part


def pick(array, index, axis=0):
    return lax.dynamic_index_in_dim(array, index, axis, keepdims=False)


def toeplitz_tables(rel, count):
    d = jnp.arange(2 * count - 1, dtype=jnp.int32)
    t = jnp.arange(count, dtype=jnp.int32)
    hot = (d[:, None, None] == t[None, None, :] - t[None, :, None] + count - 1).astype(BF)
    return jnp.einsum("hd,dtr->htr", rel.astype(BF), hot, preferred_element_type=F32)


def per_device(
    tokens, time_embed, image_lengths, grid_turns, ln1_gain, w_qkv, w_time_q, time_value_weight,
    rel_rows, rel_cols, output_projection_weight, ln2_gain, w_up, w_down, out_grad,
):
    slots, span, dm = tokens.shape
    heads = rel_rows.shape[0]
    width = dm // heads
    ff = w_up.shape[1]
    scale = width ** (-0.5)
    n_seq = lax.axis_size("seq")
    n_img = lax.axis_size("img")
    cores = n_seq // slots
    own_heads = heads // cores
    cols = own_heads * width
    me_img = lax.axis_index("img")
    me_seq = lax.axis_index("seq")
    y = me_seq // cores
    c = me_seq % cores
    mine = slots * span
    rows = dm // n_img
    over_y = [(s, (slots - 1 - s // cores) * cores + s % cores) for s in range(n_seq)]
    over_core = [(s, s // cores * cores + cores - 1 - s % cores) for s in range(n_seq)]

    def swap_y(a):
        return lax.ppermute(a, "seq", over_y)

    def swap_core(a):
        return lax.ppermute(a, "seq", over_core)

    bits = n_img.bit_length() - 1
    on_y, on_core = bits, bits + 1
    swaps = {
        k: functools.partial(
            lax.ppermute, axis_name="img", perm=[(i, i ^ (1 << k)) for i in range(n_img)]
        )
        for k in range(bits)
    }
    swaps[on_y], swaps[on_core] = swap_y, swap_core

    def across_y(parts):
        part = jnp.concatenate(parts, axis=1)
        return part, swap_y(part)

    def across_core(part, far):
        part = jnp.concatenate([jnp.where(y == 0, part, far), jnp.where(y == 0, far, part)], axis=0)
        return part, swap_core(part)

    def both_cores(part, far):
        return jnp.where(c == 0, part, far).astype(F32), jnp.where(c == 0, far, part).astype(F32)

    def order(*first):
        return list(first) + [k for k in range(bits) if k not in first]

    tok_own = pick(tokens, y)
    tok_rx = swap_y(pick(tokens, 1 - y))
    tok_own_far = swap_core(tok_own)
    block = lambda yy, cc: (yy * cores + cc) * span
    bases = jnp.stack([block(y, c), block(1 - y, c), block(y, 1 - c), block(1 - y, 1 - c)])
    feats, valid = token_features(
        pick(image_lengths, y), pick(grid_turns, y), bases.astype(jnp.int32), span, mine
    )
    coords = jnp.stack([(me_img >> k) & 1 for k in range(bits)] + [y, c]).astype(jnp.int32)
    core = c.astype(jnp.int32).reshape(1)
    pair = jnp.stack([1 - c, c]).astype(jnp.int32)
    te = pick(time_embed, y)

    def time_terms(w):
        all_heads = dot(te, w, 1, 0)
        return lax.dynamic_slice_in_dim(all_heads, c * cols, cols, 1).T

    time_q = time_terms(w_time_q)
    times = jnp.stack([time_q, jnp.zeros_like(time_q), time_terms(time_value_weight)])
    row_table = toeplitz_tables(lax.dynamic_slice_in_dim(rel_rows, c * own_heads, own_heads), SIDE)
    col_table = toeplitz_tables(lax.dynamic_slice_in_dim(rel_cols, c * own_heads, own_heads), SIDE)
    gap = jnp.zeros_like(row_table)
    tables = jnp.concatenate(
        [
            jnp.concatenate([row_table, gap], axis=2),
            jnp.concatenate([gap, col_table], axis=2),
        ],
        axis=1,
    ).astype(BF)
    ln1_row, ln2_row = ln1_gain.reshape(1, dm), ln2_gain.reshape(1, dm)
    grad_out = pick(out_grad, 1 - y)
    grad_own = pick(out_grad, y)

    img_bits = [((me_img >> k) & 1) == 1 for k in range(bits)]
    clock = Clock(coords)
    clock.passed(feats, times, tables, core, pair, grad_out, grad_own, ln1_row, ln2_row)
    tok_rx = clock.tie(tok_rx)
    grad_rx = swap_y(lax.optimization_barrier((grad_out, tok_rx))[0])
    attn_in, x, qkv = project(
        core, (tok_own, tok_rx, tok_own_far, swap_core(tok_rx)), ln1_row, times, feats, w_qkv,
        scale, own_heads,
    )
    clock.passed(qkv)
    half_heads = own_heads // 2
    o_a, lse_a = attend_forward(clock.now, qkv, tables, feats, 0, half_heads)
    clock.passed(o_a, grad_rx)
    far_a = swap_core(o_a)
    o_b, lse_b = attend_forward(clock.now, qkv, tables, feats, half_heads, half_heads)
    far_b = swap_core(o_b)

    o_own = jnp.concatenate([o_a, o_b], axis=0)
    lse = jnp.concatenate([lse_a, lse_b], axis=0)
    clock.passed(o_b)

    def turned(a):
        a = a.reshape(cols // 2, 2 * mine)
        return jnp.concatenate([a[:, mine:], a[:, :mine]], axis=1)

    o_flat = o_own.reshape(cols, 2 * mine)
    o_far = jnp.concatenate([turned(far_a), turned(far_b)], axis=0)
    attn_all = jnp.concatenate(
        [jnp.where(c == 0, o_flat, o_far), jnp.where(c == 0, o_far, o_flat)], axis=0
    )
    branch_one = dot(attn_all[:, :mine], output_projection_weight, 0, 0)
    hidden_one = x.astype(F32) + branch_one
    mlp_in = clock.tie((moments(hidden_one)[0] * ln2_gain).astype(BF))

    tile = ff // 6
    two, slope, down, mlp_in_t, grad_branch = mlp_rise(
        mlp_in, grad_own, grad_rx, valid, w_up, w_down, ff // 3
    )
    clock.passed(two)
    down = lax.psum_scatter(down, ("img", "seq"), scatter_dimension=0, tiled=True)
    img_names = list(range(bits))[::-1]
    twos = (2,) * bits
    step = functools.partial(advance, clock, swaps)

    def finish(jobs):
        while jobs[0].result is None:
            step(jobs)

    gm, send, own = mlp_fall(
        clock.now, pair, mlp_in_t, grad_branch, w_up, w_down, slope, tile, 0, 3, ()
    )
    clock.passed(gm)
    output, grad_one, gb_mine, sums = middle(
        clock.now, gm, two, branch_one, hidden_one, grad_branch, valid, ln2_row
    )
    clock.passed(output)
    gb_far = swap_core(gb_mine)
    far_up = swap_core(lax.optimization_barrier((send, gb_far))[0])
    gb_all = jnp.concatenate([gb_mine, gb_far], axis=0)
    out_far = swap_y(output[span:])
    w_proj_rows = lax.dynamic_slice_in_dim(output_projection_weight, c * cols, cols, 0)
    do = dot(w_proj_rows, gb_all, 1, 1).astype(BF).reshape(own_heads, width, 2 * mine)
    gb_cols = lax.dynamic_slice_in_dim(gb_all, c * cols, cols, 1)
    proj_part = dot(attn_all, gb_cols, 1, 0).astype(BF)
    clock.passed(do, proj_part)

    def by_row(dims, arrays, columns_of, column=0, prefix=()):
        shape = twos + (2, rows // 2)
        return Halving(
            img_names + [on_y],
            dims,
            [a.reshape(a.shape[: len(prefix)] + shape + a.shape[-1:]) for a in arrays],
            (rows // 2, columns_of),
            prefix=prefix,
            column=column,
        )

    orders = [order(0, on_y, 1), order(on_y, 1, 0), order(1, 0, on_y)]
    up_half = ff // 4
    jobs_up = [
        by_row(dims, (own, far_up), up_half, k)
        for k, dims in enumerate([order(0, 1, on_y), order(on_y, 0, 1)])
    ]
    job_proj = by_row(orders[2], (proj_part,), cols)
    clock.passed(out_far)
    step(jobs_up + [job_proj])
    grads = attend_backward(
        clock.now, qkv, o_own, do, lse, tables, feats, scale, 0, own_heads, ()
    )
    d, toe, image_grads = grads
    clock.passed(d)
    step(jobs_up)
    part = jnp.transpose(image_grads[:, :, :4], (0, 2, 1, 3)).reshape(8, cols).astype(BF)
    gather = Gather(
        clock,
        part[None, None],
        [(swap_core, c == 1, 3), (swap_y, y == 1, 1)]
        + [(swaps[k], img_bits[k], 0) for k in range(bits)],
    )
    gather.tick()
    w_part = project_weights(clock.now, attn_in, d)
    clock.passed(w_part, job_proj.arrived[0][0])
    gather.land()
    gather.part = jnp.concatenate([gather.part, te[None, None]], axis=2)
    jobs_qkv = [by_row(dims, (w_part,), cols, prefix=(p,)) for p, dims in enumerate(orders)]
    step(jobs_qkv)
    jobs_qkv.append(job_proj)
    gather.tick()
    back, back_far = project_back(clock.now, core, d, w_qkv, mine)
    clock.passed(back)
    step(jobs_up)
    back_far = swap_core(clock.tie(back_far))
    step(jobs_qkv)
    clock.passed(down)
    down_far = swap_y(clock.tie(down))
    input_grad, sums_one = last(back, back_far, x, grad_one, ln1_row)
    clock.passed(input_grad)
    reach = jnp.arange(2 * SIDE - 1, dtype=jnp.int32)
    side = jnp.arange(SIDE, dtype=jnp.int32)
    diag = (reach == side[:, None, None] - side[None, :, None] + SIDE - 1).astype(F32)
    rel = jnp.stack([toe[:, :SIDE, :SIDE], toe[:, SIDE:, SIDE:]])
    rel = jnp.einsum("khrt,rtd->khd", rel, diag, precision=lax.Precision.HIGHEST)
    rel_all = lax.dynamic_update_slice(
        jnp.zeros((2, heads, 2 * SIDE - 1), F32), rel, (0, c * own_heads, 0)
    )
    stats = jnp.concatenate([jnp.sum(sums[1:4], axis=1), jnp.sum(valid[:, 0])[None]])
    small = jnp.concatenate([sums_one[0], sums[0], rel_all.reshape(-1), stats])
    def returned(own_rows, far_rows):
        return jnp.stack(
            [jnp.where(y == 0, own_rows, far_rows), jnp.where(y == 0, far_rows, own_rows)]
        )

    small = Total(clock, small, [swap_core, swap_y] + [swaps[k] for k in range(bits)])

    small.tick()
    step(jobs_qkv)
    gather.tick()
    down = jnp.where(y == 0, jnp.stack([down, down_far]), jnp.stack([down_far, down]))
    output = returned(output[:span], out_far)
    in_far = swap_y(clock.tie(input_grad)[span:])
    clock.passed(output)
    step(jobs_up)
    small.tick()
    gather.tick()
    down_far = swap_core(down)
    step(jobs_qkv)
    small.tick()
    gather.tick()
    h0, h1 = both_cores(down, down_far)
    w_down_grad = jnp.concatenate([h0[0], h1[0], h0[1], h1[1]], axis=0)
    clock.passed(w_down_grad)
    finish(jobs_up)
    up_parts, up_far = across_y([clock.tie(job.result) for job in jobs_up])
    finish(jobs_qkv)
    qkv_parts, qkv_far = across_y([job.result for job in jobs_qkv])
    small.tick()
    gather.tick()
    clock.passed(qkv_far, up_far)
    qkv_part, qkv_far = across_core(qkv_parts, clock.tie(qkv_far))
    up_part, up_far = across_core(up_parts, clock.tie(up_far))
    clock.passed(in_far)
    in_far = clock.tie(in_far)
    small.tick()
    gather.tick()
    u0, u1 = both_cores(up_part, up_far)
    w_up_grad = jnp.concatenate(
        [u[:, k * tile : (k + 1) * tile] for k in range(3) for u in (u0, u1)], axis=1
    )
    clock.passed(w_up_grad)
    small = small.finish()
    factors = gather.finish().reshape(n_img * slots, 12, dm)

    te_rows = lax.dynamic_slice_in_dim(factors[:, 8:], me_img * rows, rows, 2)
    w_time_q_grad, w_time_v_grad = (
        lax.dot_general(
            te_rows.reshape(-1, rows),
            factors[:, 4 * k : 4 * k + 4].reshape(-1, dm),
            (((0,), (0,)), ((), ())),
            preferred_element_type=F32,
        )
        for k in range(2)
    )
    ln1_gain_grad = lax.dynamic_slice_in_dim(small, me_img * rows, rows)
    ln2_gain_grad = lax.dynamic_slice_in_dim(small, dm + me_img * rows, rows)
    rel_all = small[2 * dm : -4].reshape(2, heads, 2 * SIDE - 1)
    rms_values = jnp.sqrt(small[-4:-1] / (small[-1] * dm))
    q0, q1 = both_cores(qkv_part, qkv_far)
    w_proj_grad = jnp.concatenate([q[:, 3 * cols :] for q in (q0, q1)], axis=1)
    w_qkv_grad = jnp.concatenate(
        [q[:, p * cols : (p + 1) * cols] for p in range(3) for q in (q0, q1)], axis=1
    )

    return (
        output,
        returned(input_grad[:span], in_far),
        ln1_gain_grad,
        w_qkv_grad,
        w_time_q_grad,
        w_time_v_grad,
        rel_all[0],
        rel_all[1],
        w_proj_grad,
        ln2_gain_grad,
        w_up_grad,
        w_down_grad,
        rms_values,
    )


def solution(mesh):
    return jax.shard_map(
        per_device,
        mesh=mesh,
        in_specs=(
            P("img", "seq", None),
            P("img", None, None),
            P("img", None),
            P("img", None),
        )
        + (P(),) * 10
        + (P("img", "seq", None),),
        out_specs=(
            P("img", "seq", None),
            P("img", "seq", None),
            P("img"),
            P("img", None),
            P("img", None),
            P("img", None),
            P(),
            P(),
            P("img", None),
            P("img"),
            P("img", None),
            P("img", None),
            P(),
        ),
        check_vma=False,
    )
```

```python
import functools
import math

import jax
import jax.numpy as jnp
from jax import lax
from jax.experimental import pallas as pl
from jax.experimental.pallas import tpu as pltpu
from jax.sharding import PartitionSpec as P

SIDE = 32
EPS = 1e-06
FAR = -1e30
LANES = 128
BF = jnp.bfloat16
F32 = jnp.float32
VMEM_LIMIT = 56 * 2**20
QUERY_BLOCK = 512
FF_STEP = 512

RC = 2 * SIDE
KEY_MASK = RC
QUERY_MASK = KEY_MASK + 16
IMAGE_HOT = QUERY_MASK + 16
FEATURES = IMAGE_HOT + 16
ANYWHERE = pl.BlockSpec(memory_space=pl.ANY)


def dot(a, b, ca, cb):
    return lax.dot_general(a, b, (((ca,), (cb,)), ((), ())), preferred_element_type=F32)


def params(*semantics):
    return pltpu.CompilerParams(dimension_semantics=semantics, vmem_limit_bytes=VMEM_LIMIT)


CHEAP = pl.CostEstimate(flops=10**6, bytes_accessed=10**5, transcendentals=0)


def features_kernel(len_ref, turn_ref, base_ref, feat_ref, valid_ref, *, span):
    tokens = feat_ref.shape[1]

    def describe(shape, axis):
        index = lax.broadcasted_iota(jnp.int32, shape, axis)
        block = index // span
        pos = index - block * span
        for k in range(tokens // span):
            pos = pos + jnp.where(block == k, base_ref[k], 0)
        ends = []
        total = 0
        for j in range(4):
            total = total + len_ref[j]
            ends.append(total)
        segment = sum((pos >= ends[j]).astype(jnp.int32) for j in range(4))
        return pos, ends, segment

    pos, ends, segment = describe((1, tokens), 1)
    picked = jnp.minimum(segment, 3)
    begin = jnp.zeros_like(pos)
    length = jnp.zeros_like(pos)
    turn = jnp.zeros_like(pos)
    for j in range(4):
        here = picked == j
        begin = jnp.where(here, ends[j] - len_ref[j], begin)
        length = jnp.where(here, len_ref[j], length)
        turn = jnp.where(here, turn_ref[j], turn)
    full = length == SIDE * SIDE
    side = jnp.where(full, SIDE, SIDE // 2)
    u = pos - begin
    bits = SIDE.bit_length() - 1
    r0 = jnp.where(full, u >> bits, u >> (bits - 1))
    c0 = u & (side - 1)
    r1 = jnp.where((turn & 1) == 1, side - 1 - r0, r0)
    c1 = jnp.where(((turn >> 1) & 1) == 1, side - 1 - c0, c0)
    valid = pos < ends[3]
    row = jnp.where(valid, jnp.where(turn >= 4, c1, r1), 0)
    col = jnp.where(valid, jnp.where(turn >= 4, r1, c1), 0)
    which = lax.broadcasted_iota(jnp.int32, (SIDE, tokens), 0)
    few = lax.broadcasted_iota(jnp.int32, (16, tokens), 0)

    def put(start, value):
        feat_ref[start : start + value.shape[0], :] = value.astype(BF)

    put(0, jnp.where(which == row, 1.0, 0.0))
    put(SIDE, jnp.where(which == col, 1.0, 0.0))
    put(KEY_MASK, jnp.where(few == segment, 1.0, 0.0))
    put(QUERY_MASK, jnp.where((few < 5) & (few != segment), FAR, 0.0))
    put(IMAGE_HOT, jnp.where(few == picked, 1.0, 0.0))
    down_pos, down_ends, unused = describe(valid_ref.shape, 0)
    valid_ref[...] = jnp.where(down_pos < down_ends[3], 1.0, 0.0)


def token_features(lengths, turns, bases, span, mine):
    tokens = bases.shape[0] * span
    smem = pl.BlockSpec(memory_space=pltpu.SMEM)
    return pl.pallas_call(
        functools.partial(features_kernel, span=span),
        out_shape=(
            jax.ShapeDtypeStruct((FEATURES, tokens), BF),
            jax.ShapeDtypeStruct((mine, LANES), F32),
        ),
        in_specs=[smem, smem, smem],
        cost_estimate=CHEAP,
        name="token_features",
    )(lengths, turns, bases)


def window(cols):
    return -(-(cols + LANES // 2) // LANES) * LANES


def fetch(part, core, w_ref, room, sems, cols, dm):
    start = part * dm + (core * cols) // LANES * LANES
    start = pl.multiple_of(start, LANES)
    return pltpu.make_async_copy(
        w_ref.at[:, pl.ds(start, room.shape[2])], room.at[part], sems.at[part]
    )


def project_kernel(
    core_ref, a_ref, b_ref, c_ref, d_ref, gain_ref, time_ref, feat_ref, w_ref,
    in_ref, x_ref, qkv_ref, room, wide, sems, *, scale, cols,
):
    part = pl.program_id(0)
    core = core_ref[0]
    dm = in_ref.shape[1]
    width = qkv_ref.shape[2]

    @pl.when(part == 0)
    def _():
        for k in range(3):
            fetch(k, core, w_ref, room, sems, cols, dm).start()
        rows = a_ref.shape[0]
        x_ref[:rows, :] = a_ref[...]
        x_ref[rows:, :] = b_ref[...]
        for k, ref in enumerate((a_ref, b_ref, c_ref, d_ref)):
            x = ref[...].astype(F32)
            centre = x - jnp.mean(x, axis=-1, keepdims=True)
            spread = jnp.mean(centre * centre, axis=-1, keepdims=True)
            normed = centre * lax.rsqrt(spread + EPS) * gain_ref[...]
            in_ref[k * rows : (k + 1) * rows, :] = normed.astype(BF)

    fetch(part, core, w_ref, room, sems, cols, dm).wait()
    wide[...] = dot(room[part], in_ref[...], 0, 1)
    shift = core * cols - (core * cols) // LANES * LANES
    factor = jnp.where(part == 0, scale, 1.0)
    hot = feat_ref[IMAGE_HOT:, :].astype(F32)
    for h in range(cols // width):
        at = pl.multiple_of(shift + h * width, 8)
        x = wide[pl.ds(at, width), :]
        t = time_ref[0, h * width : (h + 1) * width, :]
        for j in range(4):
            x = x + t[:, j : j + 1] * hot[j : j + 1]
        qkv_ref[0, h] = (x * factor).astype(BF)


def project(core, blocks, gain, times, feats, w_qkv, scale, heads):
    rows, dm = blocks[0].shape
    tokens = 4 * rows
    cols = times.shape[1]
    width = cols // heads
    whole = lambda p, t: (0, 0)
    room = window(cols)
    return pl.pallas_call(
        functools.partial(project_kernel, scale=scale, cols=cols),
        grid_spec=pltpu.PrefetchScalarGridSpec(
            num_scalar_prefetch=1,
            grid=(3,),
            in_specs=[pl.BlockSpec((rows, dm), whole)] * 4
            + [
                pl.BlockSpec((1, dm), whole),
                pl.BlockSpec((1, cols, 4), lambda p, t: (p, 0, 0)),
                pl.BlockSpec(feats.shape, whole),
                ANYWHERE,
            ],
            out_specs=[
                pl.BlockSpec((tokens, dm), whole),
                pl.BlockSpec((2 * rows, dm), whole),
                pl.BlockSpec((1, heads, width, tokens), lambda p, t: (p, 0, 0, 0)),
            ],
            scratch_shapes=[
                pltpu.VMEM((3, dm, room), BF),
                pltpu.VMEM((room, tokens), F32),
                pltpu.SemaphoreType.DMA((3,)),
            ],
        ),
        out_shape=[
            jax.ShapeDtypeStruct((tokens, dm), BF),
            jax.ShapeDtypeStruct((2 * rows, dm), BF),
            jax.ShapeDtypeStruct((3, heads, width, tokens), BF),
        ],
        compiler_params=params("arbitrary"),
        cost_estimate=CHEAP,
        name="project",
    )(core, *blocks, gain, times, feats, w_qkv)


def weights_kernel(clock_ref, in_ref, d_ref, out_ref):
    d = jnp.concatenate([d_ref[0, h].astype(F32) for h in range(d_ref.shape[1])], axis=0)
    out_ref[0] = dot(in_ref[...], d.astype(BF), 0, 1).astype(BF)


def project_weights(clock, attn_in, d):
    parts, heads, width, tokens = d.shape
    dm = attn_in.shape[1]
    return pl.pallas_call(
        weights_kernel,
        grid_spec=pltpu.PrefetchScalarGridSpec(
            num_scalar_prefetch=1,
            grid=(parts,),
            in_specs=[
                pl.BlockSpec((tokens, dm), lambda p, t: (0, 0)),
                pl.BlockSpec((1, heads, width, tokens), lambda p, t: (p, 0, 0, 0)),
            ],
            out_specs=pl.BlockSpec((1, dm, heads * width), lambda p, t: (p, 0, 0)),
        ),
        out_shape=jax.ShapeDtypeStruct((parts, dm, heads * width), BF),
        compiler_params=params("arbitrary"),
        cost_estimate=CHEAP,
        name="project_weights",
    )(clock, attn_in, d)


def project_back_kernel(
    clock_ref, core_ref, d_ref, w_ref, mine_ref, far_ref, room, wide, total, sems, *, cols
):
    part = pl.program_id(0)
    core = core_ref[0]
    dm = w_ref.shape[0]
    width = d_ref.shape[2]

    @pl.when(part == 0)
    def _():
        for k in range(3):
            fetch(k, core, w_ref, room, sems, cols, dm).start()
        wide[...] = jnp.zeros_like(wide)

    shift = core * cols - (core * cols) // LANES * LANES
    for h in range(cols // width):
        at = pl.multiple_of(shift + h * width, 8)
        wide[pl.ds(at, width), :] = d_ref[0, h].astype(F32)
    fetch(part, core, w_ref, room, sems, cols, dm).wait()
    term = dot(wide[...].astype(BF), room[part], 0, 1)

    @pl.when(part == 0)
    def _():
        total[...] = term

    @pl.when(part == 1)
    def _():
        total[...] += term

    @pl.when(part == 2)
    def _():
        rows = mine_ref.shape[0]
        mine_ref[...] = total[:rows, :] + term[:rows]
        far_ref[...] = (total[rows:, :] + term[rows:]).astype(BF)


def project_back(clock, core, d, w_qkv, mine):
    parts, heads, width, tokens = d.shape
    dm = w_qkv.shape[0]
    cols = heads * width
    room = window(cols)
    whole = lambda p, t, u: (0, 0)
    return pl.pallas_call(
        functools.partial(project_back_kernel, cols=cols),
        grid_spec=pltpu.PrefetchScalarGridSpec(
            num_scalar_prefetch=2,
            grid=(parts,),
            in_specs=[
                pl.BlockSpec((1, heads, width, tokens), lambda p, t, u: (p, 0, 0, 0)),
                ANYWHERE,
            ],
            out_specs=[pl.BlockSpec((mine, dm), whole), pl.BlockSpec((tokens - mine, dm), whole)],
            scratch_shapes=[
                pltpu.VMEM((3, dm, room), BF),
                pltpu.VMEM((room, tokens), F32),
                pltpu.VMEM((tokens, dm), F32),
                pltpu.SemaphoreType.DMA((3,)),
            ],
        ),
        out_shape=[
            jax.ShapeDtypeStruct((mine, dm), F32),
            jax.ShapeDtypeStruct((tokens - mine, dm), BF),
        ],
        compiler_params=params("arbitrary"),
        cost_estimate=CHEAP,
        name="project_back",
    )(clock, core, d, w_qkv)


def query_block(b, bias, feat_ref, q):
    at = slice(b * QUERY_BLOCK, (b + 1) * QUERY_BLOCK)
    return jnp.concatenate([bias[:, at], feat_ref[QUERY_MASK:IMAGE_HOT, at], q[:, at]], axis=0)


def forward_kernel(clock_ref, p_ref, table_ref, feat_ref, o_ref, lse_ref):
    blocks = p_ref.shape[3] // QUERY_BLOCK
    q, k, v = (p_ref[p, 0] for p in range(3))
    bias = jnp.dot(table_ref[0], feat_ref[:RC], preferred_element_type=F32).astype(BF)
    key = jnp.concatenate([feat_ref[:QUERY_MASK], k], axis=0).T

    def scores(b):
        return jnp.dot(key, query_block(b, bias, feat_ref, q), preferred_element_type=F32)

    ahead = scores(0)
    for b in range(blocks):
        at = slice(b * QUERY_BLOCK, (b + 1) * QUERY_BLOCK)
        s = ahead
        top = jnp.max(s, axis=0, keepdims=True)
        if b + 1 < blocks:
            ahead = scores(b + 1)
        e = jnp.exp(s - top)
        total = jnp.sum(e, axis=0, keepdims=True)
        o = jnp.dot(v, e.astype(BF), preferred_element_type=F32) / total
        o_ref[0, :, at] = o.astype(BF)
        lse_ref[0, :, at] = top + jnp.log(total)


def attend_forward(clock, qkv, tables, feats, first, count):
    parts, heads, width, tokens = qkv.shape
    return pl.pallas_call(
        forward_kernel,
        grid_spec=pltpu.PrefetchScalarGridSpec(
            num_scalar_prefetch=1,
            grid=(count,),
            in_specs=[
                pl.BlockSpec((parts, 1, width, tokens), lambda h, t: (0, first + h, 0, 0)),
                pl.BlockSpec((1, RC, RC), lambda h, t: (first + h, 0, 0)),
                pl.BlockSpec(feats.shape, lambda h, t: (0, 0)),
            ],
            out_specs=[
                pl.BlockSpec((1, width, tokens), lambda h, t: (h, 0, 0)),
                pl.BlockSpec((1, 1, tokens), lambda h, t: (h, 0, 0)),
            ],
        ),
        out_shape=[
            jax.ShapeDtypeStruct((count, width, tokens), BF),
            jax.ShapeDtypeStruct((count, 1, tokens), F32),
        ],
        compiler_params=params("arbitrary"),
        cost_estimate=CHEAP,
        name="attention_forward",
    )(clock, qkv, tables, feats)


def backward_kernel(clock_ref, qkv_ref, o_ref, do_ref, lse_ref, table_ref, feat_ref, *rest, scale):
    d_ref, toe_ref, image_ref = rest[-3:]
    width = o_ref.shape[1]
    tokens = o_ref.shape[2]
    q, k, v = (qkv_ref[p, 0] for p in range(3))
    do = do_ref[0]
    delta = jnp.sum(do.astype(F32) * o_ref[0].astype(F32), axis=0, keepdims=True)
    rc = feat_ref[:RC]
    bias = jnp.dot(table_ref[0], rc, preferred_element_type=F32).astype(BF)
    key_t = jnp.concatenate([feat_ref[:QUERY_MASK], k], axis=0)
    key = key_t.T
    value = v.T
    dk = jnp.zeros((tokens, width), F32)
    dv = jnp.zeros((tokens, width), F32)
    dq_parts, bias_parts = [], []

    def first(b):
        at = slice(b * QUERY_BLOCK, (b + 1) * QUERY_BLOCK)
        s = jnp.dot(key, query_block(b, bias, feat_ref, q), preferred_element_type=F32)
        return s, jnp.dot(value, do[:, at], preferred_element_type=F32)

    ahead = first(0)
    for b in range(tokens // QUERY_BLOCK):
        at = slice(b * QUERY_BLOCK, (b + 1) * QUERY_BLOCK)
        s, dp = ahead
        p = jnp.exp(s - lse_ref[0, :, at])
        ds = (p * (dp - delta[:, at])).astype(BF)
        p = p.astype(BF)
        if (b + 1) * QUERY_BLOCK < tokens:
            ahead = first(b + 1)
        dq = jnp.dot(key_t, ds, preferred_element_type=F32)
        dq_parts.append((dq[QUERY_MASK:] * scale).astype(BF))
        bias_parts.append(dq[:RC].astype(BF))
        dk = dk + dot(ds, q[:, at], 1, 1)
        dv = dv + dot(p, do[:, at], 1, 1)
    toe = dot(rc, jnp.concatenate(bias_parts, axis=1), 1, 1)
    dq = jnp.concatenate(dq_parts, axis=1)
    dk = dk.T.astype(BF)
    dv = dv.T.astype(BF)
    d_ref[0, 0] = dq
    d_ref[1, 0] = dk
    d_ref[2, 0] = dv
    toe_ref[0] = toe
    hot = feat_ref[IMAGE_HOT:]
    image_ref[0, 0] = dot(hot, dq, 1, 1)
    image_ref[1, 0] = dot(hot, dv, 1, 1)


def attend_backward(clock, qkv, o, do, lse, tables, feats, scale, first, count, before):
    parts, heads, width, tokens = qkv.shape
    head3 = lambda h, t: (first + h, 0, 0)
    head4 = lambda h, t: (0, first + h, 0, 0)
    return pl.pallas_call(
        functools.partial(backward_kernel, scale=scale),
        grid_spec=pltpu.PrefetchScalarGridSpec(
            num_scalar_prefetch=1,
            grid=(count,),
            in_specs=[
                pl.BlockSpec((parts, 1, width, tokens), head4),
                pl.BlockSpec((1, width, tokens), head3),
                pl.BlockSpec((1, width, tokens), head3),
                pl.BlockSpec((1, 1, tokens), head3),
                pl.BlockSpec((1, RC, RC), head3),
                pl.BlockSpec(feats.shape, lambda h, t: (0, 0)),
            ]
            + [ANYWHERE] * len(before),
            out_specs=[
                pl.BlockSpec((parts, 1, width, tokens), head4),
                pl.BlockSpec((1, RC, RC), head3),
                pl.BlockSpec((2, 1, 16, width), head4),
            ],
        ),
        out_shape=[
            jax.ShapeDtypeStruct((parts, heads, width, tokens), BF),
            jax.ShapeDtypeStruct((heads, RC, RC), F32),
            jax.ShapeDtypeStruct((2, heads, 16, width), F32),
        ],
        input_output_aliases={7 + k: k for k in range(len(before))},
        compiler_params=params("arbitrary"),
        cost_estimate=CHEAP,
        name="attention_backward",
    )(clock, qkv, o, do, lse, tables, feats, *before)


def rise_kernel(
    m_ref, near_ref, far_ref, valid_ref, up_ref, down_ref,
    two_ref, slope_ref, wd_ref, mt_ref, g_ref,
):
    @pl.when(pl.program_id(0) == 0)
    def _():
        two_ref[...] = jnp.zeros_like(two_ref)
        mt_ref[...] = m_ref[...].T
        half = near_ref.shape[0]
        g_ref[:half, :] = (near_ref[...].astype(F32) * valid_ref[:half, :1]).astype(BF)
        g_ref[half:, :] = (far_ref[...].astype(F32) * valid_ref[half:, :1]).astype(BF)

    def up_of(j):
        return jnp.dot(m_ref[...], up_ref[:, j : j + FF_STEP], preferred_element_type=F32)

    acts = []
    tile = up_ref.shape[1]
    ahead = up_of(0)
    for j in range(0, tile, FF_STEP):
        at = slice(j, j + FF_STEP)
        up = ahead
        if j + FF_STEP < tile:
            ahead = up_of(j + FF_STEP)
        half = 0.5 + 0.5 * lax.erf(up * math.sqrt(0.5))
        slope = half + up * (jnp.exp(-0.5 * up * up) * (1.0 / math.sqrt(2.0 * math.pi)))
        slope_ref[:, at] = slope.astype(BF)
        acts.append((up * half).astype(BF))
    act = jnp.concatenate(acts, axis=1)
    wd_ref[...] = dot(act, g_ref[...], 0, 0).astype(BF)
    two_ref[...] += jnp.dot(act, down_ref[...], preferred_element_type=F32)


def mlp_rise(m, near, far, valid, w_up, w_down, tile):
    rows, dm = m.shape
    ff = w_up.shape[1]
    whole = lambda i: (0, 0)
    return pl.pallas_call(
        rise_kernel,
        grid=(ff // tile,),
        in_specs=[
            pl.BlockSpec((rows, dm), whole),
            pl.BlockSpec(near.shape, whole),
            pl.BlockSpec(far.shape, whole),
            pl.BlockSpec(valid.shape, whole),
            pl.BlockSpec((dm, tile), lambda i: (0, i)),
            pl.BlockSpec((tile, dm), lambda i: (i, 0)),
        ],
        out_specs=[
            pl.BlockSpec((rows, dm), whole),
            pl.BlockSpec((rows, tile), lambda i: (0, i)),
            pl.BlockSpec((tile, dm), lambda i: (i, 0)),
            pl.BlockSpec((dm, rows), whole),
            pl.BlockSpec((rows, dm), whole),
        ],
        out_shape=[
            jax.ShapeDtypeStruct((rows, dm), F32),
            jax.ShapeDtypeStruct((rows, ff), BF),
            jax.ShapeDtypeStruct((ff, dm), BF),
            jax.ShapeDtypeStruct((dm, rows), BF),
            jax.ShapeDtypeStruct((rows, dm), BF),
        ],
        compiler_params=params("arbitrary"),
        cost_estimate=CHEAP,
        name="feed_forward_rise",
    )(m, near, far, valid, w_up, w_down)


def fall_kernel(clock_ref, tile_ref, mt_ref, g_ref, up_ref, down_ref, slope_ref, *rest):
    gm_out, send_ref, own_ref = rest[-3:]
    step = pl.program_id(0)

    @pl.when(step == 0)
    def _():
        gm_out[...] = rest[0][...] if len(rest) > 3 else jnp.zeros_like(gm_out)

    du = (dot(g_ref[...], down_ref[...], 1, 1) * slope_ref[...].astype(F32)).astype(BF)
    gm_out[...] += dot(du, up_ref[...], 1, 1)
    wu = jnp.dot(mt_ref[...], du, preferred_element_type=F32).astype(BF)

    @pl.when(step % 2 == 0)
    def _():
        send_ref[...] = wu

    @pl.when(step % 2 == 1)
    def _():
        own_ref[...] = wu


def mlp_fall(clock, tiles, mt, g, w_up, w_down, slope, tile, first, pairs, before):
    dm, rows = mt.shape
    ff = w_up.shape[1]
    whole = lambda i, u, t: (0, 0)
    column = lambda i, u, t: (0, first + i // 2)
    at = lambda i, t: 2 * (first + i // 2) + t[i % 2]
    return pl.pallas_call(
        fall_kernel,
        grid_spec=pltpu.PrefetchScalarGridSpec(
            num_scalar_prefetch=2,
            grid=(2 * pairs,),
            in_specs=[
                pl.BlockSpec((dm, rows), whole),
                pl.BlockSpec((rows, dm), whole),
                pl.BlockSpec((dm, tile), lambda i, u, t: (0, at(i, t))),
                pl.BlockSpec((tile, dm), lambda i, u, t: (at(i, t), 0)),
                pl.BlockSpec((rows, tile), lambda i, u, t: (0, at(i, t))),
            ]
            + ([pl.BlockSpec((rows, dm), whole), ANYWHERE, ANYWHERE] if before else []),
            out_specs=[
                pl.BlockSpec((rows, dm), whole),
                pl.BlockSpec((dm, tile), column),
                pl.BlockSpec((dm, tile), column),
            ],
        ),
        out_shape=[
            jax.ShapeDtypeStruct((rows, dm), F32),
            jax.ShapeDtypeStruct((dm, ff // 2), BF),
            jax.ShapeDtypeStruct((dm, ff // 2), BF),
        ],
        input_output_aliases={8: 1, 9: 2} if before else {},
        compiler_params=params("arbitrary"),
        cost_estimate=CHEAP,
        name="feed_forward_fall",
    )(clock, tiles, mt, g, w_up, w_down, slope, *before)


def moments(x):
    centre = x - jnp.mean(x, axis=-1, keepdims=True)
    root = lax.rsqrt(jnp.mean(centre * centre, axis=-1, keepdims=True) + EPS)
    return centre * root, root


def norm_backward(d, n, root):
    return root * (
        d - jnp.mean(d, axis=-1, keepdims=True) - n * jnp.mean(d * n, axis=-1, keepdims=True)
    )


def columns(x):
    return jnp.sum(x, axis=0, keepdims=True)


def middle_kernel(
    clock_ref, gm_ref, two_ref, one_ref, h_ref, g_ref, valid_ref, gain_ref,
    out_ref, grad_ref, low_ref, sums_ref,
):
    @pl.when(pl.program_id(0) == 0)
    def _():
        sums_ref[...] = jnp.zeros_like(sums_ref)

    valid = valid_ref[:, :1]
    two, one, h = two_ref[...], one_ref[...], h_ref[...]
    h2 = h + two
    out_ref[...] = (h2 * valid).astype(BF)
    n, root = moments(h)
    gm = gm_ref[...]
    grad = g_ref[...].astype(F32) + norm_backward(gm * gain_ref[...], n, root)
    grad_ref[...] = grad
    low_ref[...] = grad.astype(BF)
    sums_ref[0:1, :] += columns(gm * n)
    sums_ref[1:2, :] += columns(valid * h2 * h2)
    sums_ref[2:3, :] += columns(valid * one * one)
    sums_ref[3:4, :] += columns(valid * two * two)


def middle(clock, gm, two, one, hidden, grads, valid, gain):
    rows, dm = gm.shape
    step = rows // 4
    block = pl.BlockSpec((step, dm), lambda i, t: (i, 0))
    return pl.pallas_call(
        middle_kernel,
        grid_spec=pltpu.PrefetchScalarGridSpec(
            num_scalar_prefetch=1,
            grid=(4,),
            in_specs=[block] * 5
            + [
                pl.BlockSpec((step, LANES), lambda i, t: (i, 0)),
                pl.BlockSpec((1, dm), lambda i, t: (0, 0)),
            ],
            out_specs=[block, block, block, pl.BlockSpec((8, dm), lambda i, t: (0, 0))],
        ),
        out_shape=[
            jax.ShapeDtypeStruct((rows, dm), BF),
            jax.ShapeDtypeStruct((rows, dm), F32),
            jax.ShapeDtypeStruct((rows, dm), BF),
            jax.ShapeDtypeStruct((8, dm), F32),
        ],
        compiler_params=params("arbitrary"),
        cost_estimate=CHEAP,
        name="middle",
    )(clock, gm, two, one, hidden, grads, valid, gain)


def last_kernel(back_ref, far_ref, x_ref, grad_ref, gain_ref, out_ref, sums_ref):
    @pl.when(pl.program_id(0) == 0)
    def _():
        sums_ref[...] = jnp.zeros_like(sums_ref)

    back = back_ref[...] + far_ref[...].astype(F32)
    n, root = moments(x_ref[...].astype(F32))
    out_ref[...] = (grad_ref[...] + norm_backward(back * gain_ref[...], n, root)).astype(BF)
    sums_ref[0:1, :] += columns(back * n)


def last(back, far, x, grad, gain):
    rows, dm = back.shape
    step = rows // 4
    block = pl.BlockSpec((step, dm), lambda i: (i, 0))
    return pl.pallas_call(
        last_kernel,
        grid=(4,),
        in_specs=[block] * 4 + [pl.BlockSpec((1, dm), lambda i: (0, 0))],
        out_specs=[block, pl.BlockSpec((8, dm), lambda i: (0, 0))],
        out_shape=[jax.ShapeDtypeStruct((rows, dm), BF), jax.ShapeDtypeStruct((8, dm), F32)],
        compiler_params=params("arbitrary"),
        cost_estimate=CHEAP,
        name="last",
    )(back, far, x, grad, gain)


class Halving:
    def __init__(self, names, dims, base, piece, prefix=(), suffix=(), column=0):
        self.names, self.dims, self.base, self.piece = names, dims, base, piece
        self.prefix, self.suffix, self.column = prefix, suffix, column
        self.stage, self.arrived, self.result = 0, [], None

    def left(self, stage):
        return [d for d in self.names if d in self.dims[stage + 1 :]]

    def specs(self, gridded):
        stage = self.stage
        open_dims = self.left(stage)

        def index(names, prefix, suffix, column):
            def at(*grid):
                t = grid[-1]
                out = list(prefix)
                for d in names:
                    if d in gridded:
                        out.append(grid[gridded.index(d)])
                    elif d in open_dims:
                        out.append(0)
                    elif stage < len(self.dims) and d == self.dims[stage]:
                        out.append(1 - t[d])
                    else:
                        out.append(t[d])
                return tuple(out) + tuple(suffix) + (0, column)

            return at

        def block(names, prefix, suffix):
            sizes = [2 if d in open_dims and d not in gridded else None for d in names]
            return (None,) * len(prefix) + tuple(sizes) + (None,) * len(suffix) + self.piece

        arrays, specs = [], []
        for array in self.base:
            arrays.append(array)
            specs.append(
                pl.BlockSpec(
                    block(self.names, self.prefix, self.suffix),
                    index(self.names, self.prefix, self.suffix, self.column),
                )
            )
        for s, (array, place) in enumerate(self.arrived):
            arrays.append(array)
            names = self.left(s)
            specs.append(pl.BlockSpec(block(names, (place,), ()), index(names, (place,), (), 0)))
        rest = index(open_dims, (), (), 0)
        inner = tuple(2 if d not in gridded else None for d in open_dims) + self.piece
        return arrays, specs, inner, rest, (2,) * len(open_dims) + self.piece


def sum_kernel(coord_ref, *refs, counts, places):
    outs = refs[sum(counts) :]
    at = 0
    for (out, place), count in zip(places, counts):
        total = refs[at][...].astype(F32)
        for k in range(1, count):
            total = total + refs[at + k][...].astype(F32)
        outs[out][place] = total.astype(BF)
        at += count


def advance(clock, swaps, jobs):
    arrays, in_specs, counts, groups, places = [], [], [], [], []
    stage = jobs[0].stage
    steps = min(2, max(0, len(jobs[0].left(stage)) - 1))
    for job in jobs:
        some, their, inner, rest, shape = job.specs(job.left(stage)[:steps])
        arrays, in_specs = arrays + some, in_specs + their
        counts.append(len(some))
        sent = job.dims[stage] if stage < len(job.dims) else None
        key = (sent, shape)
        found = [k for k, g in enumerate(groups) if g[0] == key]
        if not found:
            groups.append((key, inner, rest, []))
        group = found[0] if found else len(groups) - 1
        places.append((group, len(groups[group][3])))
        groups[group][3].append(job)
    out_specs = [
        pl.BlockSpec((len(g[3]),) + g[1], lambda *grid, f=g[2]: (0,) + f(*grid)) for g in groups
    ]
    sums = pl.pallas_call(
        functools.partial(sum_kernel, counts=counts, places=places),
        grid_spec=pltpu.PrefetchScalarGridSpec(
            num_scalar_prefetch=1,
            grid=(2,) * steps if steps else (1,),
            in_specs=in_specs,
            out_specs=out_specs,
        ),
        out_shape=[jax.ShapeDtypeStruct((len(g[3]),) + g[0][1], BF) for g in groups],
        compiler_params=params(*("arbitrary",) * max(steps, 1)),
        cost_estimate=CHEAP,
        name="sum_pieces",
    )(clock.now, *arrays)
    for (key, inner, rest, members), total in zip(groups, sums):
        if key[0] is not None:
            total = swaps[key[0]](total)
        for k, job in enumerate(members):
            if key[0] is None:
                job.result = total[k]
            else:
                job.arrived.append((total, k))
                job.stage += 1
    clock.passed(*sums)


class Clock:
    def __init__(self, now):
        self.now = now

    def passed(self, *results):
        self.now = lax.optimization_barrier((self.now, *results))[0]

    def tie(self, x):
        return lax.optimization_barrier((x, self.now))[0]


class Gather:
    def __init__(self, clock, part, swaps):
        self.clock, self.part, self.swaps, self.far = clock, part, list(swaps), None

    def land(self):
        if self.far is not None:
            bit, axis = self.put
            low, high = jnp.where(bit, self.far, self.part), jnp.where(bit, self.part, self.far)
            self.part = jnp.concatenate([low, high], axis=axis)
            self.clock.passed(self.part)
            self.far = None

    def tick(self):
        self.land()
        if self.swaps:
            swap, bit, axis = self.swaps.pop(0)
            self.put = (bit, axis)
            self.far = swap(self.clock.tie(self.part))

    def finish(self):
        while self.far is not None or self.swaps:
            self.tick()
        return self.part


class Total:
    def __init__(self, clock, part, swaps):
        self.clock, self.part, self.swaps, self.far = clock, part, list(swaps), None

    def tick(self):
        if self.far is not None:
            self.part = self.part + self.far
            self.clock.passed(self.part)
            self.far = None
        if self.swaps:
            self.far = self.swaps.pop(0)(self.clock.tie(self.part))

    def finish(self):
        while self.far is not None or self.swaps:
            self.tick()
        return self.part


def pick(array, index, axis=0):
    return lax.dynamic_index_in_dim(array, index, axis, keepdims=False)


def toeplitz_tables(rel, count):
    d = jnp.arange(2 * count - 1, dtype=jnp.int32)
    t = jnp.arange(count, dtype=jnp.int32)
    hot = (d[:, None, None] == t[None, None, :] - t[None, :, None] + count - 1).astype(BF)
    return jnp.einsum("hd,dtr->htr", rel.astype(BF), hot, preferred_element_type=F32)


def per_device(
    tokens, time_embed, image_lengths, grid_turns, ln1_gain, w_qkv, w_time_q, time_value_weight,
    rel_rows, rel_cols, output_projection_weight, ln2_gain, w_up, w_down, out_grad,
):
    slots, span, dm = tokens.shape
    heads = rel_rows.shape[0]
    width = dm // heads
    ff = w_up.shape[1]
    scale = width ** (-0.5)
    n_seq = lax.axis_size("seq")
    n_img = lax.axis_size("img")
    cores = n_seq // slots
    own_heads = heads // cores
    cols = own_heads * width
    me_img = lax.axis_index("img")
    me_seq = lax.axis_index("seq")
    y = me_seq // cores
    c = me_seq % cores
    mine = slots * span
    rows = dm // n_img
    over_y = [(s, (slots - 1 - s // cores) * cores + s % cores) for s in range(n_seq)]
    over_core = [(s, s // cores * cores + cores - 1 - s % cores) for s in range(n_seq)]

    def swap_y(a):
        return lax.ppermute(a, "seq", over_y)

    def swap_core(a):
        return lax.ppermute(a, "seq", over_core)

    bits = n_img.bit_length() - 1
    on_y, on_core = bits, bits + 1
    swaps = {
        k: functools.partial(
            lax.ppermute, axis_name="img", perm=[(i, i ^ (1 << k)) for i in range(n_img)]
        )
        for k in range(bits)
    }
    swaps[on_y], swaps[on_core] = swap_y, swap_core

    def across_y(parts):
        part = jnp.concatenate(parts, axis=1)
        return part, swap_y(part)

    def across_core(part, far):
        part = jnp.concatenate([jnp.where(y == 0, part, far), jnp.where(y == 0, far, part)], axis=0)
        return part, swap_core(part)

    def both_cores(part, far):
        return jnp.where(c == 0, part, far).astype(F32), jnp.where(c == 0, far, part).astype(F32)

    def order(*first):
        return list(first) + [k for k in range(bits) if k not in first]

    tok_own = pick(tokens, y)
    tok_rx = swap_y(pick(tokens, 1 - y))
    tok_own_far = swap_core(tok_own)
    block = lambda yy, cc: (yy * cores + cc) * span
    bases = jnp.stack([block(y, c), block(1 - y, c), block(y, 1 - c), block(1 - y, 1 - c)])
    feats, valid = token_features(
        pick(image_lengths, y), pick(grid_turns, y), bases.astype(jnp.int32), span, mine
    )
    coords = jnp.stack([(me_img >> k) & 1 for k in range(bits)] + [y, c]).astype(jnp.int32)
    core = c.astype(jnp.int32).reshape(1)
    pair = jnp.stack([1 - c, c]).astype(jnp.int32)
    te = pick(time_embed, y)

    def time_terms(w):
        all_heads = dot(te, w, 1, 0)
        return lax.dynamic_slice_in_dim(all_heads, c * cols, cols, 1).T

    time_q = time_terms(w_time_q)
    times = jnp.stack([time_q, jnp.zeros_like(time_q), time_terms(time_value_weight)])
    row_table = toeplitz_tables(lax.dynamic_slice_in_dim(rel_rows, c * own_heads, own_heads), SIDE)
    col_table = toeplitz_tables(lax.dynamic_slice_in_dim(rel_cols, c * own_heads, own_heads), SIDE)
    gap = jnp.zeros_like(row_table)
    tables = jnp.concatenate(
        [
            jnp.concatenate([row_table, gap], axis=2),
            jnp.concatenate([gap, col_table], axis=2),
        ],
        axis=1,
    ).astype(BF)
    ln1_row, ln2_row = ln1_gain.reshape(1, dm), ln2_gain.reshape(1, dm)
    grad_out = pick(out_grad, 1 - y)
    grad_own = pick(out_grad, y)

    img_bits = [((me_img >> k) & 1) == 1 for k in range(bits)]
    clock = Clock(coords)
    clock.passed(feats, times, tables, core, pair, grad_out, grad_own, ln1_row, ln2_row)
    tok_rx = clock.tie(tok_rx)
    grad_rx = swap_y(lax.optimization_barrier((grad_out, tok_rx))[0])
    attn_in, x, qkv = project(
        core, (tok_own, tok_rx, tok_own_far, swap_core(tok_rx)), ln1_row, times, feats, w_qkv,
        scale, own_heads,
    )
    clock.passed(qkv)
    half_heads = own_heads // 2
    o_a, lse_a = attend_forward(clock.now, qkv, tables, feats, 0, half_heads)
    clock.passed(o_a, grad_rx)
    far_a = swap_core(o_a)
    o_b, lse_b = attend_forward(clock.now, qkv, tables, feats, half_heads, half_heads)
    far_b = swap_core(o_b)

    o_own = jnp.concatenate([o_a, o_b], axis=0)
    lse = jnp.concatenate([lse_a, lse_b], axis=0)
    clock.passed(o_b)

    def turned(a):
        a = a.reshape(cols // 2, 2 * mine)
        return jnp.concatenate([a[:, mine:], a[:, :mine]], axis=1)

    o_flat = o_own.reshape(cols, 2 * mine)
    o_far = jnp.concatenate([turned(far_a), turned(far_b)], axis=0)
    attn_all = jnp.concatenate(
        [jnp.where(c == 0, o_flat, o_far), jnp.where(c == 0, o_far, o_flat)], axis=0
    )
    branch_one = dot(attn_all[:, :mine], output_projection_weight, 0, 0)
    hidden_one = x.astype(F32) + branch_one
    mlp_in = clock.tie((moments(hidden_one)[0] * ln2_gain).astype(BF))

    tile = ff // 6
    two, slope, down, mlp_in_t, grad_branch = mlp_rise(
        mlp_in, grad_own, grad_rx, valid, w_up, w_down, ff // 3
    )
    clock.passed(two)
    down = lax.psum_scatter(down, ("img", "seq"), scatter_dimension=0, tiled=True)
    img_names = list(range(bits))[::-1]
    twos = (2,) * bits
    step = functools.partial(advance, clock, swaps)

    def finish(jobs):
        while jobs[0].result is None:
            step(jobs)

    gm, send, own = mlp_fall(
        clock.now, pair, mlp_in_t, grad_branch, w_up, w_down, slope, tile, 0, 3, ()
    )
    clock.passed(gm)
    output, grad_one, gb_mine, sums = middle(
        clock.now, gm, two, branch_one, hidden_one, grad_branch, valid, ln2_row
    )
    clock.passed(output)
    gb_far = swap_core(gb_mine)
    far_up = swap_core(lax.optimization_barrier((send, gb_far))[0])
    gb_all = jnp.concatenate([gb_mine, gb_far], axis=0)
    out_far = swap_y(output[span:])
    w_proj_rows = lax.dynamic_slice_in_dim(output_projection_weight, c * cols, cols, 0)
    do = dot(w_proj_rows, gb_all, 1, 1).astype(BF).reshape(own_heads, width, 2 * mine)
    gb_cols = lax.dynamic_slice_in_dim(gb_all, c * cols, cols, 1)
    proj_part = dot(attn_all, gb_cols, 1, 0).astype(BF)
    clock.passed(do, proj_part)

    def by_row(dims, arrays, columns_of, column=0, prefix=()):
        shape = twos + (2, rows // 2)
        return Halving(
            img_names + [on_y],
            dims,
            [a.reshape(a.shape[: len(prefix)] + shape + a.shape[-1:]) for a in arrays],
            (rows // 2, columns_of),
            prefix=prefix,
            column=column,
        )

    orders = [order(0, on_y, 1), order(on_y, 1, 0), order(1, 0, on_y)]
    up_half = ff // 4
    jobs_up = [
        by_row(dims, (own, far_up), up_half, k)
        for k, dims in enumerate([order(0, 1, on_y), order(on_y, 0, 1)])
    ]
    job_proj = by_row(orders[2], (proj_part,), cols)
    clock.passed(out_far)
    step(jobs_up + [job_proj])
    grads = attend_backward(
        clock.now, qkv, o_own, do, lse, tables, feats, scale, 0, own_heads, ()
    )
    d, toe, image_grads = grads
    clock.passed(d)
    step(jobs_up)
    part = jnp.transpose(image_grads[:, :, :4], (0, 2, 1, 3)).reshape(8, cols).astype(BF)
    gather = Gather(
        clock,
        part[None, None],
        [(swap_core, c == 1, 3), (swap_y, y == 1, 1)]
        + [(swaps[k], img_bits[k], 0) for k in range(bits)],
    )
    gather.tick()
    w_part = project_weights(clock.now, attn_in, d)
    clock.passed(w_part, job_proj.arrived[0][0])
    gather.land()
    gather.part = jnp.concatenate([gather.part, te[None, None]], axis=2)
    jobs_qkv = [by_row(dims, (w_part,), cols, prefix=(p,)) for p, dims in enumerate(orders)]
    step(jobs_qkv)
    jobs_qkv.append(job_proj)
    back, back_far = project_back(clock.now, core, d, w_qkv, mine)
    clock.passed(back)
    step(jobs_up)
    back_far = swap_core(clock.tie(back_far))
    step(jobs_qkv)
    clock.passed(down)
    down_far = swap_y(clock.tie(down))
    input_grad, sums_one = last(back, back_far, x, grad_one, ln1_row)
    clock.passed(input_grad)
    reach = jnp.arange(2 * SIDE - 1, dtype=jnp.int32)
    side = jnp.arange(SIDE, dtype=jnp.int32)
    diag = (reach == side[:, None, None] - side[None, :, None] + SIDE - 1).astype(F32)
    rel = jnp.stack([toe[:, :SIDE, :SIDE], toe[:, SIDE:, SIDE:]])
    rel = jnp.einsum("khrt,rtd->khd", rel, diag, precision=lax.Precision.HIGHEST)
    rel_all = lax.dynamic_update_slice(
        jnp.zeros((2, heads, 2 * SIDE - 1), F32), rel, (0, c * own_heads, 0)
    )
    stats = jnp.concatenate([jnp.sum(sums[1:4], axis=1), jnp.sum(valid[:, 0])[None]])
    small = jnp.concatenate([sums_one[0], sums[0], rel_all.reshape(-1), stats])
    def returned(own_rows, far_rows):
        return jnp.stack(
            [jnp.where(y == 0, own_rows, far_rows), jnp.where(y == 0, far_rows, own_rows)]
        )

    small = Total(clock, small, [swap_core, swap_y] + [swaps[k] for k in range(bits)])

    small.tick()
    step(jobs_qkv)
    gather.tick()
    down = jnp.where(y == 0, jnp.stack([down, down_far]), jnp.stack([down_far, down]))
    output = returned(output[:span], out_far)
    in_far = swap_y(clock.tie(input_grad)[span:])
    clock.passed(output)
    step(jobs_up)
    small.tick()
    gather.tick()
    down_far = swap_core(down)
    step(jobs_qkv)
    small.tick()
    gather.tick()
    h0, h1 = both_cores(down, down_far)
    w_down_grad = jnp.concatenate([h0[0], h1[0], h0[1], h1[1]], axis=0)
    clock.passed(w_down_grad)
    finish(jobs_up)
    up_parts, up_far = across_y([clock.tie(job.result) for job in jobs_up])
    finish(jobs_qkv)
    qkv_parts, qkv_far = across_y([job.result for job in jobs_qkv])
    small.tick()
    gather.tick()
    clock.passed(qkv_far, up_far)
    qkv_part, qkv_far = across_core(qkv_parts, clock.tie(qkv_far))
    up_part, up_far = across_core(up_parts, clock.tie(up_far))
    clock.passed(in_far)
    in_far = clock.tie(in_far)
    small.tick()
    gather.tick()
    u0, u1 = both_cores(up_part, up_far)
    w_up_grad = jnp.concatenate(
        [u[:, k * tile : (k + 1) * tile] for k in range(3) for u in (u0, u1)], axis=1
    )
    clock.passed(w_up_grad)
    small = small.finish()
    factors = gather.finish().reshape(n_img * slots, 12, dm)

    te_rows = lax.dynamic_slice_in_dim(factors[:, 8:], me_img * rows, rows, 2)
    w_time_q_grad, w_time_v_grad = (
        lax.dot_general(
            te_rows.reshape(-1, rows),
            factors[:, 4 * k : 4 * k + 4].reshape(-1, dm),
            (((0,), (0,)), ((), ())),
            preferred_element_type=F32,
        )
        for k in range(2)
    )
    ln1_gain_grad = lax.dynamic_slice_in_dim(small, me_img * rows, rows)
    ln2_gain_grad = lax.dynamic_slice_in_dim(small, dm + me_img * rows, rows)
    rel_all = small[2 * dm : -4].reshape(2, heads, 2 * SIDE - 1)
    rms_values = jnp.sqrt(small[-4:-1] / (small[-1] * dm))
    q0, q1 = both_cores(qkv_part, qkv_far)
    w_proj_grad = jnp.concatenate([q[:, 3 * cols :] for q in (q0, q1)], axis=1)
    w_qkv_grad = jnp.concatenate(
        [q[:, p * cols : (p + 1) * cols] for p in range(3) for q in (q0, q1)], axis=1
    )

    return (
        output,
        returned(input_grad[:span], in_far),
        ln1_gain_grad,
        w_qkv_grad,
        w_time_q_grad,
        w_time_v_grad,
        rel_all[0],
        rel_all[1],
        w_proj_grad,
        ln2_gain_grad,
        w_up_grad,
        w_down_grad,
        rms_values,
    )


def solution(mesh):
    return jax.shard_map(
        per_device,
        mesh=mesh,
        in_specs=(
            P("img", "seq", None),
            P("img", None, None),
            P("img", None),
            P("img", None),
        )
        + (P(),) * 10
        + (P("img", "seq", None),),
        out_specs=(
            P("img", "seq", None),
            P("img", "seq", None),
            P("img"),
            P("img", None),
            P("img", None),
            P("img", None),
            P(),
            P(),
            P("img", None),
            P("img"),
            P("img", None),
            P("img", None),
            P(),
        ),
        check_vma=False,
    )
```
